128 devices in a mesh: gz: 128 (over z, y, x, core).
Axes of the slice: x: 4, y: 4, z: 4, core: 2. Of those that a mesh axis runs over, the one named last changes fastest.
Arguments:
- fraction: float32 [512, 256, 256], P('gz'), may hold values from 0 to 1
- column_dir: int32 [512, 256, 256], P('gz'), may hold values from 0 to 3
- divergence: float32 [512, 256, 256], P('gz'), may hold values from -6 to 6
Outputs:
- curvature: float32 [512, 256, 256], P('gz')
- pressure: float32 [512, 256, 256], P('gz')
The draws below stay inside these ranges and needn't reach their ends.
Inputs may be any that keep to these rules, and one draw needn't show every extreme that they name: `column_dir`: 0 names a column along z, 1 along x, 2 along y, 3 a cell without interface.
All inputs are finite; a program needn't handle non-finite values.
Results may differ from the reference program's by a relative error of at most 0.00065.
Values sent between devices are 32-bit elements; how exact they have to be, the bound alone decides.
A program may use at most 128 MiB of HBM per device.

```python
import jax
import jax.numpy as jnp
from jax import lax

NX = 256
NY = 256
NZ = 512


def set_ends(drawn, own_key, least, largest):
    longest = drawn.shape.index(max(drawn.shape))
    spots = []
    for shift in (0, 1):
        where = [jax.random.randint(jax.random.fold_in(own_key, axis), (), 0, length) for axis, length in enumerate(drawn.shape)]
        where[longest] = (where[longest] + shift) % drawn.shape[longest]
        spots.append(tuple(where))
    return drawn.at[spots[0]].set(least).at[spots[1]].set(largest)


def level_of(key, dims, split, least, high):
    gain, own = 1.0, jax.random.fold_in(key, 6)
    for position, blocks in split:
        steps = jnp.exp(jax.random.uniform(jax.random.fold_in(own, position), (blocks,), jnp.float32, least / len(split), high / len(split)))
        gain = gain * jnp.repeat(steps, dims[position] // blocks).reshape([-1 if axis == position else 1 for axis in range(len(dims))])
    return gain


def noise(stream_key, extent, width, limit, cuts=(), kind=jnp.bfloat16):
    gain = level_of(stream_key, extent, cuts, -0.22, 0.18) if cuts else 1.0
    entries = jax.random.normal(stream_key, extent, jnp.float32) * width * gain
    return jnp.minimum(jnp.maximum(entries, -limit), limit).astype(kind)


def setup_inputs(seed: int = 0) -> dict:
    keys = jax.random.split(jax.random.key(seed), 4)
    return {
        "fraction": jnp.clip(1.0 * jax.random.uniform(keys[0], (NZ, NX, NY), jnp.float32) ** level_of(keys[0], (NZ, NX, NY), ((0, 128),), -0.2, 0.2), 0.0, 1.0),
        "column_dir": set_ends(jax.random.randint(keys[1], (NZ, NX, NY), 0, 4), jax.random.fold_in(keys[1], 1), 0, 3).astype(jnp.int32),
        "divergence": noise(keys[2], (NZ, NX, NY), 1.0, 6.0, ((0, 128),), jnp.float32),
    }


TENSION = 0.2
SHIFT_SCALE = 16.0

def curvature_family(heights):
    slope_a = 0.5 * (heights[1, 0] - heights[-1, 0])
    slope_b = 0.5 * (heights[0, 1] - heights[0, -1])
    bend_aa = heights[1, 0] - 2.0 * heights[0, 0] + heights[-1, 0]
    bend_bb = heights[0, 1] - 2.0 * heights[0, 0] + heights[0, -1]
    bend_ab = 0.25 * (heights[1, 1] - heights[1, -1] - heights[-1, 1] + heights[-1, -1])
    weight = 1.0 + slope_a * slope_a + slope_b * slope_b
    upper = bend_aa * (1.0 + slope_b * slope_b) + bend_bb * (1.0 + slope_a * slope_a) - 2.0 * slope_a * slope_b * bend_ab
    return upper / (weight * jnp.sqrt(weight))

def curvature_of(extended, column_dir):
    count = extended.shape[0] - 6
    offsets = (-1, 0, 1)
    along_z = extended[0:count]
    along_x = jnp.roll(extended, 3, 1)
    along_y = jnp.roll(extended, 3, 2)
    for step in range(1, 7):
        along_z = along_z + extended[step:step + count]
        along_x = along_x + jnp.roll(extended, 3 - step, 1)
        along_y = along_y + jnp.roll(extended, 3 - step, 2)
    family_z = {(first, second): jnp.roll(jnp.roll(along_z, -first, 1), -second, 2) for first in offsets for second in offsets}
    kappa_z = curvature_family(family_z)
    family_x = {(first, second): jnp.roll(along_x[3 + first:3 + first + count], -second, 2) for first in offsets for second in offsets}
    kappa_x = curvature_family(family_x)
    family_y = {(first, second): jnp.roll(along_y[3 + first:3 + first + count], -second, 1) for first in offsets for second in offsets}
    kappa_y = curvature_family(family_y)
    zero = jnp.zeros_like(kappa_z)
    return jnp.where(column_dir == 0, kappa_z, jnp.where(column_dir == 1, kappa_x, jnp.where(column_dir == 2, kappa_y, zero)))

def tension_term(frac_pad, kappa_pad):
    face_up = 0.5 * (kappa_pad[1:-1] + kappa_pad[2:]) * (frac_pad[2:] - frac_pad[1:-1])
    face_down = 0.5 * (kappa_pad[:-2] + kappa_pad[1:-1]) * (frac_pad[1:-1] - frac_pad[:-2])
    kappa_mid = kappa_pad[1:-1]
    frac_mid = frac_pad[1:-1]
    total = face_up - face_down
    for axis in (1, 2):
        face_plus = 0.5 * (kappa_mid + jnp.roll(kappa_mid, -1, axis)) * (jnp.roll(frac_mid, -1, axis) - frac_mid)
        total = total + face_plus - jnp.roll(face_plus, 1, axis)
    return TENSION * total

def mode_diagonal(size_x, size_y, wall_shift):
    waves_x = 2.0 * jnp.sin(jnp.pi * jnp.arange(size_x).astype(jnp.float32) / size_x)
    waves_y = 2.0 * jnp.sin(jnp.pi * jnp.arange(size_y).astype(jnp.float32) / size_y)
    diag = -(2.0 + (waves_x * waves_x)[:, None] + (waves_y * waves_y)[None, :] + wall_shift)
    return diag.reshape(size_x * size_y)

def thomas(rows, diag):
    start = jnp.zeros(rows.shape[1:], jnp.float32)

    def forward(carry, row):
        prev_c, prev_d = carry
        denom = diag - prev_c
        now_c = 1.0 / denom
        now_d = (row - prev_d) / denom
        return ((now_c, now_d), (now_c, now_d))
    final, sweeps = lax.scan(forward, (start, start), rows)

    def backward(above, item):
        coef, value = item
        result = value - coef * above
        return (result, result)
    final, solved = lax.scan(backward, start, sweeps, reverse=True)
    return solved

def hartley(field):
    first = jnp.fft.fft(field, axis=1)
    field = first.real - first.imag
    second = jnp.fft.fft(field, axis=2)
    return second.real - second.imag

def reference(fraction, column_dir, divergence):
    extended = jnp.pad(fraction, ((3, 3), (0, 0), (0, 0)))
    kappa = curvature_of(extended, column_dir)
    kappa_pad = jnp.pad(kappa, ((1, 1), (0, 0), (0, 0)))
    source = divergence + tension_term(extended[2:-2], kappa_pad)
    spectrum = hartley(source).astype(jnp.float32)
    wall_shift = SHIFT_SCALE / float(NZ * NZ)
    diag = mode_diagonal(NX, NY, wall_shift)
    modal = thomas(spectrum.reshape(NZ, NX * NY), diag)
    pressure = hartley(modal.reshape(NZ, NX, NY)) / (NX * NY)
    return (kappa, pressure.astype(jnp.float32))
```

```python
import jax
import jax.numpy as jnp
import numpy as np
from jax import lax
from jax.experimental import pallas as pl
from jax.experimental.pallas import tpu as pltpu
from jax.sharding import PartitionSpec as P

TENSION = 0.2
SHIFT_SCALE = 16.0
SIZE = 256
PLANES = 512
SLAB = 4
DEVICES = 128
GROUPS = 16
RING = 4
ROWS = 32
MESH = pl.DeviceIdType.MESH
F32 = jnp.float32
BF16 = jnp.bfloat16


def tables():
    count = np.arange(SIZE)
    angle = 2.0 * np.pi / SIZE * ((count[:, None] * count[None, :]) % SIZE)
    cas = np.cos(angle) + np.sin(angle)
    high = cas.astype(jnp.bfloat16)
    low = (cas - high.astype(np.float64)).astype(jnp.bfloat16)
    waves = (2.0 * np.sin(np.pi * count / SIZE)) ** 2
    excess = waves[:, None] + waves[None, :] + SHIFT_SCALE / float(PLANES * PLANES)
    root = np.sqrt(excess * (excess + 4.0))
    ratio = 2.0 / (2.0 + excess + root)
    weight = -1.0 / (root * SIZE * SIZE)
    return high, low, ratio.astype(np.float32), weight.astype(np.float32)


def split(x):
    high = x.astype(BF16)
    return high, (x - high.astype(F32)).astype(BF16)


def mm(a, b):
    return jnp.dot(a, b, preferred_element_type=F32)


def mm3(ah, al, bh, bl):
    return mm(ah, bh) + (mm(ah, bl) + mm(al, bh))


def up(x, axis):
    return pltpu.roll(x, x.shape[axis] - 1, axis)


def down(x, axis):
    return pltpu.roll(x, 1, axis)


def window7(x, axis):
    size = x.shape[axis]
    three = x + pltpu.roll(x, 1, axis) + pltpu.roll(x, size - 1, axis)
    return x + pltpu.roll(three, 2, axis) + pltpu.roll(three, size - 2, axis)


def bend(da, db, haa, hbb, dab):
    qa = 0.25 * da * da
    qb = 0.25 * db * db
    root = lax.rsqrt(1.0 + qa + qb)
    upper = haa * (1.0 + qb) + hbb * (1.0 + qa) - 0.125 * (da * db * dab)
    return upper * (root * root * root)


def kernel(
    frac_in, dir_in, div_in, th_in, tl_in, ratio_in, weight_in,
    kap_out, pre_out,
    fx, dirs, divs, th, tl, ratio, weight,
    axc, axd, axs, ayc, ayd, ays, kap, shi, slo, spec, pre,
    lus, rc, px, rx, py, ry, od, rd, qx, dx, sd, ab,
    in_sem, out_sem, fs_sem, fr_sem, ks_sem, kr_sem, c_sem, xs_sem, xr_sem, ys_sem, yr_sem,
):
    me = lax.axis_index("gz")
    core = lax.rem(me, 2)
    xpos = lax.rem(lax.div(me, 2), RING)
    group = lax.div(me, 2 * RING)
    sibling = me + 1 - 2 * core
    has_below = me > 0
    has_above = me < DEVICES - 1
    cross = me - 1 + 2 * core
    has_cross = jnp.logical_and(cross >= 0, cross < DEVICES)

    def xpeer(p):
        return group * (2 * RING) + p * 2 + core

    def ypeer(j):
        return j * (2 * RING) + xpos * 2 + core

    loads = [
        pltpu.make_async_copy(frac_in, fx.at[pl.ds(3, SLAB)], in_sem.at[0]),
        pltpu.make_async_copy(dir_in, dirs, in_sem.at[1]),
        pltpu.make_async_copy(div_in, divs, in_sem.at[2]),
        pltpu.make_async_copy(th_in, th, in_sem.at[3]),
        pltpu.make_async_copy(tl_in, tl, in_sem.at[4]),
        pltpu.make_async_copy(ratio_in, ratio, in_sem.at[5]),
        pltpu.make_async_copy(weight_in, weight, in_sem.at[6]),
    ]
    for load in loads:
        load.start()

    barrier = pltpu.get_barrier_semaphore()

    def greet(target):
        pl.semaphore_signal(barrier, inc=1, device_id=(target,), device_id_type=MESH)

    greet(sibling)

    @pl.when(has_cross)
    def _():
        greet(cross)

    for s in range(1, RING):
        greet(xpeer(lax.rem(xpos + s, RING)))

    def greet_group(s, carry):
        greet(ypeer(lax.rem(group + s, GROUPS)))
        return carry

    lax.fori_loop(1, GROUPS, greet_group, 0)
    peers = 1 + (RING - 1) + (GROUPS - 1)
    pl.semaphore_wait(barrier, jnp.where(has_cross, peers + 1, peers))

    def frac_above(j):
        return pltpu.make_async_remote_copy(
            src_ref=frac_in.at[3 - j], dst_ref=fx.at[2 - j], send_sem=fs_sem.at[0, j],
            recv_sem=fr_sem.at[0, j], device_id=(me + 1,), device_id_type=MESH,
        )

    def frac_below(j):
        return pltpu.make_async_remote_copy(
            src_ref=frac_in.at[j], dst_ref=fx.at[7 + j], send_sem=fs_sem.at[1, j],
            recv_sem=fr_sem.at[1, j], device_id=(me - 1,), device_id_type=MESH,
        )

    def kap_above():
        return pltpu.make_async_remote_copy(
            src_ref=kap.at[4], dst_ref=kap.at[0], send_sem=ks_sem.at[0],
            recv_sem=kr_sem.at[0], device_id=(me + 1,), device_id_type=MESH,
        )

    def kap_below():
        return pltpu.make_async_remote_copy(
            src_ref=kap.at[1], dst_ref=kap.at[5], send_sem=ks_sem.at[1],
            recv_sem=kr_sem.at[1], device_id=(me - 1,), device_id_type=MESH,
        )

    @pl.when(has_above)
    def _():
        for j in range(3):
            frac_above(j).start()

    @pl.when(has_below)
    def _():
        for j in range(3):
            frac_below(j).start()

    zero_plane = jnp.zeros((SIZE, SIZE), F32)

    @pl.when(jnp.logical_not(has_below))
    def _():
        for j in range(3):
            fx[j] = zero_plane
        kap[0] = zero_plane

    @pl.when(jnp.logical_not(has_above))
    def _():
        for j in range(3):
            fx[7 + j] = zero_plane
        kap[5] = zero_plane

    def spans(i):
        r0 = pl.multiple_of(i * ROWS, ROWS)
        before = pl.multiple_of(lax.rem(r0 + SIZE - 8, SIZE), 8)
        after = pl.multiple_of(lax.rem(r0 + ROWS, SIZE), 8)
        return r0, before, after

    def wide(ref, t, span):
        r0, before, after = span
        return jnp.concatenate(
            [ref[t, pl.ds(before, 8), :], ref[t, pl.ds(r0, ROWS), :], ref[t, pl.ds(after, 8), :]], axis=0
        )

    def mid(x):
        return x[8 : 8 + ROWS]

    steps = SIZE // ROWS

    def flat_heights(t):
        def body(i, carry):
            span = spans(i)
            rows = pl.ds(span[0], ROWS)
            f = wide(fx, t + 3, span)
            cx = mid(window7(f, 0))
            lift, drop = up(cx, 1), down(cx, 1)
            axc[t + 1, rows, :] = cx
            axd[t + 1, rows, :] = lift - drop
            axs[t + 1, rows, :] = lift + drop - 2.0 * cx
            cy = window7(f, 1)
            lift, drop = mid(up(cy, 0)), mid(down(cy, 0))
            cy = mid(cy)
            ayc[t + 1, rows, :] = cy
            ayd[t + 1, rows, :] = lift - drop
            ays[t + 1, rows, :] = lift + drop - 2.0 * cy
            return carry

        lax.fori_loop(0, steps, body, 0)

    def flat_bend(t):
        def body(i, carry):
            rows = pl.ds(pl.multiple_of(i * ROWS, ROWS), ROWS)
            along_x = dirs[t, rows, :] == 1

            def pick(a, b):
                return jnp.where(along_x, a, b)

            lo = pick(axc[t, rows, :], ayc[t, rows, :])
            at = pick(axc[t + 1, rows, :], ayc[t + 1, rows, :])
            hi = pick(axc[t + 2, rows, :], ayc[t + 2, rows, :])
            d_lo = pick(axd[t, rows, :], ayd[t, rows, :])
            d_at = pick(axd[t + 1, rows, :], ayd[t + 1, rows, :])
            d_hi = pick(axd[t + 2, rows, :], ayd[t + 2, rows, :])
            s_at = pick(axs[t + 1, rows, :], ays[t + 1, rows, :])
            kap[t + 1, rows, :] = bend(hi - lo, d_at, hi + lo - 2.0 * at, s_at, d_hi - d_lo)
            return carry

        lax.fori_loop(0, steps, body, 0)

    def upright_bend(t):
        def body(i, carry):
            span = spans(i)
            rows = pl.ds(span[0], ROWS)
            h = wide(fx, t, span)
            for j in range(1, 7):
                h = h + wide(fx, t + j, span)
            right, left = up(h, 1), down(h, 1)
            db = right - left
            sb = right + left
            center = mid(h)
            plus, minus = mid(up(h, 0)), mid(down(h, 0))
            dab = mid(up(db, 0)) - mid(down(db, 0))
            value = bend(
                plus - minus, mid(db), plus + minus - 2.0 * center, mid(sb) - 2.0 * center, dab
            )
            where = dirs[t, rows, :]
            flat = kap[t + 1, rows, :]
            kap[t + 1, rows, :] = jnp.where(where == 0, value, jnp.where(where == 3, 0.0, flat))
            return carry

        lax.fori_loop(0, steps, body, 0)

    def source(t):
        def body(i, carry):
            span = spans(i)
            rows = pl.ds(span[0], ROWS)
            f = wide(fx, t + 3, span)
            k = wide(kap, t + 1, span)
            face = (k + up(k, 0)) * (up(f, 0) - f)
            total = mid(face) - mid(down(face, 0))
            f, k = mid(f), mid(k)
            face = (k + up(k, 1)) * (up(f, 1) - f)
            total = total + face - down(face, 1)
            total = total + (k + kap[t + 2, rows, :]) * (fx[t + 4, rows, :] - f)
            total = total - (k + kap[t, rows, :]) * (f - fx[t + 2, rows, :])
            value = divs[t, rows, :] + (0.5 * TENSION) * total
            high, low = split(value)
            shi[t, rows, :] = high
            slo[t, rows, :] = low
            return carry

        lax.fori_loop(0, steps, body, 0)

    def transform(t):
        inner = mm3(shi[t], slo[t], th[...], tl[...])
        ih, il = split(inner)
        return mm3(th[...], tl[...], ih, il)

    near = 3 - 3 * core
    step = 2 * core - 1

    def place(d):
        return near + step * d

    near_side = 1 - core
    near_halo = 4 - 5 * core
    far_halo = 5 * core - 1

    def wait_frac(side, j):
        pltpu.make_async_copy(frac_in.at[0], fx.at[0], fr_sem.at[side, j]).wait()

    loads[0].wait()
    lax.fori_loop(0, SLAB, lambda t, c: (flat_heights(t), c)[1], 0)
    loads[1].wait()
    lax.fori_loop(1, 3, lambda t, c: (flat_bend(t), c)[1], 0)
    for j in range(3):
        wait_frac(near_side, j)
    flat_heights(near_halo)
    flat_bend(near)
    upright_bend(near)

    @pl.when(core == 0)
    def _():
        kap_above().start()

    @pl.when(core == 1)
    def _():
        kap_below().start()

    @pl.when(has_cross)
    def _():
        wait_frac(core, 0)

    flat_heights(far_halo)
    flat_bend(place(3))
    upright_bend(place(1))

    @pl.when(has_cross)
    def _():
        wait_frac(core, 1)

    upright_bend(place(2))

    @pl.when(has_cross)
    def _():
        wait_frac(core, 2)

    upright_bend(place(3))

    @pl.when(jnp.logical_and(has_cross, core == 0))
    def _():
        kap_below().start()

    @pl.when(jnp.logical_and(has_cross, core == 1))
    def _():
        kap_above().start()

    out_kap = pltpu.make_async_copy(kap.at[pl.ds(1, SLAB)], kap_out, out_sem.at[0])
    out_kap.start()
    for load in loads[2:]:
        load.wait()

    def forward(d, carry):
        t = place(d)
        source(t)
        spec[t] = transform(t)
        return carry

    def wait_kap(side):
        pltpu.make_async_copy(frac_in.at[0], kap.at[0], kr_sem.at[side]).wait()

    lax.fori_loop(1, 3, forward, 0)
    wait_kap(near_side)
    forward(0, 0)

    @pl.when(has_cross)
    def _():
        wait_kap(core)

    forward(3, 0)

    def sums(half, i):
        rows = pl.ds(pl.multiple_of(half * 128 + i * ROWS, ROWS), ROWS)
        r = ratio[rows, :]
        f = [spec[t, rows, :] for t in range(SLAB)]
        low = r * (f[3] + r * (f[2] + r * (f[1] + r * f[0])))
        high = r * (f[0] + r * (f[1] + r * (f[2] + r * f[3])))
        return low, high

    def sums_out(i, carry):
        rows = pl.ds(pl.multiple_of(i * ROWS, ROWS), ROWS)
        lus[0, rows, :], lus[1, rows, :] = sums(1 - core, i)
        return carry

    lax.fori_loop(0, 4, sums_out, 0)
    send_c = pltpu.make_async_remote_copy(
        src_ref=lus, dst_ref=rc.at[core], send_sem=c_sem.at[0], recv_sem=c_sem.at[1],
        device_id=(sibling,), device_id_type=MESH,
    )
    send_c.start()

    def sums_own(i, carry):
        rows = pl.ds(pl.multiple_of(i * ROWS, ROWS), ROWS)
        rc[core, 0, rows, :], rc[core, 1, rows, :] = sums(core, i)
        return carry

    lax.fori_loop(0, 4, sums_own, 0)
    send_c.wait_recv()

    def power4(x):
        x = x * x
        return x * x

    def pair_rows(p):
        return pl.ds(pl.multiple_of(core * 128 + p * 32, 32), 32), pl.ds(pl.multiple_of(p * 32, 32), 32)

    def combine_pair(p, target, slot):
        table_rows, rows = pair_rows(p)
        rho = power4(ratio[table_rows, :])
        target[slot, 0] = rho * rc[0, 0, rows, :] + rc[1, 0, rows, :]
        target[slot, 1] = rc[0, 1, rows, :] + rho * rc[1, 1, rows, :]

    def send_x(s):
        p = lax.rem(xpos + s, RING)
        return pltpu.make_async_remote_copy(
            src_ref=px.at[p], dst_ref=rx.at[xpos], send_sem=xs_sem.at[0, p],
            recv_sem=xr_sem.at[0, xpos], device_id=(xpeer(p),), device_id_type=MESH,
        )

    for s in (2, 1, 3):
        combine_pair(lax.rem(xpos + s, RING), px, lax.rem(xpos + s, RING))
        send_x(s).start()
    combine_pair(xpos, rx, xpos)

    def wait_x(level, s):
        p = lax.rem(xpos + s, RING)
        pltpu.make_async_copy(px.at[0], rx.at[0], xr_sem.at[level, p]).wait()

    for s in (1, 3, 2):
        wait_x(0, s)

    my_rows = pair_rows(xpos)[0]
    r = ratio[my_rows, :]
    rho2 = power4(r * r)
    low = rx[0, 0]
    high = rx[RING - 1, 1]
    for p in range(1, RING):
        low = rho2 * low + rx[p, 0]
        high = rho2 * high + rx[RING - 1 - p, 1]

    first_half = lax.broadcasted_iota(jnp.int32, (8, 128), 0) < 4

    def swap(x):
        return pltpu.roll(x, 4, 0)

    for i in range(4):
        for lane in range(2):
            lt = low[8 * i : 8 * i + 8, 128 * lane : 128 * lane + 128]
            ut = high[8 * i : 8 * i + 8, 128 * lane : 128 * lane + 128]
            py[i * 4 + lane * 2] = jnp.where(first_half, lt, swap(ut))
            py[i * 4 + lane * 2 + 1] = jnp.where(first_half, swap(lt), ut)

    def send_y(s, level, source_ref, target_ref):
        j = lax.rem(group + s, GROUPS)
        return pltpu.make_async_remote_copy(
            src_ref=source_ref.at[j], dst_ref=target_ref.at[group], send_sem=ys_sem.at[level, j],
            recv_sem=yr_sem.at[level, group], device_id=(ypeer(j),), device_id_type=MESH,
        )

    def exchange_y(level, source_ref, target_ref):
        def go(s, carry):
            send_y(s, level, source_ref, target_ref).start()
            return carry

        lax.fori_loop(1, GROUPS, go, 0)
        target_ref[group] = source_ref[group]

        def wait(s, carry):
            j = lax.rem(group + s, GROUPS)
            pltpu.make_async_copy(py.at[0], ry.at[0], yr_sem.at[level, j]).wait()
            return carry

        lax.fori_loop(1, GROUPS, wait, 0)

    exchange_y(0, py, ry)

    tile_row = lax.div(group, 4)
    tile_lane = lax.rem(lax.div(group, 2), 2)
    tile_half = lax.rem(group, 2)
    rt = ratio[
        pl.ds(pl.multiple_of(core * 128 + xpos * 32 + tile_row * 8, 8), 8),
        pl.ds(pl.multiple_of(tile_lane * 128, 128), 128),
    ]
    keep = first_half == (tile_half == 0)
    rt = jnp.where(keep, rt, swap(rt))
    r32 = power4(power4(rt * rt))
    r513 = power4(power4(r32)) * rt
    merged = [jnp.where(first_half, ry[j], ry[GROUPS - 1 - j]) for j in range(GROUPS)]
    ends = merged[0]
    for j in range(1, GROUPS):
        ends = r32 * ends + merged[j]
    walls = (swap(ends) - r513 * ends) / (1.0 - r513 * r513)
    sweep = [-(rt * walls)]
    for j in range(GROUPS - 1):
        sweep.append(r32 * sweep[j] + merged[j])
    for j in range(GROUPS):
        od[j] = jnp.where(first_half, sweep[j], sweep[GROUPS - 1 - j])

    exchange_y(1, od, rd)

    def gather(index):
        rows = []
        for i in range(4):
            tiles = []
            for lane in range(2):
                t0, t1 = rd[i * 4 + lane * 2], rd[i * 4 + lane * 2 + 1]
                if index == 0:
                    tiles.append(jnp.where(first_half, t0, swap(t1)))
                else:
                    tiles.append(jnp.where(first_half, swap(t0), t1))
            rows.append(jnp.concatenate(tiles, axis=1))
        return jnp.concatenate(rows, axis=0)

    lower = gather(0)
    upper = gather(1)
    for p in range(RING):
        qx[p, 0] = lower
        qx[RING - 1 - p, 1] = upper
        if p < RING - 1:
            lower = rho2 * lower + rx[p, 0]
            upper = rho2 * upper + rx[RING - 1 - p, 1]

    def send_dx(s):
        p = lax.rem(xpos + s, RING)
        return pltpu.make_async_remote_copy(
            src_ref=qx.at[p], dst_ref=dx.at[xpos], send_sem=xs_sem.at[1, p],
            recv_sem=xr_sem.at[1, xpos], device_id=(xpeer(p),), device_id_type=MESH,
        )

    for s in (2, 1, 3):
        send_dx(s).start()
    dx[xpos] = qx[xpos]
    for s in (1, 3, 2):
        wait_x(1, s)

    def spread(p, carry):
        table_rows, rows = pair_rows(p)
        rho = power4(ratio[table_rows, :])
        a, b = dx[p, 0], dx[p, 1]
        a_far = rho * a + rc[0, 0, rows, :]
        b_far = rho * b + rc[1, 1, rows, :]

        @pl.when(core == 0)
        def _():
            ab[0, 0, rows, :] = a
            ab[0, 1, rows, :] = b_far
            sd[0, rows, :] = a_far
            sd[1, rows, :] = b

        @pl.when(core == 1)
        def _():
            ab[1, 0, rows, :] = a_far
            ab[1, 1, rows, :] = b
            sd[0, rows, :] = a
            sd[1, rows, :] = b_far

        return carry

    lax.fori_loop(0, RING, spread, 0)
    send_d = pltpu.make_async_remote_copy(
        src_ref=sd, dst_ref=ab.at[core], send_sem=c_sem.at[2], recv_sem=c_sem.at[3],
        device_id=(sibling,), device_id_type=MESH,
    )
    send_d.start()

    def modal(half):
        def body(i, carry):
            local = pl.ds(pl.multiple_of(i * ROWS, ROWS), ROWS)
            rows = pl.ds(pl.multiple_of(half * 128 + i * ROWS, ROWS), ROWS)
            r = ratio[rows, :]
            w = weight[rows, :]
            f = [spec[t, rows, :] for t in range(SLAB)]
            rising = [ab[half, 0, local, :] + f[0]]
            for t in range(1, SLAB):
                rising.append(r * rising[t - 1] + f[t])
            falling = ab[half, 1, local, :]
            for t in range(SLAB - 1, -1, -1):
                high, low = split(w * (rising[t] + falling))
                shi[t, rows, :] = high
                slo[t, rows, :] = low
                falling = r * (falling + f[t])
            return carry

        lax.fori_loop(0, 4, body, 0)

    modal(core)
    send_d.wait_recv()
    modal(1 - core)

    def out_pre(t):
        return pltpu.make_async_copy(pre.at[t], pre_out.at[t], out_sem.at[1 + t])

    def backward(t, carry):
        pre[t] = transform(t)
        out_pre(t).start()
        return carry

    lax.fori_loop(0, SLAB, backward, 0)

    @pl.when(has_above)
    def _():
        for j in range(3):
            frac_above(j).wait_send()
        kap_above().wait_send()

    @pl.when(has_below)
    def _():
        for j in range(3):
            frac_below(j).wait_send()
        kap_below().wait_send()

    send_c.wait_send()
    send_d.wait_send()
    for s in range(1, RING):
        send_x(s).wait_send()
        send_dx(s).wait_send()

    def drain(s, carry):
        send_y(s, 0, py, ry).wait_send()
        send_y(s, 1, od, rd).wait_send()
        return carry

    lax.fori_loop(1, GROUPS, drain, 0)
    out_kap.wait()
    for t in range(SLAB):
        out_pre(t).wait()


def shards(fraction, column_dir, divergence):
    shape = (SLAB, SIZE, SIZE)
    plane = (SIZE, SIZE)
    high, low, ratio, weight = tables()
    anywhere = pl.BlockSpec(memory_space=pl.ANY)
    vm = pltpu.VMEM
    dma = pltpu.SemaphoreType.DMA
    return pl.pallas_call(
        kernel,
        out_shape=(jax.ShapeDtypeStruct(shape, F32), jax.ShapeDtypeStruct(shape, F32)),
        in_specs=[anywhere] * 7,
        out_specs=(anywhere, anywhere),
        scratch_shapes=[
            vm((10,) + plane, F32), vm(shape, jnp.int32), vm(shape, F32),
            vm(plane, BF16), vm(plane, BF16), vm(plane, F32), vm(plane, F32),
            vm((6,) + plane, F32), vm((6,) + plane, F32), vm((6,) + plane, F32),
            vm((6,) + plane, F32), vm((6,) + plane, F32), vm((6,) + plane, F32),
            vm((6,) + plane, F32), vm(shape, BF16), vm(shape, BF16), vm(shape, F32), vm(shape, F32),
            vm((2, 128, SIZE), F32), vm((2, 2, 128, SIZE), F32),
            vm((4, 2, 32, SIZE), F32), vm((4, 2, 32, SIZE), F32),
            vm((16, 8, 128), F32), vm((16, 8, 128), F32), vm((16, 8, 128), F32), vm((16, 8, 128), F32),
            vm((4, 2, 32, SIZE), F32), vm((4, 2, 32, SIZE), F32),
            vm((2, 128, SIZE), F32), vm((2, 2, 128, SIZE), F32),
            dma((7,)), dma((5,)), dma((2, 3)), dma((2, 3)), dma((2,)), dma((2,)), dma((4,)),
            dma((2, 4)), dma((2, 4)), dma((2, 16)), dma((2, 16)),
        ],
        compiler_params=pltpu.CompilerParams(
            collective_id=0, has_side_effects=True, vmem_limit_bytes=56 * 1024 * 1024
        ),
    )(
        fraction, column_dir, divergence,
        jnp.asarray(high), jnp.asarray(low), jnp.asarray(ratio), jnp.asarray(weight),
    )


def solution(mesh):
    spec = P("gz", None, None)
    return jax.shard_map(
        shards, mesh=mesh, in_specs=(spec, spec, spec), out_specs=(spec, spec), check_vma=False
    )
```

```python
import jax
import jax.numpy as jnp
import numpy as np
from jax import lax
from jax.experimental import pallas as pl
from jax.experimental.pallas import tpu as pltpu
from jax.sharding import PartitionSpec as P

TENSION = 0.2
SHIFT_SCALE = 16.0
SIZE = 256
PLANES = 512
SLAB = 4
DEVICES = 128
CHIPS = 64
ROWS = 32
MESH = pl.DeviceIdType.MESH
F32 = jnp.float32
BF16 = jnp.bfloat16


def tables():
    count = np.arange(SIZE)
    angle = 2.0 * np.pi / SIZE * ((count[:, None] * count[None, :]) % SIZE)
    cas = np.cos(angle) + np.sin(angle)
    high = cas.astype(jnp.bfloat16)
    low = (cas - high.astype(np.float64)).astype(jnp.bfloat16)
    waves = (2.0 * np.sin(np.pi * count / SIZE)) ** 2
    excess = waves[:, None] + waves[None, :] + SHIFT_SCALE / float(PLANES * PLANES)
    root = np.sqrt(excess * (excess + 4.0))
    ratio = 2.0 / (2.0 + excess + root)
    weight = -1.0 / (root * SIZE * SIZE)
    return high, low, ratio.astype(np.float32), weight.astype(np.float32)


def split(x):
    high = x.astype(BF16)
    return high, (x - high.astype(F32)).astype(BF16)


def mm(a, b):
    return jnp.dot(a, b, preferred_element_type=F32)


def mm3(ah, al, bh, bl):
    return mm(ah, bh) + (mm(ah, bl) + mm(al, bh))


def up(x, axis):
    return pltpu.roll(x, x.shape[axis] - 1, axis)


def down(x, axis):
    return pltpu.roll(x, 1, axis)


def window7(x, axis):
    size = x.shape[axis]
    three = x + pltpu.roll(x, 1, axis) + pltpu.roll(x, size - 1, axis)
    return x + pltpu.roll(three, 2, axis) + pltpu.roll(three, size - 2, axis)


def bend(da, db, haa, hbb, dab):
    qa = 0.25 * da * da
    qb = 0.25 * db * db
    root = lax.rsqrt(1.0 + qa + qb)
    upper = haa * (1.0 + qb) + hbb * (1.0 + qa) - 0.125 * (da * db * dab)
    return upper * (root * root * root)


def kernel(
    frac_in, dir_in, div_in, th_in, tl_in, ratio_in, weight_in,
    kap_out, high_out, low_out,
    fx, dirs, divs, th, tl, ratio, weight,
    axc, axd, axs, ayc, ayd, ays, kap, shi, slo, spec, mhi, mlo,
    lus, rc, pu, ru, od, rd, sd, ab,
    in_sem, out_sem, fs_sem, fr_sem, c_sem, u_sem,
):
    me = lax.axis_index("gz")
    core = lax.rem(me, 2)
    chip = lax.div(me, 2)
    sibling = me + 1 - 2 * core
    has_below = me > 0
    has_above = me < DEVICES - 1
    cross = me - 1 + 2 * core
    has_cross = jnp.logical_and(cross >= 0, cross < DEVICES)

    digits = [lax.div(chip, 16), lax.rem(lax.div(chip, 4), 4), lax.rem(chip, 4)]
    parts = [[lax.rem(v + d, 4) * scale for d in range(4)] for v, scale in zip(digits, (16, 4, 1))]
    reach = (0, 1, 2, 1)
    offsets = [(a, b, c) for a in range(4) for b in range(4) for c in range(4) if a or b or c]
    offsets.sort(key=lambda o: -sum(reach[d] for d in o))
    others = [parts[0][a] + parts[1][b] + parts[2][c] for a, b, c in offsets]

    loads = [
        pltpu.make_async_copy(frac_in, fx.at[pl.ds(3, SLAB)], in_sem.at[0]),
        pltpu.make_async_copy(dir_in, dirs, in_sem.at[1]),
        pltpu.make_async_copy(div_in, divs, in_sem.at[2]),
        pltpu.make_async_copy(th_in, th, in_sem.at[3]),
        pltpu.make_async_copy(tl_in, tl, in_sem.at[4]),
        pltpu.make_async_copy(ratio_in, ratio, in_sem.at[5]),
        pltpu.make_async_copy(weight_in, weight, in_sem.at[6]),
    ]
    for load in loads:
        load.start()

    barrier = pltpu.get_barrier_semaphore()

    def greet(target):
        pl.semaphore_signal(barrier, inc=1, device_id=(target,), device_id_type=MESH)

    greet(sibling)

    @pl.when(has_cross)
    def _():
        greet(cross)

    for other in others:
        greet(2 * other + core)

    peers = 1 + (CHIPS - 1)
    pl.semaphore_wait(barrier, jnp.where(has_cross, peers + 1, peers))

    def frac_above(j):
        return pltpu.make_async_remote_copy(
            src_ref=frac_in.at[3 - j], dst_ref=fx.at[2 - j], send_sem=fs_sem.at[0, j],
            recv_sem=fr_sem.at[0, j], device_id=(me + 1,), device_id_type=MESH,
        )

    def frac_below(j):
        return pltpu.make_async_remote_copy(
            src_ref=frac_in.at[j], dst_ref=fx.at[7 + j], send_sem=fs_sem.at[1, j],
            recv_sem=fr_sem.at[1, j], device_id=(me - 1,), device_id_type=MESH,
        )

    @pl.when(has_above)
    def _():
        for j in range(3):
            frac_above(j).start()

    @pl.when(has_below)
    def _():
        for j in range(3):
            frac_below(j).start()

    zero_plane = jnp.zeros((SIZE, SIZE), F32)

    @pl.when(jnp.logical_not(has_below))
    def _():
        for j in range(3):
            fx[j] = zero_plane

    @pl.when(jnp.logical_not(has_above))
    def _():
        for j in range(3):
            fx[7 + j] = zero_plane

    def flat_heights(t):
        f = fx[t + 3]
        cx = window7(f, 0)
        lift, drop = up(cx, 1), down(cx, 1)
        axc[t + 1] = cx
        axd[t + 1] = lift - drop
        axs[t + 1] = lift + drop - 2.0 * cx
        cy = window7(f, 1)
        lift, drop = up(cy, 0), down(cy, 0)
        ayc[t + 1] = cy
        ayd[t + 1] = lift - drop
        ays[t + 1] = lift + drop - 2.0 * cy

    def flat_bend(t):
        along_x = dirs[t] == 1

        def pick(a, b):
            return jnp.where(along_x, a, b)

        lo = pick(axc[t], ayc[t])
        at = pick(axc[t + 1], ayc[t + 1])
        hi = pick(axc[t + 2], ayc[t + 2])
        d_lo = pick(axd[t], ayd[t])
        d_at = pick(axd[t + 1], ayd[t + 1])
        d_hi = pick(axd[t + 2], ayd[t + 2])
        s_at = pick(axs[t + 1], ays[t + 1])
        kap[t] = bend(hi - lo, d_at, hi + lo - 2.0 * at, s_at, d_hi - d_lo)

    def upright_bend(t):
        h = fx[t]
        for j in range(1, 7):
            h = h + fx[t + j]
        right, left = up(h, 1), down(h, 1)
        db = right - left
        sb = right + left
        plus, minus = up(h, 0), down(h, 0)
        dab = up(db, 0) - down(db, 0)
        value = bend(plus - minus, db, plus + minus - 2.0 * h, sb - 2.0 * h, dab)
        where = dirs[t]
        kap[t] = jnp.where(where == 0, value, jnp.where(where == 3, 0.0, kap[t]))

    def store(t, value):
        shi[t + 1], slo[t + 1] = split(value)

    def source(t):
        f = fx[t + 3]
        k = kap[t]
        face = (k + up(k, 0)) * (up(f, 0) - f)
        total = face - down(face, 0)
        face = (k + up(k, 1)) * (up(f, 1) - f)
        total = total + face - down(face, 1)
        above = jnp.where(t == SLAB - 1, 0.0, kap[jnp.minimum(t + 1, SLAB - 1)])
        below = jnp.where(t == 0, 0.0, kap[jnp.maximum(t - 1, 0)])
        total = total + (k + above) * (fx[t + 4] - f) - (k + below) * (f - fx[t + 2])
        store(t, divs[t] + (0.5 * TENSION) * total)

    def beyond(t, outer, exists):
        scale = jnp.where(exists, 0.5 * TENSION, 0.0)
        store(outer, scale * kap[t] * (fx[t + 3] - fx[outer + 3]))

    def transform(t):
        inner = mm3(shi[t + 1], slo[t + 1], th[...], tl[...])
        ih, il = split(inner)
        spec[t + 1] = mm3(th[...], tl[...], ih, il)

    near = 3 - 3 * core
    step = 2 * core - 1

    def place(d):
        return near + step * d

    near_side = 1 - core
    near_halo = 4 - 5 * core
    far_halo = 5 * core - 1

    def wait_frac(side, j):
        pltpu.make_async_copy(frac_in.at[0], fx.at[0], fr_sem.at[side, j]).wait()

    def wait_far(j):
        @pl.when(has_cross)
        def _():
            wait_frac(core, j)

    loads[0].wait()
    lax.fori_loop(0, SLAB, lambda t, c: (flat_heights(t), c)[1], 0)
    loads[1].wait()
    lax.fori_loop(1, 3, lambda t, c: (flat_bend(t), c)[1], 0)
    for j in range(3):
        wait_frac(near_side, j)
    flat_heights(near_halo)
    flat_bend(near)
    upright_bend(near)
    for load in loads[2:]:
        load.wait()
    beyond(near, near_halo, True)
    transform(near_halo)
    wait_far(0)
    flat_heights(far_halo)
    flat_bend(place(3))
    upright_bend(place(1))
    source(near)
    transform(near)
    wait_far(1)
    upright_bend(place(2))
    source(place(1))
    transform(place(1))
    wait_far(2)
    upright_bend(place(3))
    out_kap = pltpu.make_async_copy(kap, kap_out, out_sem.at[0])
    out_kap.start()
    beyond(place(3), far_halo, has_cross)
    source(place(2))
    source(place(3))
    transform(place(2))
    transform(place(3))
    transform(far_halo)

    def sums(half, i):
        rows = pl.ds(pl.multiple_of(half * 128 + i * ROWS, ROWS), ROWS)
        r = ratio[rows, :]
        f = [spec[t, rows, :] for t in range(SLAB + 2)]
        low, high = f[0], f[SLAB + 1]
        for t in range(1, SLAB + 1):
            low = r * low + f[t]
            high = r * high + f[SLAB + 1 - t]
        low = r * low + f[SLAB + 1]
        high = r * high + f[0]
        return low, high

    def sums_out(i, carry):
        rows = pl.ds(pl.multiple_of(i * ROWS, ROWS), ROWS)
        lus[0, rows, :], lus[1, rows, :] = sums(1 - core, i)
        return carry

    lax.fori_loop(0, 4, sums_out, 0)
    send_c = pltpu.make_async_remote_copy(
        src_ref=lus, dst_ref=rc.at[core], send_sem=c_sem.at[0], recv_sem=c_sem.at[1],
        device_id=(sibling,), device_id_type=MESH,
    )
    send_c.start()

    def sums_own(i, carry):
        rows = pl.ds(pl.multiple_of(i * ROWS, ROWS), ROWS)
        rc[core, 0, rows, :], rc[core, 1, rows, :] = sums(core, i)
        return carry

    lax.fori_loop(0, 4, sums_own, 0)
    send_c.wait_recv()

    def power4(x):
        x = x * x
        return x * x

    first_half = lax.broadcasted_iota(jnp.int32, (8, 128), 0) < 4

    def swap(x):
        return pltpu.roll(x, 4, 0)

    def cut(i, carry):
        rows = pl.ds(pl.multiple_of(i * 8, 8), 8)
        rho = power4(ratio[pl.ds(pl.multiple_of(core * 128 + i * 8, 8), 8), :])
        low = rho * rc[0, 0, rows, :] + rc[1, 0, rows, :]
        high = rc[0, 1, rows, :] + rho * rc[1, 1, rows, :]
        for lane in range(2):
            lt = low[:, 128 * lane : 128 * lane + 128]
            ut = high[:, 128 * lane : 128 * lane + 128]
            pu[i * 4 + lane * 2] = jnp.where(first_half, lt, swap(ut))
            pu[i * 4 + lane * 2 + 1] = jnp.where(first_half, swap(lt), ut)
        return carry

    lax.fori_loop(0, 16, cut, 0, unroll=4)

    def send_part(other, level, source_ref, target_ref):
        return pltpu.make_async_remote_copy(
            src_ref=source_ref.at[other], dst_ref=target_ref.at[chip], send_sem=u_sem.at[level, 0],
            recv_sem=u_sem.at[level, 1], device_id=(2 * other + core,), device_id_type=MESH,
        )

    def wait_parts(level, way):
        span = pl.ds(0, CHIPS - 1)
        pltpu.make_async_copy(pu.at[span], ru.at[span], u_sem.at[level, way]).wait()

    for other in others:
        send_part(other, 0, pu, ru).start()
    ru[chip] = pu[chip]
    wait_parts(0, 1)

    tile_row = lax.div(chip, 4)
    tile_lane = lax.rem(lax.div(chip, 2), 2)
    tile_half = lax.rem(chip, 2)
    rt = ratio[
        pl.ds(pl.multiple_of(core * 128 + tile_row * 8, 8), 8),
        pl.ds(pl.multiple_of(tile_lane * 128, 128), 128),
    ]
    keep = first_half == (tile_half == 0)
    rt = jnp.where(keep, rt, swap(rt))
    r8 = power4(rt * rt)
    r64 = power4(r8 * r8)
    r513 = power4(r64 * r64) * rt
    merged = [jnp.where(first_half, ru[j], ru[CHIPS - 1 - j]) for j in range(CHIPS)]
    blocks = []
    for b in range(8):
        total = merged[8 * b]
        for j in range(1, 8):
            total = r8 * total + merged[8 * b + j]
        blocks.append(total)
    ends = blocks[0]
    for b in range(1, 8):
        ends = r64 * ends + blocks[b]
    walls = (swap(ends) - r513 * ends) / (1.0 - r513 * r513)
    starts = [-(rt * walls)]
    for b in range(7):
        starts.append(r64 * starts[b] + blocks[b])
    sweep = []
    for b in range(8):
        sweep.append(starts[b])
        for j in range(7):
            sweep.append(r8 * sweep[-1] + merged[8 * b + j])
    for j in range(CHIPS):
        od[j] = jnp.where(first_half, sweep[j], sweep[CHIPS - 1 - j])

    for other in others:
        send_part(other, 1, od, rd).start()
    rd[chip] = od[chip]
    wait_parts(1, 1)

    def spread(i, carry):
        rows = pl.ds(pl.multiple_of(i * 8, 8), 8)
        rho = power4(ratio[pl.ds(pl.multiple_of(core * 128 + i * 8, 8), 8), :])
        tiles = [rd[i * 4 + k] for k in range(4)]
        a = jnp.concatenate([jnp.where(first_half, tiles[k], swap(tiles[k + 1])) for k in (0, 2)], axis=1)
        b = jnp.concatenate([jnp.where(first_half, swap(tiles[k]), tiles[k + 1]) for k in (0, 2)], axis=1)
        a_far = rho * a + rc[0, 0, rows, :]
        b_far = rho * b + rc[1, 1, rows, :]
        even = core == 0
        ab[core, 0, rows, :] = jnp.where(even, a, a_far)
        ab[core, 1, rows, :] = jnp.where(even, b_far, b)
        sd[0, rows, :] = jnp.where(even, a_far, a)
        sd[1, rows, :] = jnp.where(even, b, b_far)
        return carry

    lax.fori_loop(0, 16, spread, 0, unroll=4)
    send_d = pltpu.make_async_remote_copy(
        src_ref=sd, dst_ref=ab.at[core], send_sem=c_sem.at[2], recv_sem=c_sem.at[3],
        device_id=(sibling,), device_id_type=MESH,
    )
    send_d.start()

    def modal(half):
        def body(i, carry):
            local = pl.ds(pl.multiple_of(i * ROWS, ROWS), ROWS)
            rows = pl.ds(pl.multiple_of(half * 128 + i * ROWS, ROWS), ROWS)
            r = ratio[rows, :]
            w = weight[rows, :]
            f = [spec[t, rows, :] for t in range(SLAB + 2)]
            rising = [r * f[0] + ab[half, 0, local, :] + f[1]]
            for t in range(1, SLAB):
                rising.append(r * rising[t - 1] + f[t + 1])
            falling = ab[half, 1, local, :] + r * f[SLAB + 1]
            for t in range(SLAB - 1, -1, -1):
                mhi[t, rows, :], mlo[t, rows, :] = split(w * (rising[t] + falling))
                falling = r * (falling + f[t + 1])
            return carry

        lax.fori_loop(0, 4, body, 0, unroll=2)

    modal(core)
    send_d.wait_recv()
    modal(1 - core)

    out_high = pltpu.make_async_copy(mhi, high_out, out_sem.at[1])
    out_low = pltpu.make_async_copy(mlo, low_out, out_sem.at[2])
    out_high.start()
    out_low.start()

    @pl.when(has_above)
    def _():
        for j in range(3):
            frac_above(j).wait_send()

    @pl.when(has_below)
    def _():
        for j in range(3):
            frac_below(j).wait_send()

    send_c.wait_send()
    send_d.wait_send()
    wait_parts(0, 0)
    wait_parts(1, 0)
    out_kap.wait()
    out_high.wait()
    out_low.wait()


def finish(kap_in, high_in, low_in, th_in, tl_in, kap_out, pre_out, mhi, mlo, th, tl, pre, sem):
    passing = pltpu.make_async_copy(kap_in, kap_out, sem.at[0])
    passing.start()
    loads = [
        pltpu.make_async_copy(source, target, sem.at[1 + i])
        for i, (source, target) in enumerate(((th_in, th), (tl_in, tl), (high_in, mhi), (low_in, mlo)))
    ]
    for load in loads:
        load.start()
    for load in loads:
        load.wait()
    stores = []
    for t in range(SLAB):
        ih, il = split(mm3(mhi[t], mlo[t], th[...], tl[...]))
        pre[t] = mm3(th[...], tl[...], ih, il)
        stores.append(pltpu.make_async_copy(pre.at[t], pre_out.at[t], sem.at[5 + t]))
        stores[t].start()
    passing.wait()
    for copy in stores:
        copy.wait()


def shards(fraction, column_dir, divergence):
    shape = (SLAB, SIZE, SIZE)
    plane = (SIZE, SIZE)
    high, low, ratio, weight = tables()
    anywhere = pl.BlockSpec(memory_space=pl.ANY)
    vm = pltpu.VMEM
    dma = pltpu.SemaphoreType.DMA
    high, low = jnp.asarray(high), jnp.asarray(low)
    whole = jax.ShapeDtypeStruct(shape, F32)
    half = jax.ShapeDtypeStruct(shape, BF16)
    params = dict(vmem_limit_bytes=56 * 1024 * 1024)
    six = vm((SLAB + 2,) + plane, F32)
    curvature, modal_high, modal_low = pl.pallas_call(
        kernel,
        out_shape=(whole, half, half),
        in_specs=[anywhere] * 7,
        out_specs=(anywhere,) * 3,
        scratch_shapes=[
            vm((10,) + plane, F32), vm(shape, jnp.int32), vm(shape, F32),
            vm(plane, BF16), vm(plane, BF16), vm(plane, F32), vm(plane, F32),
            six, six, six, six, six, six,
            vm(shape, F32), vm((SLAB + 2,) + plane, BF16), vm((SLAB + 2,) + plane, BF16), six,
            vm(shape, BF16), vm(shape, BF16),
            vm((2, 128, SIZE), F32), vm((2, 2, 128, SIZE), F32),
            vm((CHIPS, 8, 128), F32), vm((CHIPS, 8, 128), F32),
            vm((CHIPS, 8, 128), F32), vm((CHIPS, 8, 128), F32),
            vm((2, 128, SIZE), F32), vm((2, 2, 128, SIZE), F32),
            dma((7,)), dma((3,)), dma((2, 3)), dma((2, 3)), dma((4,)), dma((2, 2)),
        ],
        compiler_params=pltpu.CompilerParams(collective_id=0, has_side_effects=True, **params),
    )(fraction, column_dir, divergence, high, low, jnp.asarray(ratio), jnp.asarray(weight))
    return pl.pallas_call(
        finish,
        out_shape=(whole, whole),
        in_specs=[anywhere] * 5,
        out_specs=(anywhere,) * 2,
        scratch_shapes=[
            vm(shape, BF16), vm(shape, BF16), vm(plane, BF16), vm(plane, BF16), vm(shape, F32), dma((9,)),
        ],
        compiler_params=pltpu.CompilerParams(**params),
    )(curvature, modal_high, modal_low, high, low)


def solution(mesh):
    spec = P("gz", None, None)
    return jax.shard_map(
        shards, mesh=mesh, in_specs=(spec, spec, spec), out_specs=(spec, spec), check_vma=False
    )
```

```python
import jax
import jax.numpy as jnp
import numpy as np
from jax import lax
from jax.experimental import pallas as pl
from jax.experimental.pallas import tpu as pltpu
from jax.sharding import PartitionSpec as P

TENSION = 0.2
SHIFT_SCALE = 16.0
SIZE = 256
PLANES = 512
SLAB = 4
DEVICES = 128
CHIPS = 64
ROWS = 32
MESH = pl.DeviceIdType.MESH
F32 = jnp.float32
BF16 = jnp.bfloat16


def tables():
    count = np.arange(SIZE)
    angle = 2.0 * np.pi / SIZE * ((count[:, None] * count[None, :]) % SIZE)
    cas = np.cos(angle) + np.sin(angle)
    high = cas.astype(jnp.bfloat16)
    low = (cas - high.astype(np.float64)).astype(jnp.bfloat16)
    waves = (2.0 * np.sin(np.pi * count / SIZE)) ** 2
    excess = waves[:, None] + waves[None, :] + SHIFT_SCALE / float(PLANES * PLANES)
    root = np.sqrt(excess * (excess + 4.0))
    ratio = 2.0 / (2.0 + excess + root)
    weight = -1.0 / (root * SIZE * SIZE)
    return high, low, ratio.astype(np.float32), weight.astype(np.float32)


def split(x):
    high = x.astype(BF16)
    return high, (x - high.astype(F32)).astype(BF16)


def mm(a, b):
    return jnp.dot(a, b, preferred_element_type=F32)


def mm3(ah, al, bh, bl):
    return mm(ah, bh) + (mm(ah, bl) + mm(al, bh))


def up(x, axis):
    return pltpu.roll(x, x.shape[axis] - 1, axis)


def down(x, axis):
    return pltpu.roll(x, 1, axis)


def window7(x, axis):
    size = x.shape[axis]
    three = x + pltpu.roll(x, 1, axis) + pltpu.roll(x, size - 1, axis)
    return x + pltpu.roll(three, 2, axis) + pltpu.roll(three, size - 2, axis)


def bend(da, db, haa, hbb, dab):
    qa = 0.25 * da * da
    qb = 0.25 * db * db
    root = lax.rsqrt(1.0 + qa + qb)
    upper = haa * (1.0 + qb) + hbb * (1.0 + qa) - 0.125 * (da * db * dab)
    return upper * (root * root * root)


def kernel(
    frac_in, dir_in, div_in, th_in, tl_in, ratio_in, weight_in,
    kap_out, high_out, low_out,
    fx, dirs, divs, th, tl, ratio, weight,
    axc, axd, axs, ayc, ayd, ays, kap, shi, slo, spec, mhi, mlo,
    lus, rc, pu, ru, od, rd, sd, ab,
    in_sem, out_sem, fs_sem, fr_sem, c_sem, u_sem,
):
    me = lax.axis_index("gz")
    core = lax.rem(me, 2)
    chip = lax.div(me, 2)
    sibling = me + 1 - 2 * core
    has_below = me > 0
    has_above = me < DEVICES - 1
    cross = me - 1 + 2 * core
    has_cross = jnp.logical_and(cross >= 0, cross < DEVICES)

    digits = [lax.div(chip, 16), lax.rem(lax.div(chip, 4), 4), lax.rem(chip, 4)]
    parts = [[lax.rem(v + d, 4) * scale for d in range(4)] for v, scale in zip(digits, (16, 4, 1))]
    reach = (0, 1, 2, 1)
    offsets = [(a, b, c) for a in range(4) for b in range(4) for c in range(4) if a or b or c]
    offsets.sort(key=lambda o: -sum(reach[d] for d in o))
    others = [parts[0][a] + parts[1][b] + parts[2][c] for a, b, c in offsets]

    loads = [
        pltpu.make_async_copy(frac_in, fx.at[pl.ds(3, SLAB)], in_sem.at[0]),
        pltpu.make_async_copy(dir_in, dirs, in_sem.at[1]),
        pltpu.make_async_copy(div_in, divs, in_sem.at[2]),
        pltpu.make_async_copy(th_in, th, in_sem.at[3]),
        pltpu.make_async_copy(tl_in, tl, in_sem.at[4]),
        pltpu.make_async_copy(ratio_in, ratio, in_sem.at[5]),
        pltpu.make_async_copy(weight_in, weight, in_sem.at[6]),
    ]
    for load in loads:
        load.start()

    barrier = pltpu.get_barrier_semaphore()

    def greet(target):
        pl.semaphore_signal(barrier, inc=1, device_id=(target,), device_id_type=MESH)

    greet(sibling)

    @pl.when(has_cross)
    def _():
        greet(cross)

    for other in others:
        greet(2 * other + core)

    peers = 1 + (CHIPS - 1)
    pl.semaphore_wait(barrier, jnp.where(has_cross, peers + 1, peers))

    def frac_above(j):
        return pltpu.make_async_remote_copy(
            src_ref=frac_in.at[3 - j], dst_ref=fx.at[2 - j], send_sem=fs_sem.at[0, j],
            recv_sem=fr_sem.at[0, j], device_id=(me + 1,), device_id_type=MESH,
        )

    def frac_below(j):
        return pltpu.make_async_remote_copy(
            src_ref=frac_in.at[j], dst_ref=fx.at[7 + j], send_sem=fs_sem.at[1, j],
            recv_sem=fr_sem.at[1, j], device_id=(me - 1,), device_id_type=MESH,
        )

    @pl.when(has_above)
    def _():
        for j in range(3):
            frac_above(j).start()

    @pl.when(has_below)
    def _():
        for j in range(3):
            frac_below(j).start()

    zero_plane = jnp.zeros((SIZE, SIZE), F32)

    @pl.when(jnp.logical_not(has_below))
    def _():
        for j in range(3):
            fx[j] = zero_plane

    @pl.when(jnp.logical_not(has_above))
    def _():
        for j in range(3):
            fx[7 + j] = zero_plane

    def flat_heights(t):
        f = fx[t + 3]
        cx = window7(f, 0)
        lift, drop = up(cx, 1), down(cx, 1)
        axc[t + 1] = cx
        axd[t + 1] = lift - drop
        axs[t + 1] = lift + drop - 2.0 * cx
        cy = window7(f, 1)
        lift, drop = up(cy, 0), down(cy, 0)
        ayc[t + 1] = cy
        ayd[t + 1] = lift - drop
        ays[t + 1] = lift + drop - 2.0 * cy

    def flat_bend(t):
        along_x = dirs[t] == 1

        def pick(a, b):
            return jnp.where(along_x, a, b)

        lo = pick(axc[t], ayc[t])
        at = pick(axc[t + 1], ayc[t + 1])
        hi = pick(axc[t + 2], ayc[t + 2])
        d_lo = pick(axd[t], ayd[t])
        d_at = pick(axd[t + 1], ayd[t + 1])
        d_hi = pick(axd[t + 2], ayd[t + 2])
        s_at = pick(axs[t + 1], ays[t + 1])
        kap[t] = bend(hi - lo, d_at, hi + lo - 2.0 * at, s_at, d_hi - d_lo)

    def upright_bend(t):
        h = fx[t]
        for j in range(1, 7):
            h = h + fx[t + j]
        right, left = up(h, 1), down(h, 1)
        db = right - left
        sb = right + left
        plus, minus = up(h, 0), down(h, 0)
        dab = up(db, 0) - down(db, 0)
        value = bend(plus - minus, db, plus + minus - 2.0 * h, sb - 2.0 * h, dab)
        where = dirs[t]
        kap[t] = jnp.where(where == 0, value, jnp.where(where == 3, 0.0, kap[t]))

    def store(t, value):
        shi[t + 1], slo[t + 1] = split(value)

    def source(t):
        f = fx[t + 3]
        k = kap[t]
        face = (k + up(k, 0)) * (up(f, 0) - f)
        total = face - down(face, 0)
        face = (k + up(k, 1)) * (up(f, 1) - f)
        total = total + face - down(face, 1)
        above = jnp.where(t == SLAB - 1, 0.0, kap[jnp.minimum(t + 1, SLAB - 1)])
        below = jnp.where(t == 0, 0.0, kap[jnp.maximum(t - 1, 0)])
        total = total + (k + above) * (fx[t + 4] - f) - (k + below) * (f - fx[t + 2])
        store(t, divs[t] + (0.5 * TENSION) * total)

    def beyond(t, outer, exists):
        scale = jnp.where(exists, 0.5 * TENSION, 0.0)
        store(outer, scale * kap[t] * (fx[t + 3] - fx[outer + 3]))

    def transform(t):
        inner = mm3(shi[t + 1], slo[t + 1], th[...], tl[...])
        ih, il = split(inner)
        spec[t + 1] = mm3(th[...], tl[...], ih, il)

    near = 3 - 3 * core
    step = 2 * core - 1

    def place(d):
        return near + step * d

    near_side = 1 - core
    near_halo = 4 - 5 * core
    far_halo = 5 * core - 1

    def wait_frac(side, j):
        pltpu.make_async_copy(frac_in.at[0], fx.at[0], fr_sem.at[side, j]).wait()

    def wait_far(j):
        @pl.when(has_cross)
        def _():
            wait_frac(core, j)

    loads[0].wait()
    lax.fori_loop(0, SLAB, lambda t, c: (flat_heights(t), c)[1], 0)
    loads[1].wait()
    lax.fori_loop(1, 3, lambda t, c: (flat_bend(t), c)[1], 0)
    for j in range(3):
        wait_frac(near_side, j)
    flat_heights(near_halo)
    flat_bend(near)
    upright_bend(near)
    for load in loads[2:]:
        load.wait()
    beyond(near, near_halo, True)
    transform(near_halo)
    wait_far(0)
    flat_heights(far_halo)
    flat_bend(place(3))
    upright_bend(place(1))
    source(near)
    transform(near)
    wait_far(1)
    upright_bend(place(2))
    source(place(1))
    transform(place(1))
    wait_far(2)
    upright_bend(place(3))
    out_kap = pltpu.make_async_copy(kap, kap_out, out_sem.at[0])
    out_kap.start()
    beyond(place(3), far_halo, has_cross)
    source(place(2))
    source(place(3))
    transform(place(2))
    transform(place(3))
    transform(far_halo)

    def sums(half, i):
        rows = pl.ds(pl.multiple_of(half * 128 + i * ROWS, ROWS), ROWS)
        r = ratio[rows, :]
        f = [spec[t, rows, :] for t in range(SLAB + 2)]
        low, high = f[0], f[SLAB + 1]
        for t in range(1, SLAB + 1):
            low = r * low + f[t]
            high = r * high + f[SLAB + 1 - t]
        low = r * low + f[SLAB + 1]
        high = r * high + f[0]
        return low, high

    def sums_out(i, carry):
        rows = pl.ds(pl.multiple_of(i * ROWS, ROWS), ROWS)
        lus[0, rows, :], lus[1, rows, :] = sums(1 - core, i)
        return carry

    lax.fori_loop(0, 4, sums_out, 0)
    send_c = pltpu.make_async_remote_copy(
        src_ref=lus, dst_ref=rc.at[core], send_sem=c_sem.at[0], recv_sem=c_sem.at[1],
        device_id=(sibling,), device_id_type=MESH,
    )
    send_c.start()

    def sums_own(i, carry):
        rows = pl.ds(pl.multiple_of(i * ROWS, ROWS), ROWS)
        rc[core, 0, rows, :], rc[core, 1, rows, :] = sums(core, i)
        return carry

    lax.fori_loop(0, 4, sums_own, 0)
    send_c.wait_recv()

    def power4(x):
        x = x * x
        return x * x

    first_half = lax.broadcasted_iota(jnp.int32, (8, 128), 0) < 4

    def swap(x):
        return pltpu.roll(x, 4, 0)

    def cut(i, carry):
        rows = pl.ds(pl.multiple_of(i * 8, 8), 8)
        rho = power4(ratio[pl.ds(pl.multiple_of(core * 128 + i * 8, 8), 8), :])
        low = rho * rc[0, 0, rows, :] + rc[1, 0, rows, :]
        high = rc[0, 1, rows, :] + rho * rc[1, 1, rows, :]
        for lane in range(2):
            lt = low[:, 128 * lane : 128 * lane + 128]
            ut = high[:, 128 * lane : 128 * lane + 128]
            pu[i * 4 + lane * 2] = jnp.where(first_half, lt, swap(ut))
            pu[i * 4 + lane * 2 + 1] = jnp.where(first_half, swap(lt), ut)
        return carry

    lax.fori_loop(0, 16, cut, 0, unroll=4)

    def send_part(other, level, source_ref, target_ref):
        return pltpu.make_async_remote_copy(
            src_ref=source_ref.at[other], dst_ref=target_ref.at[chip], send_sem=u_sem.at[level, 0],
            recv_sem=u_sem.at[level, 1], device_id=(2 * other + core,), device_id_type=MESH,
        )

    def wait_parts(level, way):
        span = pl.ds(0, CHIPS - 1)
        pltpu.make_async_copy(pu.at[span], ru.at[span], u_sem.at[level, way]).wait()

    for other in others:
        send_part(other, 0, pu, ru).start()
    ru[chip] = pu[chip]
    wait_parts(0, 1)

    tile_row = lax.div(chip, 4)
    tile_lane = lax.rem(lax.div(chip, 2), 2)
    tile_half = lax.rem(chip, 2)
    rt = ratio[
        pl.ds(pl.multiple_of(core * 128 + tile_row * 8, 8), 8),
        pl.ds(pl.multiple_of(tile_lane * 128, 128), 128),
    ]
    keep = first_half == (tile_half == 0)
    rt = jnp.where(keep, rt, swap(rt))
    r8 = power4(rt * rt)
    r64 = power4(r8 * r8)
    r513 = power4(r64 * r64) * rt
    merged = [jnp.where(first_half, ru[j], ru[CHIPS - 1 - j]) for j in range(CHIPS)]
    blocks = []
    for b in range(8):
        total = merged[8 * b]
        for j in range(1, 8):
            total = r8 * total + merged[8 * b + j]
        blocks.append(total)
    ends = blocks[0]
    for b in range(1, 8):
        ends = r64 * ends + blocks[b]
    walls = (swap(ends) - r513 * ends) / (1.0 - r513 * r513)
    starts = [-(rt * walls)]
    for b in range(7):
        starts.append(r64 * starts[b] + blocks[b])
    sweep = []
    for b in range(8):
        sweep.append(starts[b])
        for j in range(7):
            sweep.append(r8 * sweep[-1] + merged[8 * b + j])
    for j in range(CHIPS):
        od[j] = jnp.where(first_half, sweep[j], sweep[CHIPS - 1 - j])

    for other in others:
        send_part(other, 1, od, rd).start()
    rd[chip] = od[chip]
    wait_parts(1, 1)

    def spread(i, carry):
        rows = pl.ds(pl.multiple_of(i * 8, 8), 8)
        rho = power4(ratio[pl.ds(pl.multiple_of(core * 128 + i * 8, 8), 8), :])
        tiles = [rd[i * 4 + k] for k in range(4)]
        a = jnp.concatenate([jnp.where(first_half, tiles[k], swap(tiles[k + 1])) for k in (0, 2)], axis=1)
        b = jnp.concatenate([jnp.where(first_half, swap(tiles[k]), tiles[k + 1]) for k in (0, 2)], axis=1)
        a_far = rho * a + rc[0, 0, rows, :]
        b_far = rho * b + rc[1, 1, rows, :]
        even = core == 0
        ab[core, 0, rows, :] = jnp.where(even, a, a_far)
        ab[core, 1, rows, :] = jnp.where(even, b_far, b)
        sd[0, rows, :] = jnp.where(even, a_far, a)
        sd[1, rows, :] = jnp.where(even, b, b_far)
        return carry

    lax.fori_loop(0, 16, spread, 0, unroll=4)
    send_d = pltpu.make_async_remote_copy(
        src_ref=sd, dst_ref=ab.at[core], send_sem=c_sem.at[2], recv_sem=c_sem.at[3],
        device_id=(sibling,), device_id_type=MESH,
    )
    send_d.start()

    def modal(half):
        def body(i, carry):
            local = pl.ds(pl.multiple_of(i * ROWS, ROWS), ROWS)
            rows = pl.ds(pl.multiple_of(half * 128 + i * ROWS, ROWS), ROWS)
            r = ratio[rows, :]
            w = weight[rows, :]
            f = [spec[t, rows, :] for t in range(SLAB + 2)]
            rising = [r * f[0] + ab[half, 0, local, :] + f[1]]
            for t in range(1, SLAB):
                rising.append(r * rising[t - 1] + f[t + 1])
            falling = ab[half, 1, local, :] + r * f[SLAB + 1]
            for t in range(SLAB - 1, -1, -1):
                mhi[t, rows, :], mlo[t, rows, :] = split(w * (rising[t] + falling))
                falling = r * (falling + f[t + 1])
            return carry

        lax.fori_loop(0, 4, body, 0, unroll=2)

    modal(core)
    send_d.wait_recv()
    modal(1 - core)

    out_high = pltpu.make_async_copy(mhi, high_out, out_sem.at[1])
    out_low = pltpu.make_async_copy(mlo, low_out, out_sem.at[2])
    out_high.start()
    out_low.start()

    @pl.when(has_above)
    def _():
        for j in range(3):
            frac_above(j).wait_send()

    @pl.when(has_below)
    def _():
        for j in range(3):
            frac_below(j).wait_send()

    send_c.wait_send()
    send_d.wait_send()
    wait_parts(0, 0)
    wait_parts(1, 0)
    out_kap.wait()
    out_high.wait()
    out_low.wait()


def finish(kap_in, high_in, low_in, th_in, tl_in, kap_out, pre_out, kap, mhi, mlo, th, tl, pre, sem):
    loads = [
        pltpu.make_async_copy(source, target, sem.at[1 + i])
        for i, (source, target) in enumerate(((th_in, th), (tl_in, tl), (high_in, mhi), (low_in, mlo)))
    ]
    fetch = pltpu.make_async_copy(kap_in, kap, sem.at[0])
    passing = pltpu.make_async_copy(kap, kap_out, sem.at[9])
    for load in loads:
        load.start()
    fetch.start()
    for load in loads:
        load.wait()
    fetch.wait()
    passing.start()
    stores = []
    for t in range(SLAB):
        ih, il = split(mm3(mhi[t], mlo[t], th[...], tl[...]))
        pre[t] = mm3(th[...], tl[...], ih, il)
        stores.append(pltpu.make_async_copy(pre.at[t], pre_out.at[t], sem.at[5 + t]))
        stores[t].start()
    passing.wait()
    for copy in stores:
        copy.wait()


def shards(fraction, column_dir, divergence):
    shape = (SLAB, SIZE, SIZE)
    plane = (SIZE, SIZE)
    high, low, ratio, weight = tables()
    anywhere = pl.BlockSpec(memory_space=pl.ANY)
    vm = pltpu.VMEM
    dma = pltpu.SemaphoreType.DMA
    high, low = jnp.asarray(high), jnp.asarray(low)
    whole = jax.ShapeDtypeStruct(shape, F32)
    half = jax.ShapeDtypeStruct(shape, BF16)
    params = dict(vmem_limit_bytes=56 * 1024 * 1024)
    six = vm((SLAB + 2,) + plane, F32)
    curvature, modal_high, modal_low = pl.pallas_call(
        kernel,
        out_shape=(whole, half, half),
        in_specs=[anywhere] * 7,
        out_specs=(anywhere,) * 3,
        scratch_shapes=[
            vm((10,) + plane, F32), vm(shape, jnp.int32), vm(shape, F32),
            vm(plane, BF16), vm(plane, BF16), vm(plane, F32), vm(plane, F32),
            six, six, six, six, six, six,
            vm(shape, F32), vm((SLAB + 2,) + plane, BF16), vm((SLAB + 2,) + plane, BF16), six,
            vm(shape, BF16), vm(shape, BF16),
            vm((2, 128, SIZE), F32), vm((2, 2, 128, SIZE), F32),
            vm((CHIPS, 8, 128), F32), vm((CHIPS, 8, 128), F32),
            vm((CHIPS, 8, 128), F32), vm((CHIPS, 8, 128), F32),
            vm((2, 128, SIZE), F32), vm((2, 2, 128, SIZE), F32),
            dma((7,)), dma((3,)), dma((2, 3)), dma((2, 3)), dma((4,)), dma((2, 2)),
        ],
        compiler_params=pltpu.CompilerParams(collective_id=0, has_side_effects=True, **params),
    )(fraction, column_dir, divergence, high, low, jnp.asarray(ratio), jnp.asarray(weight))
    return pl.pallas_call(
        finish,
        out_shape=(whole, whole),
        in_specs=[anywhere] * 5,
        out_specs=(anywhere,) * 2,
        scratch_shapes=[
            vm(shape, F32), vm(shape, BF16), vm(shape, BF16), vm(plane, BF16), vm(plane, BF16), vm(shape, F32), dma((10,)),
        ],
        compiler_params=pltpu.CompilerParams(**params),
    )(curvature, modal_high, modal_low, high, low)


def solution(mesh):
    spec = P("gz", None, None)
    return jax.shard_map(
        shards, mesh=mesh, in_specs=(spec, spec, spec), out_specs=(spec, spec), check_vma=False
    )
```

```python
import jax
import jax.numpy as jnp
import numpy as np
from jax import lax
from jax.experimental import pallas as pl
from jax.experimental.pallas import tpu as pltpu
from jax.sharding import PartitionSpec as P

TENSION = 0.2
SHIFT_SCALE = 16.0
SIZE = 256
PLANES = 512
SLAB = 4
DEVICES = 128
CHIPS = 64
ROWS = 32
MESH = pl.DeviceIdType.MESH
F32 = jnp.float32
BF16 = jnp.bfloat16


def tables():
    count = np.arange(SIZE)
    angle = 2.0 * np.pi / SIZE * ((count[:, None] * count[None, :]) % SIZE)
    cas = np.cos(angle) + np.sin(angle)
    high = cas.astype(jnp.bfloat16)
    low = (cas - high.astype(np.float64)).astype(jnp.bfloat16)
    waves = (2.0 * np.sin(np.pi * count / SIZE)) ** 2
    excess = waves[:, None] + waves[None, :] + SHIFT_SCALE / float(PLANES * PLANES)
    root = np.sqrt(excess * (excess + 4.0))
    ratio = 2.0 / (2.0 + excess + root)
    weight = -1.0 / (root * SIZE * SIZE)
    return high, low, ratio.astype(np.float32), weight.astype(np.float32)


def split(x):
    high = x.astype(BF16)
    return high, (x - high.astype(F32)).astype(BF16)


def mm(a, b):
    return jnp.dot(a, b, preferred_element_type=F32)


def mm3(ah, al, bh, bl):
    return mm(ah, bh) + (mm(ah, bl) + mm(al, bh))


def up(x, axis):
    return pltpu.roll(x, x.shape[axis] - 1, axis)


def down(x, axis):
    return pltpu.roll(x, 1, axis)


def window7(x, axis):
    size = x.shape[axis]
    three = x + pltpu.roll(x, 1, axis) + pltpu.roll(x, size - 1, axis)
    return x + pltpu.roll(three, 2, axis) + pltpu.roll(three, size - 2, axis)


def bend(da, db, haa, hbb, dab):
    qa = 0.25 * da * da
    qb = 0.25 * db * db
    root = lax.rsqrt(1.0 + qa + qb)
    upper = haa * (1.0 + qb) + hbb * (1.0 + qa) - 0.125 * (da * db * dab)
    return upper * (root * root * root)


def kernel(
    frac_in, dir_in, div_in, th_in, tl_in, ratio_in, weight_in,
    kap_out, high_out, low_out,
    fx, dirs, divs, th, tl, ratio, weight,
    axc, axd, axs, ayc, ayd, ays, kap, shi, slo, spec, mhi, mlo,
    lus, rc, pu, ru, od, rd, sd, ab,
    in_sem, out_sem, fs_sem, fr_sem, c_sem, u_sem, round_sem,
):
    me = lax.axis_index("gz")
    core = lax.rem(me, 2)
    chip = lax.div(me, 2)
    sibling = me + 1 - 2 * core
    has_below = me > 0
    has_above = me < DEVICES - 1
    cross = me - 1 + 2 * core
    has_cross = jnp.logical_and(cross >= 0, cross < DEVICES)

    digits = [lax.div(chip, 16), lax.rem(lax.div(chip, 4), 4), lax.rem(chip, 4)]
    parts = [[lax.rem(v + d, 4) * scale for d in range(4)] for v, scale in zip(digits, (16, 4, 1))]
    reach = (0, 1, 2, 1)
    offsets = [(a, b, c) for a in range(4) for b in range(4) for c in range(4) if a or b or c]
    offsets.sort(key=lambda o: -sum(reach[d] for d in o))

    def chips_at(places):
        return [parts[0][a] + parts[1][b] + parts[2][c] for a, b, c in places]

    others = chips_at(offsets)
    nearest = chips_at([(1, 0, 0), (3, 0, 0), (0, 1, 0), (0, 3, 0), (0, 0, 1), (0, 0, 3)])
    y_ring = chips_at([(0, 2, 0), (0, 1, 0), (0, 3, 0)])
    z_ring = chips_at([(2, 0, 0), (1, 0, 0), (3, 0, 0)])

    loads = [
        pltpu.make_async_copy(frac_in, fx.at[pl.ds(3, SLAB)], in_sem.at[0]),
        pltpu.make_async_copy(dir_in, dirs, in_sem.at[1]),
        pltpu.make_async_copy(div_in, divs, in_sem.at[2]),
        pltpu.make_async_copy(th_in, th, in_sem.at[3]),
        pltpu.make_async_copy(tl_in, tl, in_sem.at[4]),
        pltpu.make_async_copy(ratio_in, ratio, in_sem.at[5]),
        pltpu.make_async_copy(weight_in, weight, in_sem.at[6]),
    ]
    for load in loads:
        load.start()

    barrier = pltpu.get_barrier_semaphore()

    def greet(target):
        pl.semaphore_signal(barrier, inc=1, device_id=(target,), device_id_type=MESH)

    greet(sibling)

    @pl.when(has_cross)
    def _():
        greet(cross)

    for other in nearest:
        greet(2 * other + core)

    peers = 1 + len(nearest)
    pl.semaphore_wait(barrier, jnp.where(has_cross, peers + 1, peers))

    def hail(i, chips):
        for other in chips:
            pl.semaphore_signal(
                round_sem.at[i], inc=1, device_id=(2 * other + core,), device_id_type=MESH
            )

    def frac_above(j):
        return pltpu.make_async_remote_copy(
            src_ref=frac_in.at[3 - j], dst_ref=fx.at[2 - j], send_sem=fs_sem.at[0, j],
            recv_sem=fr_sem.at[0, j], device_id=(me + 1,), device_id_type=MESH,
        )

    def frac_below(j):
        return pltpu.make_async_remote_copy(
            src_ref=frac_in.at[j], dst_ref=fx.at[7 + j], send_sem=fs_sem.at[1, j],
            recv_sem=fr_sem.at[1, j], device_id=(me - 1,), device_id_type=MESH,
        )

    @pl.when(has_above)
    def _():
        for j in range(3):
            frac_above(j).start()

    @pl.when(has_below)
    def _():
        for j in range(3):
            frac_below(j).start()

    hail(0, nearest)
    zero_plane = jnp.zeros((SIZE, SIZE), F32)

    @pl.when(jnp.logical_not(has_below))
    def _():
        for j in range(3):
            fx[j] = zero_plane

    @pl.when(jnp.logical_not(has_above))
    def _():
        for j in range(3):
            fx[7 + j] = zero_plane

    def flat_heights(t):
        f = fx[t + 3]
        cx = window7(f, 0)
        lift, drop = up(cx, 1), down(cx, 1)
        axc[t + 1] = cx
        axd[t + 1] = lift - drop
        axs[t + 1] = lift + drop - 2.0 * cx
        cy = window7(f, 1)
        lift, drop = up(cy, 0), down(cy, 0)
        ayc[t + 1] = cy
        ayd[t + 1] = lift - drop
        ays[t + 1] = lift + drop - 2.0 * cy

    def flat_bend(t):
        along_x = dirs[t] == 1

        def pick(a, b):
            return jnp.where(along_x, a, b)

        lo = pick(axc[t], ayc[t])
        at = pick(axc[t + 1], ayc[t + 1])
        hi = pick(axc[t + 2], ayc[t + 2])
        d_lo = pick(axd[t], ayd[t])
        d_at = pick(axd[t + 1], ayd[t + 1])
        d_hi = pick(axd[t + 2], ayd[t + 2])
        s_at = pick(axs[t + 1], ays[t + 1])
        kap[t] = bend(hi - lo, d_at, hi + lo - 2.0 * at, s_at, d_hi - d_lo)

    def upright_bend(t):
        h = fx[t]
        for j in range(1, 7):
            h = h + fx[t + j]
        right, left = up(h, 1), down(h, 1)
        db = right - left
        sb = right + left
        plus, minus = up(h, 0), down(h, 0)
        dab = up(db, 0) - down(db, 0)
        value = bend(plus - minus, db, plus + minus - 2.0 * h, sb - 2.0 * h, dab)
        where = dirs[t]
        kap[t] = jnp.where(where == 0, value, jnp.where(where == 3, 0.0, kap[t]))

    def store(t, value):
        shi[t + 1], slo[t + 1] = split(value)

    def source(t):
        f = fx[t + 3]
        k = kap[t]
        face = (k + up(k, 0)) * (up(f, 0) - f)
        total = face - down(face, 0)
        face = (k + up(k, 1)) * (up(f, 1) - f)
        total = total + face - down(face, 1)
        above = jnp.where(t == SLAB - 1, 0.0, kap[jnp.minimum(t + 1, SLAB - 1)])
        below = jnp.where(t == 0, 0.0, kap[jnp.maximum(t - 1, 0)])
        total = total + (k + above) * (fx[t + 4] - f) - (k + below) * (f - fx[t + 2])
        store(t, divs[t] + (0.5 * TENSION) * total)

    def beyond(t, outer, exists):
        scale = jnp.where(exists, 0.5 * TENSION, 0.0)
        store(outer, scale * kap[t] * (fx[t + 3] - fx[outer + 3]))

    def transform(t):
        inner = mm3(shi[t + 1], slo[t + 1], th[...], tl[...])
        ih, il = split(inner)
        spec[t + 1] = mm3(th[...], tl[...], ih, il)

    near = 3 - 3 * core
    step = 2 * core - 1

    def place(d):
        return near + step * d

    near_side = 1 - core
    near_halo = 4 - 5 * core
    far_halo = 5 * core - 1

    def wait_frac(side, j):
        pltpu.make_async_copy(frac_in.at[0], fx.at[0], fr_sem.at[side, j]).wait()

    def wait_far(j):
        @pl.when(has_cross)
        def _():
            wait_frac(core, j)

    loads[0].wait()
    lax.fori_loop(0, SLAB, lambda t, c: (flat_heights(t), c)[1], 0)
    pl.semaphore_wait(round_sem.at[0], len(nearest))
    hail(1, y_ring)
    loads[1].wait()
    lax.fori_loop(1, 3, lambda t, c: (flat_bend(t), c)[1], 0)
    for j in range(3):
        wait_frac(near_side, j)
    flat_heights(near_halo)
    flat_bend(near)
    upright_bend(near)
    for load in loads[2:]:
        load.wait()
    beyond(near, near_halo, True)
    transform(near_halo)
    pl.semaphore_wait(round_sem.at[1], len(y_ring))
    hail(2, z_ring)
    wait_far(0)
    flat_heights(far_halo)
    flat_bend(place(3))
    upright_bend(place(1))
    source(near)
    transform(near)
    wait_far(1)
    upright_bend(place(2))
    source(place(1))
    transform(place(1))
    wait_far(2)
    upright_bend(place(3))
    out_kap = pltpu.make_async_copy(kap, kap_out, out_sem.at[0])
    out_kap.start()
    beyond(place(3), far_halo, has_cross)
    source(place(2))
    source(place(3))
    transform(place(2))
    transform(place(3))
    transform(far_halo)

    def sums(half, i):
        rows = pl.ds(pl.multiple_of(half * 128 + i * ROWS, ROWS), ROWS)
        r = ratio[rows, :]
        f = [spec[t, rows, :] for t in range(SLAB + 2)]
        low, high = f[0], f[SLAB + 1]
        for t in range(1, SLAB + 1):
            low = r * low + f[t]
            high = r * high + f[SLAB + 1 - t]
        low = r * low + f[SLAB + 1]
        high = r * high + f[0]
        return low, high

    def sums_out(i, carry):
        rows = pl.ds(pl.multiple_of(i * ROWS, ROWS), ROWS)
        lus[0, rows, :], lus[1, rows, :] = sums(1 - core, i)
        return carry

    lax.fori_loop(0, 4, sums_out, 0)
    send_c = pltpu.make_async_remote_copy(
        src_ref=lus, dst_ref=rc.at[core], send_sem=c_sem.at[0], recv_sem=c_sem.at[1],
        device_id=(sibling,), device_id_type=MESH,
    )
    send_c.start()

    def sums_own(i, carry):
        rows = pl.ds(pl.multiple_of(i * ROWS, ROWS), ROWS)
        rc[core, 0, rows, :], rc[core, 1, rows, :] = sums(core, i)
        return carry

    lax.fori_loop(0, 4, sums_own, 0)
    send_c.wait_recv()

    def power4(x):
        x = x * x
        return x * x

    first_half = lax.broadcasted_iota(jnp.int32, (8, 128), 0) < 4

    def swap(x):
        return pltpu.roll(x, 4, 0)

    def cut(i, carry):
        rows = pl.ds(pl.multiple_of(i * 8, 8), 8)
        rho = power4(ratio[pl.ds(pl.multiple_of(core * 128 + i * 8, 8), 8), :])
        low = rho * rc[0, 0, rows, :] + rc[1, 0, rows, :]
        high = rc[0, 1, rows, :] + rho * rc[1, 1, rows, :]
        for lane in range(2):
            lt = low[:, 128 * lane : 128 * lane + 128]
            ut = high[:, 128 * lane : 128 * lane + 128]
            pu[i * 4 + lane * 2] = jnp.where(first_half, lt, swap(ut))
            pu[i * 4 + lane * 2 + 1] = jnp.where(first_half, swap(lt), ut)
        return carry

    lax.fori_loop(0, 16, cut, 0, unroll=4)

    def send_part(other, level, source_ref, target_ref):
        return pltpu.make_async_remote_copy(
            src_ref=source_ref.at[other], dst_ref=target_ref.at[chip], send_sem=u_sem.at[level, 0],
            recv_sem=u_sem.at[level, 1], device_id=(2 * other + core,), device_id_type=MESH,
        )

    def wait_parts(level, way):
        span = pl.ds(0, CHIPS - 1)
        pltpu.make_async_copy(pu.at[span], ru.at[span], u_sem.at[level, way]).wait()

    pl.semaphore_wait(round_sem.at[2], len(z_ring))
    for other in others:
        send_part(other, 0, pu, ru).start()
    ru[chip] = pu[chip]
    wait_parts(0, 1)

    tile_row = lax.div(chip, 4)
    tile_lane = lax.rem(lax.div(chip, 2), 2)
    tile_half = lax.rem(chip, 2)
    rt = ratio[
        pl.ds(pl.multiple_of(core * 128 + tile_row * 8, 8), 8),
        pl.ds(pl.multiple_of(tile_lane * 128, 128), 128),
    ]
    keep = first_half == (tile_half == 0)
    rt = jnp.where(keep, rt, swap(rt))
    r8 = power4(rt * rt)
    r64 = power4(r8 * r8)
    r513 = power4(r64 * r64) * rt
    merged = [jnp.where(first_half, ru[j], ru[CHIPS - 1 - j]) for j in range(CHIPS)]
    blocks = []
    for b in range(8):
        total = merged[8 * b]
        for j in range(1, 8):
            total = r8 * total + merged[8 * b + j]
        blocks.append(total)
    ends = blocks[0]
    for b in range(1, 8):
        ends = r64 * ends + blocks[b]
    walls = (swap(ends) - r513 * ends) / (1.0 - r513 * r513)
    starts = [-(rt * walls)]
    for b in range(7):
        starts.append(r64 * starts[b] + blocks[b])
    sweep = []
    for b in range(8):
        sweep.append(starts[b])
        for j in range(7):
            sweep.append(r8 * sweep[-1] + merged[8 * b + j])
    for j in range(CHIPS):
        od[j] = jnp.where(first_half, sweep[j], sweep[CHIPS - 1 - j])

    for other in others:
        send_part(other, 1, od, rd).start()
    rd[chip] = od[chip]
    wait_parts(1, 1)

    def spread(i, carry):
        rows = pl.ds(pl.multiple_of(i * 8, 8), 8)
        rho = power4(ratio[pl.ds(pl.multiple_of(core * 128 + i * 8, 8), 8), :])
        tiles = [rd[i * 4 + k] for k in range(4)]
        a = jnp.concatenate([jnp.where(first_half, tiles[k], swap(tiles[k + 1])) for k in (0, 2)], axis=1)
        b = jnp.concatenate([jnp.where(first_half, swap(tiles[k]), tiles[k + 1]) for k in (0, 2)], axis=1)
        a_far = rho * a + rc[0, 0, rows, :]
        b_far = rho * b + rc[1, 1, rows, :]
        even = core == 0
        ab[core, 0, rows, :] = jnp.where(even, a, a_far)
        ab[core, 1, rows, :] = jnp.where(even, b_far, b)
        sd[0, rows, :] = jnp.where(even, a_far, a)
        sd[1, rows, :] = jnp.where(even, b, b_far)
        return carry

    lax.fori_loop(0, 16, spread, 0, unroll=4)
    send_d = pltpu.make_async_remote_copy(
        src_ref=sd, dst_ref=ab.at[core], send_sem=c_sem.at[2], recv_sem=c_sem.at[3],
        device_id=(sibling,), device_id_type=MESH,
    )
    send_d.start()

    def modal(half):
        def body(i, carry):
            local = pl.ds(pl.multiple_of(i * ROWS, ROWS), ROWS)
            rows = pl.ds(pl.multiple_of(half * 128 + i * ROWS, ROWS), ROWS)
            r = ratio[rows, :]
            w = weight[rows, :]
            f = [spec[t, rows, :] for t in range(SLAB + 2)]
            rising = [r * f[0] + ab[half, 0, local, :] + f[1]]
            for t in range(1, SLAB):
                rising.append(r * rising[t - 1] + f[t + 1])
            falling = ab[half, 1, local, :] + r * f[SLAB + 1]
            for t in range(SLAB - 1, -1, -1):
                mhi[t, rows, :], mlo[t, rows, :] = split(w * (rising[t] + falling))
                falling = r * (falling + f[t + 1])
            return carry

        lax.fori_loop(0, 4, body, 0, unroll=2)

    modal(core)
    send_d.wait_recv()
    modal(1 - core)

    out_high = pltpu.make_async_copy(mhi, high_out, out_sem.at[1])
    out_low = pltpu.make_async_copy(mlo, low_out, out_sem.at[2])
    out_high.start()
    out_low.start()

    @pl.when(has_above)
    def _():
        for j in range(3):
            frac_above(j).wait_send()

    @pl.when(has_below)
    def _():
        for j in range(3):
            frac_below(j).wait_send()

    send_c.wait_send()
    send_d.wait_send()
    wait_parts(0, 0)
    wait_parts(1, 0)
    out_kap.wait()
    out_high.wait()
    out_low.wait()


def finish(kap_in, high_in, low_in, th_in, tl_in, kap_out, pre_out, kap, mhi, mlo, th, tl, pre, sem):
    loads = [
        pltpu.make_async_copy(source, target, sem.at[1 + i])
        for i, (source, target) in enumerate(((th_in, th), (tl_in, tl), (high_in, mhi), (low_in, mlo)))
    ]
    fetch = pltpu.make_async_copy(kap_in, kap, sem.at[0])
    passing = pltpu.make_async_copy(kap, kap_out, sem.at[9])
    for load in loads:
        load.start()
    fetch.start()
    for load in loads:
        load.wait()
    fetch.wait()
    passing.start()
    stores = []
    for t in range(SLAB):
        ih, il = split(mm3(mhi[t], mlo[t], th[...], tl[...]))
        pre[t] = mm3(th[...], tl[...], ih, il)
        stores.append(pltpu.make_async_copy(pre.at[t], pre_out.at[t], sem.at[5 + t]))
        stores[t].start()
    passing.wait()
    for copy in stores:
        copy.wait()


def shards(fraction, column_dir, divergence):
    shape = (SLAB, SIZE, SIZE)
    plane = (SIZE, SIZE)
    high, low, ratio, weight = tables()
    anywhere = pl.BlockSpec(memory_space=pl.ANY)
    vm = pltpu.VMEM
    dma = pltpu.SemaphoreType.DMA
    high, low = jnp.asarray(high), jnp.asarray(low)
    whole = jax.ShapeDtypeStruct(shape, F32)
    half = jax.ShapeDtypeStruct(shape, BF16)
    params = dict(vmem_limit_bytes=56 * 1024 * 1024)
    six = vm((SLAB + 2,) + plane, F32)
    curvature, modal_high, modal_low = pl.pallas_call(
        kernel,
        out_shape=(whole, half, half),
        in_specs=[anywhere] * 7,
        out_specs=(anywhere,) * 3,
        scratch_shapes=[
            vm((10,) + plane, F32), vm(shape, jnp.int32), vm(shape, F32),
            vm(plane, BF16), vm(plane, BF16), vm(plane, F32), vm(plane, F32),
            six, six, six, six, six, six,
            vm(shape, F32), vm((SLAB + 2,) + plane, BF16), vm((SLAB + 2,) + plane, BF16), six,
            vm(shape, BF16), vm(shape, BF16),
            vm((2, 128, SIZE), F32), vm((2, 2, 128, SIZE), F32),
            vm((CHIPS, 8, 128), F32), vm((CHIPS, 8, 128), F32),
            vm((CHIPS, 8, 128), F32), vm((CHIPS, 8, 128), F32),
            vm((2, 128, SIZE), F32), vm((2, 2, 128, SIZE), F32),
            dma((7,)), dma((3,)), dma((2, 3)), dma((2, 3)), dma((4,)), dma((2, 2)), pltpu.SemaphoreType.REGULAR((3,)),
        ],
        compiler_params=pltpu.CompilerParams(collective_id=0, has_side_effects=True, **params),
    )(fraction, column_dir, divergence, high, low, jnp.asarray(ratio), jnp.asarray(weight))
    return pl.pallas_call(
        finish,
        out_shape=(whole, whole),
        in_specs=[anywhere] * 5,
        out_specs=(anywhere,) * 2,
        scratch_shapes=[
            vm(shape, F32), vm(shape, BF16), vm(shape, BF16), vm(plane, BF16), vm(plane, BF16), vm(shape, F32), dma((10,)),
        ],
        compiler_params=pltpu.CompilerParams(**params),
    )(curvature, modal_high, modal_low, high, low)


def solution(mesh):
    spec = P("gz", None, None)
    return jax.shard_map(
        shards, mesh=mesh, in_specs=(spec, spec, spec), out_specs=(spec, spec), check_vma=False
    )
```

```python
import jax
import jax.numpy as jnp
import numpy as np
from jax import lax
from jax.experimental import pallas as pl
from jax.experimental.pallas import tpu as pltpu
from jax.sharding import PartitionSpec as P

TENSION = 0.2
SHIFT_SCALE = 16.0
SIZE = 256
PLANES = 512
SLAB = 4
DEVICES = 128
CHIPS = 64
ROWS = 32
MESH = pl.DeviceIdType.MESH
F32 = jnp.float32
BF16 = jnp.bfloat16


def tables():
    count = np.arange(SIZE)
    angle = 2.0 * np.pi / SIZE * ((count[:, None] * count[None, :]) % SIZE)
    cas = np.cos(angle) + np.sin(angle)
    high = cas.astype(jnp.bfloat16)
    low = (cas - high.astype(np.float64)).astype(jnp.bfloat16)
    waves = (2.0 * np.sin(np.pi * count / SIZE)) ** 2
    excess = waves[:, None] + waves[None, :] + SHIFT_SCALE / float(PLANES * PLANES)
    root = np.sqrt(excess * (excess + 4.0))
    ratio = 2.0 / (2.0 + excess + root)
    weight = -1.0 / (root * SIZE * SIZE)
    return high, low, ratio.astype(np.float32), weight.astype(np.float32)


def split(x):
    high = x.astype(BF16)
    return high, (x - high.astype(F32)).astype(BF16)


def mm(a, b):
    return jnp.dot(a, b, preferred_element_type=F32)


def mm3(ah, al, bh, bl):
    return mm(ah, bh) + (mm(ah, bl) + mm(al, bh))


def up(x, axis):
    return pltpu.roll(x, x.shape[axis] - 1, axis)


def down(x, axis):
    return pltpu.roll(x, 1, axis)


def window7(x, axis):
    size = x.shape[axis]
    three = x + pltpu.roll(x, 1, axis) + pltpu.roll(x, size - 1, axis)
    return x + pltpu.roll(three, 2, axis) + pltpu.roll(three, size - 2, axis)


def bend(da, db, haa, hbb, dab):
    qa = 0.25 * da * da
    qb = 0.25 * db * db
    root = lax.rsqrt(1.0 + qa + qb)
    upper = haa * (1.0 + qb) + hbb * (1.0 + qa) - 0.125 * (da * db * dab)
    return upper * (root * root * root)


def kernel(
    frac_in, dir_in, div_in, th_in, tl_in, ratio_in, weight_in,
    kap, inner_high, inner_low, th, tl,
    fx, dirs, divs, ratio, weight,
    axc, axd, axs, ayc, ayd, ays, shi, slo, fhi, flo, spec,
    lus, rc, pu, ru, od, rd, sd, ab,
    in_sem, fs_sem, fr_sem, c_sem, u_sem, round_sem,
):
    me = lax.axis_index("gz")
    core = lax.rem(me, 2)
    chip = lax.div(me, 2)
    sibling = me + 1 - 2 * core
    has_below = me > 0
    has_above = me < DEVICES - 1
    cross = me - 1 + 2 * core
    has_cross = jnp.logical_and(cross >= 0, cross < DEVICES)

    digits = [lax.div(chip, 16), lax.rem(lax.div(chip, 4), 4), lax.rem(chip, 4)]
    parts = [[lax.rem(v + d, 4) * scale for d in range(4)] for v, scale in zip(digits, (16, 4, 1))]
    reach = (0, 1, 2, 1)
    offsets = [(a, b, c) for a in range(4) for b in range(4) for c in range(4) if a or b or c]
    offsets.sort(key=lambda o: -sum(reach[d] for d in o))

    def chips_at(places):
        return [parts[0][a] + parts[1][b] + parts[2][c] for a, b, c in places]

    others = chips_at(offsets)
    nearest = chips_at([(1, 0, 0), (3, 0, 0), (0, 1, 0), (0, 3, 0), (0, 0, 1), (0, 0, 3)])
    y_ring = chips_at([(0, 2, 0), (0, 1, 0), (0, 3, 0)])
    z_ring = chips_at([(2, 0, 0), (1, 0, 0), (3, 0, 0)])

    loads = [
        pltpu.make_async_copy(frac_in, fx.at[pl.ds(3, SLAB)], in_sem.at[0]),
        pltpu.make_async_copy(dir_in, dirs, in_sem.at[1]),
        pltpu.make_async_copy(div_in, divs, in_sem.at[2]),
        pltpu.make_async_copy(th_in, th, in_sem.at[3]),
        pltpu.make_async_copy(tl_in, tl, in_sem.at[4]),
        pltpu.make_async_copy(ratio_in, ratio, in_sem.at[5]),
        pltpu.make_async_copy(weight_in, weight, in_sem.at[6]),
    ]
    for load in loads:
        load.start()

    barrier = pltpu.get_barrier_semaphore()

    def greet(target):
        pl.semaphore_signal(barrier, inc=1, device_id=(target,), device_id_type=MESH)

    greet(sibling)

    @pl.when(has_cross)
    def _():
        greet(cross)

    for other in nearest:
        greet(2 * other + core)

    peers = 1 + len(nearest)
    pl.semaphore_wait(barrier, jnp.where(has_cross, peers + 1, peers))

    def hail(i, chips):
        for other in chips:
            pl.semaphore_signal(
                round_sem.at[i], inc=1, device_id=(2 * other + core,), device_id_type=MESH
            )

    def frac_above(j):
        return pltpu.make_async_remote_copy(
            src_ref=frac_in.at[3 - j], dst_ref=fx.at[2 - j], send_sem=fs_sem.at[0, j],
            recv_sem=fr_sem.at[0, j], device_id=(me + 1,), device_id_type=MESH,
        )

    def frac_below(j):
        return pltpu.make_async_remote_copy(
            src_ref=frac_in.at[j], dst_ref=fx.at[7 + j], send_sem=fs_sem.at[1, j],
            recv_sem=fr_sem.at[1, j], device_id=(me - 1,), device_id_type=MESH,
        )

    @pl.when(has_above)
    def _():
        for j in range(3):
            frac_above(j).start()

    @pl.when(has_below)
    def _():
        for j in range(3):
            frac_below(j).start()

    hail(0, nearest)
    zero_plane = jnp.zeros((SIZE, SIZE), F32)

    @pl.when(jnp.logical_not(has_below))
    def _():
        for j in range(3):
            fx[j] = zero_plane

    @pl.when(jnp.logical_not(has_above))
    def _():
        for j in range(3):
            fx[7 + j] = zero_plane

    def flat_heights(t):
        f = fx[t + 3]
        cx = window7(f, 0)
        lift, drop = up(cx, 1), down(cx, 1)
        axc[t + 1] = cx
        axd[t + 1] = lift - drop
        axs[t + 1] = lift + drop - 2.0 * cx
        cy = window7(f, 1)
        lift, drop = up(cy, 0), down(cy, 0)
        ayc[t + 1] = cy
        ayd[t + 1] = lift - drop
        ays[t + 1] = lift + drop - 2.0 * cy

    def flat_bend(t):
        along_x = dirs[t] == 1

        def pick(a, b):
            return jnp.where(along_x, a, b)

        lo = pick(axc[t], ayc[t])
        at = pick(axc[t + 1], ayc[t + 1])
        hi = pick(axc[t + 2], ayc[t + 2])
        d_lo = pick(axd[t], ayd[t])
        d_at = pick(axd[t + 1], ayd[t + 1])
        d_hi = pick(axd[t + 2], ayd[t + 2])
        s_at = pick(axs[t + 1], ays[t + 1])
        kap[t] = bend(hi - lo, d_at, hi + lo - 2.0 * at, s_at, d_hi - d_lo)

    def upright_bend(t):
        h = fx[t]
        for j in range(1, 7):
            h = h + fx[t + j]
        right, left = up(h, 1), down(h, 1)
        db = right - left
        sb = right + left
        plus, minus = up(h, 0), down(h, 0)
        dab = up(db, 0) - down(db, 0)
        value = bend(plus - minus, db, plus + minus - 2.0 * h, sb - 2.0 * h, dab)
        where = dirs[t]
        kap[t] = jnp.where(where == 0, value, jnp.where(where == 3, 0.0, kap[t]))

    def store(t, value):
        shi[t + 1], slo[t + 1] = split(value)

    def source(t):
        f = fx[t + 3]
        k = kap[t]
        face = (k + up(k, 0)) * (up(f, 0) - f)
        total = face - down(face, 0)
        face = (k + up(k, 1)) * (up(f, 1) - f)
        total = total + face - down(face, 1)
        above = jnp.where(t == SLAB - 1, 0.0, kap[jnp.minimum(t + 1, SLAB - 1)])
        below = jnp.where(t == 0, 0.0, kap[jnp.maximum(t - 1, 0)])
        total = total + (k + above) * (fx[t + 4] - f) - (k + below) * (f - fx[t + 2])
        store(t, divs[t] + (0.5 * TENSION) * total)

    def beyond(t, outer, exists):
        scale = jnp.where(exists, 0.5 * TENSION, 0.0)
        store(outer, scale * kap[t] * (fx[t + 3] - fx[outer + 3]))

    def first_stage(planes):
        for t in planes:
            fhi[t + 1], flo[t + 1] = split(mm3(shi[t + 1], slo[t + 1], th[...], tl[...]))

    def second_stage(planes, rows):
        for t in planes:
            spec[t + 1, rows, :] = mm3(th[rows, :], tl[rows, :], fhi[t + 1], flo[t + 1])

    near = 3 - 3 * core
    step = 2 * core - 1

    def place(d):
        return near + step * d

    near_side = 1 - core
    near_halo = 4 - 5 * core
    far_halo = 5 * core - 1

    def wait_frac(side, j):
        pltpu.make_async_copy(frac_in.at[0], fx.at[0], fr_sem.at[side, j]).wait()

    def wait_far(j):
        @pl.when(has_cross)
        def _():
            wait_frac(core, j)

    loads[0].wait()
    lax.fori_loop(0, SLAB, lambda t, c: (flat_heights(t), c)[1], 0)
    pl.semaphore_wait(round_sem.at[0], len(nearest))
    hail(1, y_ring)
    loads[1].wait()
    lax.fori_loop(1, 3, lambda t, c: (flat_bend(t), c)[1], 0)
    for j in range(3):
        wait_frac(near_side, j)
    flat_heights(near_halo)
    flat_bend(near)
    upright_bend(near)
    for load in loads[2:]:
        load.wait()
    beyond(near, near_halo, True)
    pl.semaphore_wait(round_sem.at[1], len(y_ring))
    hail(2, z_ring)
    wait_far(0)
    flat_heights(far_halo)
    flat_bend(place(3))
    upright_bend(place(1))
    source(near)
    wait_far(1)
    upright_bend(place(2))
    source(place(1))
    early = (near_halo, near, place(1))
    first_stage(early)
    second_stage(early, slice(None))
    wait_far(2)
    upright_bend(place(3))
    beyond(place(3), far_halo, has_cross)
    source(place(2))
    source(place(3))
    late = (place(2), place(3), far_halo)
    first_stage(late)

    def half_rows(half):
        return pl.ds(pl.multiple_of(half * 128, 128), 128)

    def sums(half, i):
        rows = pl.ds(pl.multiple_of(half * 128 + i * ROWS, ROWS), ROWS)
        r = ratio[rows, :]
        f = [spec[t, rows, :] for t in range(SLAB + 2)]
        low, high = f[0], f[SLAB + 1]
        for t in range(1, SLAB + 1):
            low = r * low + f[t]
            high = r * high + f[SLAB + 1 - t]
        low = r * low + f[SLAB + 1]
        high = r * high + f[0]
        return low, high

    second_stage(late, half_rows(1 - core))

    def sums_out(i, carry):
        rows = pl.ds(pl.multiple_of(i * ROWS, ROWS), ROWS)
        lus[0, rows, :], lus[1, rows, :] = sums(1 - core, i)
        return carry

    lax.fori_loop(0, 4, sums_out, 0, unroll=True)
    send_c = pltpu.make_async_remote_copy(
        src_ref=lus, dst_ref=rc.at[core], send_sem=c_sem.at[0], recv_sem=c_sem.at[1],
        device_id=(sibling,), device_id_type=MESH,
    )
    send_c.start()

    second_stage(late, half_rows(core))

    def sums_own(i, carry):
        rows = pl.ds(pl.multiple_of(i * ROWS, ROWS), ROWS)
        rc[core, 0, rows, :], rc[core, 1, rows, :] = sums(core, i)
        return carry

    lax.fori_loop(0, 4, sums_own, 0, unroll=True)
    send_c.wait_recv()

    def power4(x):
        x = x * x
        return x * x

    first_half = lax.broadcasted_iota(jnp.int32, (8, 128), 0) < 4

    def swap(x):
        return pltpu.roll(x, 4, 0)

    def cut(i, carry):
        rows = pl.ds(pl.multiple_of(i * 8, 8), 8)
        rho = power4(ratio[pl.ds(pl.multiple_of(core * 128 + i * 8, 8), 8), :])
        low = rho * rc[0, 0, rows, :] + rc[1, 0, rows, :]
        high = rc[0, 1, rows, :] + rho * rc[1, 1, rows, :]
        for lane in range(2):
            lt = low[:, 128 * lane : 128 * lane + 128]
            ut = high[:, 128 * lane : 128 * lane + 128]
            pu[i * 4 + lane * 2] = jnp.where(first_half, lt, swap(ut))
            pu[i * 4 + lane * 2 + 1] = jnp.where(first_half, swap(lt), ut)
        return carry

    lax.fori_loop(0, 16, cut, 0, unroll=4)

    def send_part(other, level, source_ref, target_ref):
        return pltpu.make_async_remote_copy(
            src_ref=source_ref.at[other], dst_ref=target_ref.at[chip], send_sem=u_sem.at[level, 0],
            recv_sem=u_sem.at[level, 1], device_id=(2 * other + core,), device_id_type=MESH,
        )

    def wait_parts(level, way):
        span = pl.ds(0, CHIPS - 1)
        pltpu.make_async_copy(pu.at[span], ru.at[span], u_sem.at[level, way]).wait()

    pl.semaphore_wait(round_sem.at[2], len(z_ring))
    for other in others:
        send_part(other, 0, pu, ru).start()
    ru[chip] = pu[chip]
    wait_parts(0, 1)

    tile_row = lax.div(chip, 4)
    tile_lane = lax.rem(lax.div(chip, 2), 2)
    tile_half = lax.rem(chip, 2)
    rt = ratio[
        pl.ds(pl.multiple_of(core * 128 + tile_row * 8, 8), 8),
        pl.ds(pl.multiple_of(tile_lane * 128, 128), 128),
    ]
    keep = first_half == (tile_half == 0)
    rt = jnp.where(keep, rt, swap(rt))
    r8 = power4(rt * rt)
    r64 = power4(r8 * r8)
    r513 = power4(r64 * r64) * rt
    merged = [jnp.where(first_half, ru[j], ru[CHIPS - 1 - j]) for j in range(CHIPS)]
    blocks = []
    for b in range(8):
        total = merged[8 * b]
        for j in range(1, 8):
            total = r8 * total + merged[8 * b + j]
        blocks.append(total)
    ends = blocks[0]
    for b in range(1, 8):
        ends = r64 * ends + blocks[b]
    walls = (swap(ends) - r513 * ends) / (1.0 - r513 * r513)
    starts = [-(rt * walls)]
    for b in range(7):
        starts.append(r64 * starts[b] + blocks[b])
    sweep = []
    for b in range(8):
        sweep.append(starts[b])
        for j in range(7):
            sweep.append(r8 * sweep[-1] + merged[8 * b + j])
    for j in range(CHIPS):
        od[j] = jnp.where(first_half, sweep[j], sweep[CHIPS - 1 - j])

    for other in others:
        send_part(other, 1, od, rd).start()
    rd[chip] = od[chip]
    wait_parts(1, 1)

    def spread(i, carry):
        rows = pl.ds(pl.multiple_of(i * 8, 8), 8)
        rho = power4(ratio[pl.ds(pl.multiple_of(core * 128 + i * 8, 8), 8), :])
        tiles = [rd[i * 4 + k] for k in range(4)]
        a = jnp.concatenate([jnp.where(first_half, tiles[k], swap(tiles[k + 1])) for k in (0, 2)], axis=1)
        b = jnp.concatenate([jnp.where(first_half, swap(tiles[k]), tiles[k + 1]) for k in (0, 2)], axis=1)
        a_far = rho * a + rc[0, 0, rows, :]
        b_far = rho * b + rc[1, 1, rows, :]
        even = core == 0
        ab[core, 0, rows, :] = jnp.where(even, a, a_far)
        ab[core, 1, rows, :] = jnp.where(even, b_far, b)
        sd[0, rows, :] = jnp.where(even, a_far, a)
        sd[1, rows, :] = jnp.where(even, b, b_far)
        return carry

    lax.fori_loop(0, 16, spread, 0, unroll=4)
    send_d = pltpu.make_async_remote_copy(
        src_ref=sd, dst_ref=ab.at[core], send_sem=c_sem.at[2], recv_sem=c_sem.at[3],
        device_id=(sibling,), device_id_type=MESH,
    )
    send_d.start()

    def modal(half):
        def body(i, carry):
            local = pl.ds(pl.multiple_of(i * ROWS, ROWS), ROWS)
            rows = pl.ds(pl.multiple_of(half * 128 + i * ROWS, ROWS), ROWS)
            r = ratio[rows, :]
            w = weight[rows, :]
            f = [spec[t, rows, :] for t in range(SLAB + 2)]
            rising = [r * f[0] + ab[half, 0, local, :] + f[1]]
            for t in range(1, SLAB):
                rising.append(r * rising[t - 1] + f[t + 1])
            falling = ab[half, 1, local, :] + r * f[SLAB + 1]
            for t in range(SLAB - 1, -1, -1):
                shi[t, rows, :], slo[t, rows, :] = split(w * (rising[t] + falling))
                falling = r * (falling + f[t + 1])
            return carry

        lax.fori_loop(0, 4, body, 0, unroll=True)
        rows = half_rows(half)
        for t in range(SLAB):
            inner_high[t, rows, :], inner_low[t, rows, :] = split(
                mm3(shi[t, rows, :], slo[t, rows, :], th[...], tl[...])
            )

    modal(core)
    send_d.wait_recv()
    modal(1 - core)

    @pl.when(has_above)
    def _():
        for j in range(3):
            frac_above(j).wait_send()

    @pl.when(has_below)
    def _():
        for j in range(3):
            frac_below(j).wait_send()

    send_c.wait_send()
    send_d.wait_send()
    wait_parts(0, 0)
    wait_parts(1, 0)


def finish(kap, high, low, th, tl, kap_out, pre_out, pre, sem):
    passing = pltpu.make_async_copy(kap, kap_out, sem.at[SLAB])
    passing.start()
    stores = []
    for t in range(SLAB):
        pre[t] = mm3(th[...], tl[...], high[t], low[t])
        stores.append(pltpu.make_async_copy(pre.at[t], pre_out.at[t], sem.at[t]))
        stores[t].start()
    passing.wait()
    for copy in stores:
        copy.wait()


def shards(fraction, column_dir, divergence):
    shape = (SLAB, SIZE, SIZE)
    plane = (SIZE, SIZE)
    high, low, ratio, weight = tables()
    far = pl.BlockSpec(memory_space=pltpu.HBM)
    vm = pltpu.VMEM
    close = pl.BlockSpec(memory_space=vm)
    dma = pltpu.SemaphoreType.DMA
    whole = jax.ShapeDtypeStruct(shape, F32)
    half = jax.ShapeDtypeStruct(shape, BF16)
    table = jax.ShapeDtypeStruct(plane, BF16)
    params = dict(vmem_limit_bytes=40 * 1024 * 1024)
    six = vm((SLAB + 2,) + plane, F32)
    six_half = vm((SLAB + 2,) + plane, BF16)
    inputs = (
        fraction, column_dir, divergence, jnp.asarray(high), jnp.asarray(low), jnp.asarray(ratio), jnp.asarray(weight),
    )
    handed_on = pl.pallas_call(
        kernel,
        out_shape=(whole, half, half, table, table),
        in_specs=[far] * 7,
        out_specs=(close,) * 5,
        scratch_shapes=[
            vm((10,) + plane, F32), vm(shape, jnp.int32), vm(shape, F32),
            vm(plane, F32), vm(plane, F32),
            six, six, six, six, six, six,
            six_half, six_half, six_half, six_half, six,
            vm((2, 128, SIZE), F32), vm((2, 2, 128, SIZE), F32),
            vm((CHIPS, 8, 128), F32), vm((CHIPS, 8, 128), F32),
            vm((CHIPS, 8, 128), F32), vm((CHIPS, 8, 128), F32),
            vm((2, 128, SIZE), F32), vm((2, 2, 128, SIZE), F32),
            dma((7,)), dma((2, 3)), dma((2, 3)), dma((4,)), dma((2, 2)), pltpu.SemaphoreType.REGULAR((3,)),
        ],
        compiler_params=pltpu.CompilerParams(collective_id=0, has_side_effects=True, **params),
    )(*(pltpu.with_memory_space_constraint(value, pltpu.HBM) for value in inputs))
    return pl.pallas_call(
        finish,
        out_shape=(whole, whole),
        in_specs=[close] * 5,
        out_specs=(far,) * 2,
        scratch_shapes=[
            vm(shape, F32), dma((SLAB + 1,)),
        ],
        compiler_params=pltpu.CompilerParams(**params),
    )(*handed_on)


def solution(mesh):
    spec = P("gz", None, None)
    return jax.shard_map(
        shards, mesh=mesh, in_specs=(spec, spec, spec), out_specs=(spec, spec), check_vma=False
    )
```

```python
import jax
import jax.numpy as jnp
import numpy as np
from jax import lax
from jax.experimental import pallas as pl
from jax.experimental.pallas import tpu as pltpu
from jax.sharding import PartitionSpec as P

TENSION = 0.2
SHIFT_SCALE = 16.0
SIZE = 256
PLANES = 512
SLAB = 4
DEVICES = 128
CHIPS = 64
ROWS = 32
PIECES = ((0, 80), (80, 144), (144, 208), (208, 256))
BENT = ((8, 72), (72, 136), (136, 200), (200, 264))
FED = ((16, 64), (64, 128), (128, 192), (192, 272))
MESH = pl.DeviceIdType.MESH
F32 = jnp.float32
BF16 = jnp.bfloat16


def tables():
    count = np.arange(SIZE)
    angle = 2.0 * np.pi / SIZE * ((count[:, None] * count[None, :]) % SIZE)
    cas = np.cos(angle) + np.sin(angle)
    high = cas.astype(jnp.bfloat16)
    low = (cas - high.astype(np.float64)).astype(jnp.bfloat16)
    waves = (2.0 * np.sin(np.pi * count / SIZE)) ** 2
    excess = waves[:, None] + waves[None, :] + SHIFT_SCALE / float(PLANES * PLANES)
    root = np.sqrt(excess * (excess + 4.0))
    ratio = 2.0 / (2.0 + excess + root)
    weight = -1.0 / (root * SIZE * SIZE)
    return high, low, ratio.astype(np.float32), weight.astype(np.float32)


def split(x):
    high = x.astype(BF16)
    return high, (x - high.astype(F32)).astype(BF16)


def mm(a, b):
    return jnp.dot(a, b, preferred_element_type=F32)


def mm3(ah, al, bh, bl):
    return mm(ah, bh) + (mm(ah, bl) + mm(al, bh))


def up(x, axis):
    return pltpu.roll(x, x.shape[axis] - 1, axis)


def down(x, axis):
    return pltpu.roll(x, 1, axis)


def window7(x, axis):
    size = x.shape[axis]
    three = x + pltpu.roll(x, 1, axis) + pltpu.roll(x, size - 1, axis)
    return x + pltpu.roll(three, 2, axis) + pltpu.roll(three, size - 2, axis)


def bend(da, db, haa, hbb, dab):
    qa = 0.25 * da * da
    qb = 0.25 * db * db
    root = lax.rsqrt(1.0 + qa + qb)
    upper = haa * (1.0 + qb) + hbb * (1.0 + qa) - 0.125 * (da * db * dab)
    return upper * (root * root * root)


def kernel(
    frac_in, dir_in, div_in, th_in, tl_in, ratio_in, weight_in,
    kap, inner_high, inner_low, th, tl,
    fx, dirs, divs, ratio, weight,
    axc, axd, axs, ayc, ayd, ays, shi, slo, fhi, flo, spec, part, heights,
    lus, rc, pu, ru, od, rd, sd, ab,
    in_sem, fs_sem, fr_sem, c_sem, u_sem, round_sem,
):
    me = lax.axis_index("gz")
    core = lax.rem(me, 2)
    chip = lax.div(me, 2)
    sibling = me + 1 - 2 * core
    has_below = me > 0
    has_above = me < DEVICES - 1
    cross = me - 1 + 2 * core
    has_cross = jnp.logical_and(cross >= 0, cross < DEVICES)

    digits = [lax.div(chip, 16), lax.rem(lax.div(chip, 4), 4), lax.rem(chip, 4)]
    parts = [[lax.rem(v + d, 4) * scale for d in range(4)] for v, scale in zip(digits, (16, 4, 1))]
    reach = (0, 1, 2, 1)
    offsets = [(a, b, c) for a in range(4) for b in range(4) for c in range(4) if a or b or c]
    offsets.sort(key=lambda o: -sum(reach[d] for d in o))

    def chips_at(places):
        return [parts[0][a] + parts[1][b] + parts[2][c] for a, b, c in places]

    others = chips_at(offsets)
    nearest = chips_at([(1, 0, 0), (3, 0, 0), (0, 1, 0), (0, 3, 0), (0, 0, 1), (0, 0, 3)])
    y_ring = chips_at([(0, 2, 0), (0, 1, 0), (0, 3, 0)])
    z_ring = chips_at([(2, 0, 0), (1, 0, 0), (3, 0, 0)])

    barrier = pltpu.get_barrier_semaphore()

    def greet(target):
        pl.semaphore_signal(barrier, inc=1, device_id=(target,), device_id_type=MESH)

    @pl.when(has_cross)
    def _():
        greet(cross)

    greet(sibling)
    for other in nearest:
        greet(2 * other + core)

    loads = [
        pltpu.make_async_copy(frac_in, fx.at[pl.ds(3, SLAB)], in_sem.at[0]),
        pltpu.make_async_copy(dir_in, dirs, in_sem.at[1]),
        pltpu.make_async_copy(div_in, divs, in_sem.at[2]),
        pltpu.make_async_copy(th_in, th, in_sem.at[3]),
        pltpu.make_async_copy(tl_in, tl, in_sem.at[4]),
        pltpu.make_async_copy(ratio_in, ratio, in_sem.at[5]),
        pltpu.make_async_copy(weight_in, weight, in_sem.at[6]),
    ]
    for load in loads:
        load.start()

    peers = 1 + len(nearest)
    pl.semaphore_wait(barrier, jnp.where(has_cross, peers + 1, peers))

    def hail(i, chips):
        for other in chips:
            pl.semaphore_signal(
                round_sem.at[i], inc=1, device_id=(2 * other + core,), device_id_type=MESH
            )

    def halo_copies(side):
        for piece in range(2 + len(PIECES)):
            j = min(piece, 2)
            first, last = (0, SIZE) if piece < 2 else PIECES[piece - 2]
            rows = pl.ds(first, last - first)
            source, target = (3 - j, 2 - j) if side == 0 else (j, 7 + j)
            yield pltpu.make_async_remote_copy(
                src_ref=frac_in.at[source, rows], dst_ref=fx.at[target, rows],
                send_sem=fs_sem.at[side, piece], recv_sem=fr_sem.at[side, piece],
                device_id=(me + 1 - 2 * side,), device_id_type=MESH,
            )

    def send_halo(side):
        for copy in halo_copies(side):
            copy.start()

    @pl.when(jnp.logical_and(core == 0, has_below))
    def _():
        send_halo(1)

    @pl.when(core == 0)
    def _():
        send_halo(0)

    @pl.when(jnp.logical_and(core == 1, has_above))
    def _():
        send_halo(0)

    @pl.when(core == 1)
    def _():
        send_halo(1)

    hail(0, nearest)
    zero_plane = jnp.zeros((SIZE, SIZE), F32)

    @pl.when(jnp.logical_not(has_below))
    def _():
        for j in range(3):
            fx[j] = zero_plane

    @pl.when(jnp.logical_not(has_above))
    def _():
        for j in range(3):
            fx[7 + j] = zero_plane

    def flat_heights(t):
        f = fx[t + 3]
        cx = window7(f, 0)
        lift, drop = up(cx, 1), down(cx, 1)
        axc[t + 1] = cx
        axd[t + 1] = lift - drop
        axs[t + 1] = lift + drop - 2.0 * cx
        cy = window7(f, 1)
        lift, drop = up(cy, 0), down(cy, 0)
        ayc[t + 1] = cy
        ayd[t + 1] = lift - drop
        ays[t + 1] = lift + drop - 2.0 * cy

    def flat_bend(t):
        along_x = dirs[t] == 1

        def pick(a, b):
            return jnp.where(along_x, a, b)

        lo = pick(axc[t], ayc[t])
        at = pick(axc[t + 1], ayc[t + 1])
        hi = pick(axc[t + 2], ayc[t + 2])
        d_lo = pick(axd[t], ayd[t])
        d_at = pick(axd[t + 1], ayd[t + 1])
        d_hi = pick(axd[t + 2], ayd[t + 2])
        s_at = pick(axs[t + 1], ays[t + 1])
        kap[t] = bend(hi - lo, d_at, hi + lo - 2.0 * at, s_at, d_hi - d_lo)

    def upright(h):
        right, left = up(h, 1), down(h, 1)
        db = right - left
        sb = right + left
        plus, minus = up(h, 0), down(h, 0)
        dab = up(db, 0) - down(db, 0)
        return bend(plus - minus, db, plus + minus - 2.0 * h, sb - 2.0 * h, dab)

    def upright_bend(t):
        h = fx[t]
        for j in range(1, 7):
            h = h + fx[t + j]
        value = upright(h)
        where = dirs[t]
        kap[t] = jnp.where(where == 0, value, jnp.where(where == 3, 0.0, kap[t]))

    def store(t, value):
        shi[t + 1], slo[t + 1] = split(value)

    def source(t, hidden):
        f = fx[t + 3]
        k = kap[t]
        face = (k + up(k, 0)) * (up(f, 0) - f)
        total = face - down(face, 0)
        face = (k + up(k, 1)) * (up(f, 1) - f)
        total = total + face - down(face, 1)

        def beside(other):
            shown = jnp.logical_and(jnp.logical_and(other >= 0, other < SLAB), other != hidden)
            return jnp.where(shown, kap[jnp.clip(other, 0, SLAB - 1)], 0.0)

        total = total + (k + beside(t + 1)) * (fx[t + 4] - f) - (k + beside(t - 1)) * (f - fx[t + 2])
        return divs[t] + (0.5 * TENSION) * total

    def beyond(t, outer):
        store(outer, (0.5 * TENSION) * kap[t] * (fx[t + 3] - fx[outer + 3]))

    def ring(ref, t, first, last):
        if first < 0:
            return jnp.concatenate([ref[t, first + SIZE : SIZE], ref[t, 0:last]], axis=0)
        if last > SIZE:
            return jnp.concatenate([ref[t, first:SIZE], ref[t, 0 : last - SIZE]], axis=0)
        return ref[t, first:last]

    def put(ref, t, first, last, value):
        if last > SIZE:
            ref[t, first:SIZE] = value[: SIZE - first]
            ref[t, 0 : last - SIZE] = value[SIZE - first :]
        else:
            ref[t, first:last] = value

    def inner_rows(x):
        return x[8 : x.shape[0] - 8]

    def first_stage(planes):
        for t in planes:
            fhi[t + 1], flo[t + 1] = split(mm3(shi[t + 1], slo[t + 1], th[...], tl[...]))

    def second_stage(planes, rows):
        for t in planes:
            spec[t + 1, rows, :] = mm3(th[rows, :], tl[rows, :], fhi[t + 1], flo[t + 1])

    near = 3 - 3 * core
    step = 2 * core - 1

    def place(d):
        return near + step * d

    near_side = 1 - core
    near_halo = 4 - 5 * core
    far_halo = 5 * core - 1

    def wait_frac(side, piece):
        first, last = (0, SIZE) if piece < 2 else PIECES[piece - 2]
        rows = pl.ds(first, last - first)
        pltpu.make_async_copy(frac_in.at[0, rows], fx.at[0, rows], fr_sem.at[side, piece]).wait()

    def wait_far(piece):
        @pl.when(has_cross)
        def _():
            wait_frac(core, piece)

    loads[0].wait()
    lax.fori_loop(0, SLAB, lambda t, c: (flat_heights(t), c)[1], 0)
    pl.semaphore_wait(round_sem.at[0], len(nearest))
    hail(1, y_ring)
    loads[1].wait()
    lax.fori_loop(1, 3, lambda t, c: (flat_bend(t), c)[1], 0)
    for piece in range(2 + len(PIECES)):
        wait_frac(near_side, piece)
    flat_heights(near_halo)
    flat_bend(near)
    upright_bend(near)
    for load in loads[2:]:
        load.wait()
    beyond(near, near_halo)
    pl.semaphore_wait(round_sem.at[1], len(y_ring))
    hail(2, z_ring)
    wait_far(0)
    flat_heights(far_halo)
    flat_bend(place(3))
    upright_bend(place(1))
    store(near, source(near, -1))
    wait_far(1)
    upright_bend(place(2))
    store(place(1), source(place(1), -1))
    early = (near_halo, near, place(1))
    first_stage(early)
    second_stage(early, slice(None))
    outer, third = place(3), place(2)
    part[0] = source(third, outer)
    summed = fx[1 + 2 * core]
    for j in range(1, 6):
        summed = summed + fx[1 + 2 * core + j]
    heights[0] = summed
    scale = jnp.where(has_cross, 0.5 * TENSION, 0.0)
    late = (third, outer, far_halo)

    for c in range(len(PIECES)):
        wait_far(2 + c)
        a, b = BENT[c]
        h = ring(heights, 0, a - 8, b + 8) + ring(fx, 9 * core, a - 8, b + 8)
        value = inner_rows(upright(h))
        where = ring(dirs, outer, a, b)
        flat = ring(kap, outer, a, b)
        put(kap, outer, a, b, jnp.where(where == 0, value, jnp.where(where == 3, 0.0, flat)))
        a, b = FED[c]
        f, k = ring(fx, outer + 3, a - 8, b + 8), ring(kap, outer, a - 8, b + 8)
        face = (k + up(k, 0)) * (up(f, 0) - f)
        total = inner_rows(face - down(face, 0))
        f, k = inner_rows(f), inner_rows(k)
        face = (k + up(k, 1)) * (up(f, 1) - f)
        total = total + face - down(face, 1)
        f_third, f_halo = ring(fx, third + 3, a, b), ring(fx, far_halo + 3, a, b)
        total = total + (ring(kap, third, a, b) + k) * (f_third - f) + k * (f_halo - f)
        fed = (
            ring(part, 0, a, b) + (0.5 * TENSION) * k * (f - f_third),
            ring(divs, outer, a, b) + (0.5 * TENSION) * total,
            scale * k * (f - f_halo),
        )
        for t, rows in zip(late, fed):
            high, low = split(mm3(*split(rows), th[...], tl[...]))
            put(fhi, t + 1, a, b, high)
            put(flo, t + 1, a, b, low)

    def half_rows(half):
        return pl.ds(pl.multiple_of(half * 128, 128), 128)

    def sums(half, i):
        rows = pl.ds(pl.multiple_of(half * 128 + i * ROWS, ROWS), ROWS)
        r = ratio[rows, :]
        f = [spec[t, rows, :] for t in range(SLAB + 2)]
        low, high = f[0], f[SLAB + 1]
        for t in range(1, SLAB + 1):
            low = r * low + f[t]
            high = r * high + f[SLAB + 1 - t]
        low = r * low + f[SLAB + 1]
        high = r * high + f[0]
        return low, high

    second_stage(late, half_rows(1 - core))

    def give(q):
        rows = pl.ds(64 * q, 64)
        return pltpu.make_async_remote_copy(
            src_ref=lus.at[:, rows], dst_ref=rc.at[core, :, rows], send_sem=c_sem.at[0, q], recv_sem=c_sem.at[1, q],
            device_id=(sibling,), device_id_type=MESH,
        )

    for q in range(2):
        for i in (2 * q, 2 * q + 1):
            rows = pl.ds(i * ROWS, ROWS)
            lus[0, rows, :], lus[1, rows, :] = sums(1 - core, i)
        give(q).start()

    second_stage(late, half_rows(core))
    for i in range(4):
        rows = pl.ds(i * ROWS, ROWS)
        rc[core, 0, rows, :], rc[core, 1, rows, :] = sums(core, i)

    def power4(x):
        x = x * x
        return x * x

    first_half = lax.broadcasted_iota(jnp.int32, (8, 128), 0) < 4

    def swap(x):
        return pltpu.roll(x, 4, 0)

    def cut(i, carry):
        rows = pl.ds(pl.multiple_of(i * 8, 8), 8)
        rho = power4(ratio[pl.ds(pl.multiple_of(core * 128 + i * 8, 8), 8), :])
        low = rho * rc[0, 0, rows, :] + rc[1, 0, rows, :]
        high = rc[0, 1, rows, :] + rho * rc[1, 1, rows, :]
        for lane in range(2):
            lt = low[:, 128 * lane : 128 * lane + 128]
            ut = high[:, 128 * lane : 128 * lane + 128]
            pu[i * 4 + lane * 2] = jnp.where(first_half, lt, swap(ut))
            pu[i * 4 + lane * 2 + 1] = jnp.where(first_half, swap(lt), ut)
        return carry

    for q in range(2):
        give(q).wait_recv()
        lax.fori_loop(8 * q, 8 * q + 8, cut, 0, unroll=True)

    def send_part(other, level, source_ref, target_ref):
        return pltpu.make_async_remote_copy(
            src_ref=source_ref.at[other], dst_ref=target_ref.at[chip], send_sem=u_sem.at[level, 0],
            recv_sem=u_sem.at[level, 1], device_id=(2 * other + core,), device_id_type=MESH,
        )

    def wait_parts(level, way):
        span = pl.ds(0, CHIPS - 1)
        pltpu.make_async_copy(pu.at[span], ru.at[span], u_sem.at[level, way]).wait()

    pl.semaphore_wait(round_sem.at[2], len(z_ring))
    for other in others:
        send_part(other, 0, pu, ru).start()
    ru[chip] = pu[chip]
    wait_parts(0, 1)

    tile_row = lax.div(chip, 4)
    tile_lane = lax.rem(lax.div(chip, 2), 2)
    tile_half = lax.rem(chip, 2)
    rt = ratio[
        pl.ds(pl.multiple_of(core * 128 + tile_row * 8, 8), 8),
        pl.ds(pl.multiple_of(tile_lane * 128, 128), 128),
    ]
    keep = first_half == (tile_half == 0)
    rt = jnp.where(keep, rt, swap(rt))
    r8 = power4(rt * rt)
    r64 = power4(r8 * r8)
    r513 = power4(r64 * r64) * rt
    merged = [jnp.where(first_half, ru[j], ru[CHIPS - 1 - j]) for j in range(CHIPS)]
    blocks = []
    for b in range(8):
        total = merged[8 * b]
        for j in range(1, 8):
            total = r8 * total + merged[8 * b + j]
        blocks.append(total)
    ends = blocks[0]
    for b in range(1, 8):
        ends = r64 * ends + blocks[b]
    walls = (swap(ends) - r513 * ends) / (1.0 - r513 * r513)
    starts = [-(rt * walls)]
    for b in range(7):
        starts.append(r64 * starts[b] + blocks[b])
    sweep = []
    for b in range(8):
        sweep.append(starts[b])
        for j in range(7):
            sweep.append(r8 * sweep[-1] + merged[8 * b + j])
    for j in range(CHIPS):
        od[j] = jnp.where(first_half, sweep[j], sweep[CHIPS - 1 - j])

    for other in others:
        send_part(other, 1, od, rd).start()
    rd[chip] = od[chip]
    wait_parts(1, 1)

    def spread(i, carry):
        rows = pl.ds(pl.multiple_of(i * 8, 8), 8)
        rho = power4(ratio[pl.ds(pl.multiple_of(core * 128 + i * 8, 8), 8), :])
        tiles = [rd[i * 4 + k] for k in range(4)]
        a = jnp.concatenate([jnp.where(first_half, tiles[k], swap(tiles[k + 1])) for k in (0, 2)], axis=1)
        b = jnp.concatenate([jnp.where(first_half, swap(tiles[k]), tiles[k + 1]) for k in (0, 2)], axis=1)
        a_far = rho * a + rc[0, 0, rows, :]
        b_far = rho * b + rc[1, 1, rows, :]
        even = core == 0
        ab[core, 0, rows, :] = jnp.where(even, a, a_far)
        ab[core, 1, rows, :] = jnp.where(even, b_far, b)
        sd[0, rows, :] = jnp.where(even, a_far, a)
        sd[1, rows, :] = jnp.where(even, b, b_far)
        return carry

    def hand(q):
        rows = pl.ds(64 * q, 64)
        return pltpu.make_async_remote_copy(
            src_ref=sd.at[:, rows], dst_ref=ab.at[core, :, rows], send_sem=c_sem.at[2, q], recv_sem=c_sem.at[3, q],
            device_id=(sibling,), device_id_type=MESH,
        )

    for q in range(2):
        lax.fori_loop(8 * q, 8 * q + 8, spread, 0, unroll=True)
        hand(q).start()

    def modal(half):
        def body(i, carry):
            local = pl.ds(pl.multiple_of(i * ROWS, ROWS), ROWS)
            rows = pl.ds(pl.multiple_of(half * 128 + i * ROWS, ROWS), ROWS)
            r = ratio[rows, :]
            w = weight[rows, :]
            f = [spec[t, rows, :] for t in range(SLAB + 2)]
            rising = [r * f[0] + ab[half, 0, local, :] + f[1]]
            for t in range(1, SLAB):
                rising.append(r * rising[t - 1] + f[t + 1])
            falling = ab[half, 1, local, :] + r * f[SLAB + 1]
            for t in range(SLAB - 1, -1, -1):
                shi[t, rows, :], slo[t, rows, :] = split(w * (rising[t] + falling))
                falling = r * (falling + f[t + 1])
            return carry

        lax.fori_loop(0, 4, body, 0, unroll=True)
        rows = half_rows(half)
        for t in range(SLAB):
            inner_high[t, rows, :], inner_low[t, rows, :] = split(
                mm3(shi[t, rows, :], slo[t, rows, :], th[...], tl[...])
            )

    modal(core)
    for q in range(2):
        hand(q).wait_recv()
    modal(1 - core)

    @pl.when(has_above)
    def _():
        for copy in halo_copies(0):
            copy.wait_send()

    @pl.when(has_below)
    def _():
        for copy in halo_copies(1):
            copy.wait_send()

    for q in range(2):
        give(q).wait_send()
        hand(q).wait_send()
    wait_parts(0, 0)
    wait_parts(1, 0)


def finish(kap, high, low, th, tl, kap_out, pre_out, pre, sem):
    passing = pltpu.make_async_copy(kap, kap_out, sem.at[SLAB])
    passing.start()
    stores = []
    for t in range(SLAB):
        pre[t] = mm3(th[...], tl[...], high[t], low[t])
        stores.append(pltpu.make_async_copy(pre.at[t], pre_out.at[t], sem.at[t]))
        stores[t].start()
    passing.wait()
    for copy in stores:
        copy.wait()


def shards(fraction, column_dir, divergence):
    shape = (SLAB, SIZE, SIZE)
    plane = (SIZE, SIZE)
    high, low, ratio, weight = tables()
    far = pl.BlockSpec(memory_space=pltpu.HBM)
    vm = pltpu.VMEM
    close = pl.BlockSpec(memory_space=vm)
    dma = pltpu.SemaphoreType.DMA
    whole = jax.ShapeDtypeStruct(shape, F32)
    half = jax.ShapeDtypeStruct(shape, BF16)
    table = jax.ShapeDtypeStruct(plane, BF16)
    params = dict(vmem_limit_bytes=40 * 1024 * 1024)
    six = vm((SLAB + 2,) + plane, F32)
    six_half = vm((SLAB + 2,) + plane, BF16)
    inputs = (
        fraction, column_dir, divergence, jnp.asarray(high), jnp.asarray(low), jnp.asarray(ratio), jnp.asarray(weight),
    )
    handed_on = pl.pallas_call(
        kernel,
        out_shape=(whole, half, half, table, table),
        in_specs=[far] * 7,
        out_specs=(close,) * 5,
        scratch_shapes=[
            vm((10,) + plane, F32), vm(shape, jnp.int32), vm(shape, F32),
            vm(plane, F32), vm(plane, F32),
            six, six, six, six, six, six,
            six_half, six_half, six_half, six_half, six,
            vm((1,) + plane, F32), vm((1,) + plane, F32),
            vm((2, 128, SIZE), F32), vm((2, 2, 128, SIZE), F32),
            vm((CHIPS, 8, 128), F32), vm((CHIPS, 8, 128), F32),
            vm((CHIPS, 8, 128), F32), vm((CHIPS, 8, 128), F32),
            vm((2, 128, SIZE), F32), vm((2, 2, 128, SIZE), F32),
            dma((7,)), dma((2, 6)), dma((2, 6)), dma((4, 2)), dma((2, 2)), pltpu.SemaphoreType.REGULAR((3,)),
        ],
        compiler_params=pltpu.CompilerParams(collective_id=0, has_side_effects=True, **params),
    )(*(pltpu.with_memory_space_constraint(value, pltpu.HBM) for value in inputs))
    return pl.pallas_call(
        finish,
        out_shape=(whole, whole),
        in_specs=[close] * 5,
        out_specs=(far,) * 2,
        scratch_shapes=[
            vm(shape, F32), dma((SLAB + 1,)),
        ],
        compiler_params=pltpu.CompilerParams(**params),
    )(*handed_on)


def solution(mesh):
    spec = P("gz", None, None)
    return jax.shard_map(
        shards, mesh=mesh, in_specs=(spec, spec, spec), out_specs=(spec, spec), check_vma=False
    )
```

```python
import jax
import jax.numpy as jnp
import numpy as np
from jax import lax
from jax.experimental import pallas as pl
from jax.experimental.pallas import tpu as pltpu
from jax.sharding import PartitionSpec as P

TENSION = 0.2
SHIFT_SCALE = 16.0
SIZE = 256
PLANES = 512
SLAB = 4
DEVICES = 128
CHIPS = 64
ROWS = 32
PIECES = ((0, 96), (96, 192), (192, 256))
BENT = ((8, 88), (88, 184), (184, 264))
FED = ((16, 80), (80, 176), (176, 272))
MESH = pl.DeviceIdType.MESH
F32 = jnp.float32
BF16 = jnp.bfloat16


def tables():
    count = np.arange(SIZE)
    angle = 2.0 * np.pi / SIZE * ((count[:, None] * count[None, :]) % SIZE)
    cas = np.cos(angle) + np.sin(angle)
    high = cas.astype(jnp.bfloat16)
    low = (cas - high.astype(np.float64)).astype(jnp.bfloat16)
    waves = (2.0 * np.sin(np.pi * count / SIZE)) ** 2
    excess = waves[:, None] + waves[None, :] + SHIFT_SCALE / float(PLANES * PLANES)
    root = np.sqrt(excess * (excess + 4.0))
    ratio = 2.0 / (2.0 + excess + root)
    weight = -1.0 / (root * SIZE * SIZE)
    return high, low, ratio.astype(np.float32), weight.astype(np.float32)


def split(x):
    high = x.astype(BF16)
    return high, (x - high.astype(F32)).astype(BF16)


def mm(a, b):
    return jnp.dot(a, b, preferred_element_type=F32)


def mm3(ah, al, bh, bl):
    return mm(ah, bh) + (mm(ah, bl) + mm(al, bh))


def up(x, axis):
    return pltpu.roll(x, x.shape[axis] - 1, axis)


def down(x, axis):
    return pltpu.roll(x, 1, axis)


def window7(x, axis):
    size = x.shape[axis]
    three = x + pltpu.roll(x, 1, axis) + pltpu.roll(x, size - 1, axis)
    return x + pltpu.roll(three, 2, axis) + pltpu.roll(three, size - 2, axis)


def bend(da, db, haa, hbb, dab):
    qa = 0.25 * da * da
    qb = 0.25 * db * db
    root = lax.rsqrt(1.0 + qa + qb)
    upper = haa * (1.0 + qb) + hbb * (1.0 + qa) - 0.125 * (da * db * dab)
    return upper * (root * root * root)


def kernel(
    frac_in, dir_in, div_in, th_in, tl_in, ratio_in, weight_in,
    kap, inner_high, inner_low, th, tl,
    fx, dirs, divs, ratio, weight,
    axc, axd, axs, ayc, ayd, ays, shi, slo, fhi, flo, spec, part, heights,
    lus, rc, pu, ru, od, rd, sd, ab,
    in_sem, fs_sem, fr_sem, c_sem, u_sem, round_sem,
):
    me = lax.axis_index("gz")
    core = lax.rem(me, 2)
    chip = lax.div(me, 2)
    sibling = me + 1 - 2 * core
    has_below = me > 0
    has_above = me < DEVICES - 1
    cross = me - 1 + 2 * core
    has_cross = jnp.logical_and(cross >= 0, cross < DEVICES)

    digits = [lax.div(chip, 16), lax.rem(lax.div(chip, 4), 4), lax.rem(chip, 4)]
    parts = [[lax.rem(v + d, 4) * scale for d in range(4)] for v, scale in zip(digits, (16, 4, 1))]
    reach = (0, 1, 2, 1)
    offsets = [(a, b, c) for a in range(4) for b in range(4) for c in range(4) if a or b or c]
    offsets.sort(key=lambda o: -sum(reach[d] for d in o))

    def chips_at(places):
        return [parts[0][a] + parts[1][b] + parts[2][c] for a, b, c in places]

    others = chips_at(offsets)
    nearest = chips_at([(1, 0, 0), (3, 0, 0), (0, 1, 0), (0, 3, 0), (0, 0, 1), (0, 0, 3)])
    y_ring = chips_at([(0, 2, 0), (0, 1, 0), (0, 3, 0)])
    z_ring = chips_at([(2, 0, 0), (1, 0, 0), (3, 0, 0)])

    barrier = pltpu.get_barrier_semaphore()

    def greet(target):
        pl.semaphore_signal(barrier, inc=1, device_id=(target,), device_id_type=MESH)

    @pl.when(has_cross)
    def _():
        greet(cross)

    greet(sibling)
    for other in nearest:
        greet(2 * other + core)

    loads = [
        pltpu.make_async_copy(frac_in, fx.at[pl.ds(3, SLAB)], in_sem.at[0]),
        pltpu.make_async_copy(dir_in, dirs, in_sem.at[1]),
        pltpu.make_async_copy(div_in, divs, in_sem.at[2]),
        pltpu.make_async_copy(th_in, th, in_sem.at[3]),
        pltpu.make_async_copy(tl_in, tl, in_sem.at[4]),
        pltpu.make_async_copy(ratio_in, ratio, in_sem.at[5]),
        pltpu.make_async_copy(weight_in, weight, in_sem.at[6]),
    ]
    for load in loads:
        load.start()

    peers = 1 + len(nearest)
    pl.semaphore_wait(barrier, jnp.where(has_cross, peers + 1, peers))

    def hail(i, chips):
        for other in chips:
            pl.semaphore_signal(
                round_sem.at[i], inc=1, device_id=(2 * other + core,), device_id_type=MESH
            )

    def halo_copies(side):
        for piece in range(2 + len(PIECES)):
            j = min(piece, 2)
            first, last = (0, SIZE) if piece < 2 else PIECES[piece - 2]
            rows = pl.ds(first, last - first)
            source, target = (3 - j, 2 - j) if side == 0 else (j, 7 + j)
            yield pltpu.make_async_remote_copy(
                src_ref=frac_in.at[source, rows], dst_ref=fx.at[target, rows],
                send_sem=fs_sem.at[side, piece], recv_sem=fr_sem.at[side, piece],
                device_id=(me + 1 - 2 * side,), device_id_type=MESH,
            )

    def send_halo(side):
        for copy in halo_copies(side):
            copy.start()

    @pl.when(jnp.logical_and(core == 0, has_below))
    def _():
        send_halo(1)

    @pl.when(core == 0)
    def _():
        send_halo(0)

    @pl.when(jnp.logical_and(core == 1, has_above))
    def _():
        send_halo(0)

    @pl.when(core == 1)
    def _():
        send_halo(1)

    hail(0, nearest)
    zero_plane = jnp.zeros((SIZE, SIZE), F32)

    @pl.when(jnp.logical_not(has_below))
    def _():
        for j in range(3):
            fx[j] = zero_plane

    @pl.when(jnp.logical_not(has_above))
    def _():
        for j in range(3):
            fx[7 + j] = zero_plane

    def flat_heights(t):
        f = fx[t + 3]
        cx = window7(f, 0)
        lift, drop = up(cx, 1), down(cx, 1)
        axc[t + 1] = cx
        axd[t + 1] = lift - drop
        axs[t + 1] = lift + drop - 2.0 * cx
        cy = window7(f, 1)
        lift, drop = up(cy, 0), down(cy, 0)
        ayc[t + 1] = cy
        ayd[t + 1] = lift - drop
        ays[t + 1] = lift + drop - 2.0 * cy

    def flat_bend(t):
        along_x = dirs[t] == 1

        def pick(a, b):
            return jnp.where(along_x, a, b)

        lo = pick(axc[t], ayc[t])
        at = pick(axc[t + 1], ayc[t + 1])
        hi = pick(axc[t + 2], ayc[t + 2])
        d_lo = pick(axd[t], ayd[t])
        d_at = pick(axd[t + 1], ayd[t + 1])
        d_hi = pick(axd[t + 2], ayd[t + 2])
        s_at = pick(axs[t + 1], ays[t + 1])
        kap[t] = bend(hi - lo, d_at, hi + lo - 2.0 * at, s_at, d_hi - d_lo)

    def upright(h):
        right, left = up(h, 1), down(h, 1)
        db = right - left
        sb = right + left
        plus, minus = up(h, 0), down(h, 0)
        dab = up(db, 0) - down(db, 0)
        return bend(plus - minus, db, plus + minus - 2.0 * h, sb - 2.0 * h, dab)

    def upright_bend(t):
        h = fx[t]
        for j in range(1, 7):
            h = h + fx[t + j]
        value = upright(h)
        where = dirs[t]
        kap[t] = jnp.where(where == 0, value, jnp.where(where == 3, 0.0, kap[t]))

    def store(t, value):
        shi[t + 1], slo[t + 1] = split(value)

    def source(t, hidden):
        f = fx[t + 3]
        k = kap[t]
        face = (k + up(k, 0)) * (up(f, 0) - f)
        total = face - down(face, 0)
        face = (k + up(k, 1)) * (up(f, 1) - f)
        total = total + face - down(face, 1)

        def beside(other):
            shown = jnp.logical_and(jnp.logical_and(other >= 0, other < SLAB), other != hidden)
            return jnp.where(shown, kap[jnp.clip(other, 0, SLAB - 1)], 0.0)

        total = total + (k + beside(t + 1)) * (fx[t + 4] - f) - (k + beside(t - 1)) * (f - fx[t + 2])
        return divs[t] + (0.5 * TENSION) * total

    def beyond(t, outer):
        store(outer, (0.5 * TENSION) * kap[t] * (fx[t + 3] - fx[outer + 3]))

    def ring(ref, t, first, last):
        if first < 0:
            return jnp.concatenate([ref[t, first + SIZE : SIZE], ref[t, 0:last]], axis=0)
        if last > SIZE:
            return jnp.concatenate([ref[t, first:SIZE], ref[t, 0 : last - SIZE]], axis=0)
        return ref[t, first:last]

    def put(ref, t, first, last, value):
        if last > SIZE:
            ref[t, first:SIZE] = value[: SIZE - first]
            ref[t, 0 : last - SIZE] = value[SIZE - first :]
        else:
            ref[t, first:last] = value

    def inner_rows(x):
        return x[8 : x.shape[0] - 8]

    def first_stage(planes):
        for t in planes:
            fhi[t + 1], flo[t + 1] = split(mm3(shi[t + 1], slo[t + 1], th[...], tl[...]))

    def second_stage(planes, rows):
        for t in planes:
            spec[t + 1, rows, :] = mm3(th[rows, :], tl[rows, :], fhi[t + 1], flo[t + 1])

    near = 3 - 3 * core
    step = 2 * core - 1

    def place(d):
        return near + step * d

    near_side = 1 - core
    near_halo = 4 - 5 * core
    far_halo = 5 * core - 1

    def wait_frac(side, piece):
        first, last = (0, SIZE) if piece < 2 else PIECES[piece - 2]
        rows = pl.ds(first, last - first)
        pltpu.make_async_copy(frac_in.at[0, rows], fx.at[0, rows], fr_sem.at[side, piece]).wait()

    def wait_far(piece):
        @pl.when(has_cross)
        def _():
            wait_frac(core, piece)

    loads[0].wait()
    lax.fori_loop(0, SLAB, lambda t, c: (flat_heights(t), c)[1], 0)
    pl.semaphore_wait(round_sem.at[0], len(nearest))
    hail(1, y_ring)
    loads[1].wait()
    lax.fori_loop(1, 3, lambda t, c: (flat_bend(t), c)[1], 0)
    for piece in range(2 + len(PIECES)):
        wait_frac(near_side, piece)
    flat_heights(near_halo)
    flat_bend(near)
    upright_bend(near)
    for load in loads[2:]:
        load.wait()
    beyond(near, near_halo)
    pl.semaphore_wait(round_sem.at[1], len(y_ring))
    hail(2, z_ring)
    wait_far(0)
    flat_heights(far_halo)
    flat_bend(place(3))
    upright_bend(place(1))
    store(near, source(near, -1))
    second = place(1)
    part[1] = source(second, place(2))
    first_stage((near_halo, near))
    second_stage((near_halo, near), slice(None))
    wait_far(1)
    upright_bend(place(2))
    store(second, part[1] + (0.5 * TENSION) * kap[place(2)] * (fx[place(2) + 3] - fx[second + 3]))
    outer, third = place(3), place(2)
    late = (third, outer, far_halo)

    def prepare():
        part[0] = source(third, outer)
        summed = fx[1 + 2 * core]
        for j in range(1, 6):
            summed = summed + fx[1 + 2 * core + j]
        heights[0] = summed

    def late_piece(c):
        scale = jnp.where(has_cross, 0.5 * TENSION, 0.0)
        a, b = BENT[c]
        h = ring(heights, 0, a - 8, b + 8) + ring(fx, 9 * core, a - 8, b + 8)
        value = inner_rows(upright(h))
        where = ring(dirs, outer, a, b)
        flat = ring(kap, outer, a, b)
        put(kap, outer, a, b, jnp.where(where == 0, value, jnp.where(where == 3, 0.0, flat)))
        a, b = FED[c]
        f, k = ring(fx, outer + 3, a - 8, b + 8), ring(kap, outer, a - 8, b + 8)
        face = (k + up(k, 0)) * (up(f, 0) - f)
        total = inner_rows(face - down(face, 0))
        f, k = inner_rows(f), inner_rows(k)
        face = (k + up(k, 1)) * (up(f, 1) - f)
        total = total + face - down(face, 1)
        f_third, f_halo = ring(fx, third + 3, a, b), ring(fx, far_halo + 3, a, b)
        total = total + (ring(kap, third, a, b) + k) * (f_third - f) + k * (f_halo - f)
        fed = (
            ring(part, 0, a, b) + (0.5 * TENSION) * k * (f - f_third),
            ring(divs, outer, a, b) + (0.5 * TENSION) * total,
            scale * k * (f - f_halo),
        )
        high, low = split(mm3(*split(jnp.concatenate(fed, axis=0)), th[...], tl[...]))
        for n, t in enumerate(late):
            rows = slice(n * (b - a), (n + 1) * (b - a))
            put(fhi, t + 1, a, b, high[rows])
            put(flo, t + 1, a, b, low[rows])

    prepare()
    for c in range(len(PIECES)):
        wait_far(2 + c)
        late_piece(c)
        if c == 0:
            first_stage((second,))

    def half_rows(half):
        return pl.ds(pl.multiple_of(half * 128, 128), 128)

    def sums(half, i):
        rows = pl.ds(pl.multiple_of(half * 128 + i * ROWS, ROWS), ROWS)
        r = ratio[rows, :]
        f = [spec[t, rows, :] for t in range(SLAB + 2)]
        low, high = f[0], f[SLAB + 1]
        for t in range(1, SLAB + 1):
            low = r * low + f[t]
            high = r * high + f[SLAB + 1 - t]
        low = r * low + f[SLAB + 1]
        high = r * high + f[0]
        return low, high

    second_stage((second,) + late, half_rows(1 - core))

    def give(q):
        rows = pl.ds(64 * q, 64)
        return pltpu.make_async_remote_copy(
            src_ref=lus.at[:, rows], dst_ref=rc.at[core, :, rows], send_sem=c_sem.at[0, q], recv_sem=c_sem.at[1, q],
            device_id=(sibling,), device_id_type=MESH,
        )

    for q in range(2):
        for i in (2 * q, 2 * q + 1):
            rows = pl.ds(i * ROWS, ROWS)
            lus[0, rows, :], lus[1, rows, :] = sums(1 - core, i)
        give(q).start()

    second_stage((second,) + late, half_rows(core))
    for i in range(4):
        rows = pl.ds(i * ROWS, ROWS)
        rc[core, 0, rows, :], rc[core, 1, rows, :] = sums(core, i)

    def power4(x):
        x = x * x
        return x * x

    first_half = lax.broadcasted_iota(jnp.int32, (8, 128), 0) < 4

    def swap(x):
        return pltpu.roll(x, 4, 0)

    def cut(i, carry):
        rows = pl.ds(pl.multiple_of(i * 8, 8), 8)
        rho = power4(ratio[pl.ds(pl.multiple_of(core * 128 + i * 8, 8), 8), :])
        low = rho * rc[0, 0, rows, :] + rc[1, 0, rows, :]
        high = rc[0, 1, rows, :] + rho * rc[1, 1, rows, :]
        for lane in range(2):
            lt = low[:, 128 * lane : 128 * lane + 128]
            ut = high[:, 128 * lane : 128 * lane + 128]
            pu[i * 4 + lane * 2] = jnp.where(first_half, lt, swap(ut))
            pu[i * 4 + lane * 2 + 1] = jnp.where(first_half, swap(lt), ut)
        return carry

    for q in range(2):
        give(q).wait_recv()
        lax.fori_loop(8 * q, 8 * q + 8, cut, 0, unroll=True)

    def send_part(other, level, source_ref, target_ref):
        return pltpu.make_async_remote_copy(
            src_ref=source_ref.at[other], dst_ref=target_ref.at[chip], send_sem=u_sem.at[level, 0],
            recv_sem=u_sem.at[level, 1], device_id=(2 * other + core,), device_id_type=MESH,
        )

    def wait_parts(level, way):
        span = pl.ds(0, CHIPS - 1)
        pltpu.make_async_copy(pu.at[span], ru.at[span], u_sem.at[level, way]).wait()

    pl.semaphore_wait(round_sem.at[2], len(z_ring))
    for other in others:
        send_part(other, 0, pu, ru).start()
    ru[chip] = pu[chip]
    wait_parts(0, 1)

    tile_row = lax.div(chip, 4)
    tile_lane = lax.rem(lax.div(chip, 2), 2)
    tile_half = lax.rem(chip, 2)
    rt = ratio[
        pl.ds(pl.multiple_of(core * 128 + tile_row * 8, 8), 8),
        pl.ds(pl.multiple_of(tile_lane * 128, 128), 128),
    ]
    keep = first_half == (tile_half == 0)
    rt = jnp.where(keep, rt, swap(rt))
    r8 = power4(rt * rt)
    r64 = power4(r8 * r8)
    r513 = power4(r64 * r64) * rt
    merged = [jnp.where(first_half, ru[j], ru[CHIPS - 1 - j]) for j in range(CHIPS)]
    blocks = []
    for b in range(8):
        total = merged[8 * b]
        for j in range(1, 8):
            total = r8 * total + merged[8 * b + j]
        blocks.append(total)
    ends = blocks[0]
    for b in range(1, 8):
        ends = r64 * ends + blocks[b]
    walls = (swap(ends) - r513 * ends) / (1.0 - r513 * r513)
    starts = [-(rt * walls)]
    for b in range(7):
        starts.append(r64 * starts[b] + blocks[b])
    sweep = []
    for b in range(8):
        sweep.append(starts[b])
        for j in range(7):
            sweep.append(r8 * sweep[-1] + merged[8 * b + j])
    for j in range(CHIPS):
        od[j] = jnp.where(first_half, sweep[j], sweep[CHIPS - 1 - j])

    for other in others:
        send_part(other, 1, od, rd).start()
    rd[chip] = od[chip]
    wait_parts(1, 1)

    def spread(i, carry):
        rows = pl.ds(pl.multiple_of(i * 8, 8), 8)
        rho = power4(ratio[pl.ds(pl.multiple_of(core * 128 + i * 8, 8), 8), :])
        tiles = [rd[i * 4 + k] for k in range(4)]
        a = jnp.concatenate([jnp.where(first_half, tiles[k], swap(tiles[k + 1])) for k in (0, 2)], axis=1)
        b = jnp.concatenate([jnp.where(first_half, swap(tiles[k]), tiles[k + 1]) for k in (0, 2)], axis=1)
        a_far = rho * a + rc[0, 0, rows, :]
        b_far = rho * b + rc[1, 1, rows, :]
        even = core == 0
        ab[core, 0, rows, :] = jnp.where(even, a, a_far)
        ab[core, 1, rows, :] = jnp.where(even, b_far, b)
        sd[0, rows, :] = jnp.where(even, a_far, a)
        sd[1, rows, :] = jnp.where(even, b, b_far)
        return carry

    def hand(q):
        rows = pl.ds(64 * q, 64)
        return pltpu.make_async_remote_copy(
            src_ref=sd.at[:, rows], dst_ref=ab.at[core, :, rows], send_sem=c_sem.at[2, q], recv_sem=c_sem.at[3, q],
            device_id=(sibling,), device_id_type=MESH,
        )

    for q in range(2):
        lax.fori_loop(8 * q, 8 * q + 8, spread, 0, unroll=True)
        hand(q).start()

    def modal(half):
        def body(i, carry):
            local = pl.ds(pl.multiple_of(i * ROWS, ROWS), ROWS)
            rows = pl.ds(pl.multiple_of(half * 128 + i * ROWS, ROWS), ROWS)
            r = ratio[rows, :]
            w = weight[rows, :]
            f = [spec[t, rows, :] for t in range(SLAB + 2)]
            rising = [r * f[0] + ab[half, 0, local, :] + f[1]]
            for t in range(1, SLAB):
                rising.append(r * rising[t - 1] + f[t + 1])
            falling = ab[half, 1, local, :] + r * f[SLAB + 1]
            for t in range(SLAB - 1, -1, -1):
                shi[t, rows, :], slo[t, rows, :] = split(w * (rising[t] + falling))
                falling = r * (falling + f[t + 1])
            return carry

        lax.fori_loop(0, 4, body, 0, unroll=True)
        rows = half_rows(half)
        for t in range(SLAB):
            inner_high[t, rows, :], inner_low[t, rows, :] = split(
                mm3(shi[t, rows, :], slo[t, rows, :], th[...], tl[...])
            )

    modal(core)
    for q in range(2):
        hand(q).wait_recv()
    modal(1 - core)

    @pl.when(has_above)
    def _():
        for copy in halo_copies(0):
            copy.wait_send()

    @pl.when(has_below)
    def _():
        for copy in halo_copies(1):
            copy.wait_send()

    for q in range(2):
        give(q).wait_send()
        hand(q).wait_send()
    wait_parts(0, 0)
    wait_parts(1, 0)


def finish(kap, high, low, th, tl, kap_out, pre_out, pre, sem):
    passing = pltpu.make_async_copy(kap, kap_out, sem.at[SLAB])
    passing.start()
    stores = []
    for t in range(SLAB):
        pre[t] = mm3(th[...], tl[...], high[t], low[t])
        stores.append(pltpu.make_async_copy(pre.at[t], pre_out.at[t], sem.at[t]))
        stores[t].start()
    passing.wait()
    for copy in stores:
        copy.wait()


def shards(fraction, column_dir, divergence):
    shape = (SLAB, SIZE, SIZE)
    plane = (SIZE, SIZE)
    high, low, ratio, weight = tables()
    far = pl.BlockSpec(memory_space=pltpu.HBM)
    vm = pltpu.VMEM
    close = pl.BlockSpec(memory_space=vm)
    dma = pltpu.SemaphoreType.DMA
    whole = jax.ShapeDtypeStruct(shape, F32)
    half = jax.ShapeDtypeStruct(shape, BF16)
    table = jax.ShapeDtypeStruct(plane, BF16)
    params = dict(vmem_limit_bytes=40 * 1024 * 1024)
    six = vm((SLAB + 2,) + plane, F32)
    six_half = vm((SLAB + 2,) + plane, BF16)
    inputs = (
        fraction, column_dir, divergence, jnp.asarray(high), jnp.asarray(low), jnp.asarray(ratio), jnp.asarray(weight),
    )
    handed_on = pl.pallas_call(
        kernel,
        out_shape=(whole, half, half, table, table),
        in_specs=[far] * 7,
        out_specs=(close,) * 5,
        scratch_shapes=[
            vm((10,) + plane, F32), vm(shape, jnp.int32), vm(shape, F32),
            vm(plane, F32), vm(plane, F32),
            six, six, six, six, six, six,
            six_half, six_half, six_half, six_half, six,
            vm((2,) + plane, F32), vm((1,) + plane, F32),
            vm((2, 128, SIZE), F32), vm((2, 2, 128, SIZE), F32),
            vm((CHIPS, 8, 128), F32), vm((CHIPS, 8, 128), F32),
            vm((CHIPS, 8, 128), F32), vm((CHIPS, 8, 128), F32),
            vm((2, 128, SIZE), F32), vm((2, 2, 128, SIZE), F32),
            dma((7,)), dma((2, 5)), dma((2, 5)), dma((4, 2)), dma((2, 2)), pltpu.SemaphoreType.REGULAR((3,)),
        ],
        compiler_params=pltpu.CompilerParams(collective_id=0, has_side_effects=True, **params),
    )(*(pltpu.with_memory_space_constraint(value, pltpu.HBM) for value in inputs))
    return pl.pallas_call(
        finish,
        out_shape=(whole, whole),
        in_specs=[close] * 5,
        out_specs=(far,) * 2,
        scratch_shapes=[
            vm(shape, F32), dma((SLAB + 1,)),
        ],
        compiler_params=pltpu.CompilerParams(**params),
    )(*handed_on)


def solution(mesh):
    spec = P("gz", None, None)
    return jax.shard_map(
        shards, mesh=mesh, in_specs=(spec, spec, spec), out_specs=(spec, spec), check_vma=False
    )
```

```python
import jax
import jax.numpy as jnp
import numpy as np
from jax import lax
from jax.experimental import pallas as pl
from jax.experimental.pallas import tpu as pltpu
from jax.sharding import PartitionSpec as P

TENSION = 0.2
SHIFT_SCALE = 16.0
SIZE = 256
PLANES = 512
SLAB = 4
DEVICES = 128
CHIPS = 64
ROWS = 32
PIECES = ((0, 96), (96, 192), (192, 256))
BENT = ((8, 88), (88, 184), (184, 264))
FED = ((16, 80), (80, 176), (176, 272))
MESH = pl.DeviceIdType.MESH
F32 = jnp.float32
BF16 = jnp.bfloat16


def tables():
    count = np.arange(SIZE)
    angle = 2.0 * np.pi / SIZE * ((count[:, None] * count[None, :]) % SIZE)
    cas = np.cos(angle) + np.sin(angle)
    high = cas.astype(jnp.bfloat16)
    low = (cas - high.astype(np.float64)).astype(jnp.bfloat16)
    waves = (2.0 * np.sin(np.pi * count / SIZE)) ** 2
    excess = waves[:, None] + waves[None, :] + SHIFT_SCALE / float(PLANES * PLANES)
    root = np.sqrt(excess * (excess + 4.0))
    ratio = 2.0 / (2.0 + excess + root)
    weight = -1.0 / (root * SIZE * SIZE)
    return high, low, ratio.astype(np.float32), weight.astype(np.float32)


def split(x):
    high = x.astype(BF16)
    return high, (x - high.astype(F32)).astype(BF16)


def mm(a, b):
    return jnp.dot(a, b, preferred_element_type=F32)


def mm3(ah, al, bh, bl):
    return mm(ah, bh) + (mm(ah, bl) + mm(al, bh))


def up(x, axis):
    return pltpu.roll(x, x.shape[axis] - 1, axis)


def down(x, axis):
    return pltpu.roll(x, 1, axis)


def window7(x, axis):
    size = x.shape[axis]
    three = x + pltpu.roll(x, 1, axis) + pltpu.roll(x, size - 1, axis)
    return x + pltpu.roll(three, 2, axis) + pltpu.roll(three, size - 2, axis)


def bend(da, db, haa, hbb, dab):
    qa = 0.25 * da * da
    qb = 0.25 * db * db
    root = lax.rsqrt(1.0 + qa + qb)
    upper = haa * (1.0 + qb) + hbb * (1.0 + qa) - 0.125 * (da * db * dab)
    return upper * (root * root * root)


def kernel(
    frac_in, dir_in, div_in, th_in, tl_in, ratio_in, weight_in,
    kap, inner_high, inner_low, th, tl,
    fx, dirs, divs, ratio, weight,
    axc, axd, axs, ayc, ayd, ays, shi, slo, fhi, flo, spec, part, heights,
    lus, rc, pu, ru, od, rd, sd, ab,
    in_sem, fs_sem, fr_sem, c_sem, u_sem, round_sem,
):
    me = lax.axis_index("gz")
    core = lax.rem(me, 2)
    chip = lax.div(me, 2)
    sibling = me + 1 - 2 * core
    has_below = me > 0
    has_above = me < DEVICES - 1
    cross = me - 1 + 2 * core
    has_cross = jnp.logical_and(cross >= 0, cross < DEVICES)

    digits = [lax.div(chip, 16), lax.rem(lax.div(chip, 4), 4), lax.rem(chip, 4)]
    parts = [[lax.rem(v + d, 4) * scale for d in range(4)] for v, scale in zip(digits, (16, 4, 1))]
    reach = (0, 1, 2, 1)
    offsets = [(a, b, c) for a in range(4) for b in range(4) for c in range(4) if a or b or c]
    offsets.sort(key=lambda o: -sum(reach[d] for d in o))

    def chips_at(places):
        return [parts[0][a] + parts[1][b] + parts[2][c] for a, b, c in places]

    others = chips_at(offsets)
    nearest = chips_at([(1, 0, 0), (3, 0, 0), (0, 1, 0), (0, 3, 0), (0, 0, 1), (0, 0, 3)])
    y_ring = chips_at([(0, 2, 0), (0, 1, 0), (0, 3, 0)])
    z_ring = chips_at([(2, 0, 0), (1, 0, 0), (3, 0, 0)])

    barrier = pltpu.get_barrier_semaphore()

    def greet(target):
        pl.semaphore_signal(barrier, inc=1, device_id=(target,), device_id_type=MESH)

    @pl.when(has_cross)
    def _():
        greet(cross)

    greet(sibling)
    for other in nearest:
        greet(2 * other + core)

    loads = [
        pltpu.make_async_copy(frac_in, fx.at[pl.ds(3, SLAB)], in_sem.at[0]),
        pltpu.make_async_copy(dir_in, dirs, in_sem.at[1]),
        pltpu.make_async_copy(div_in, divs, in_sem.at[2]),
        pltpu.make_async_copy(th_in, th, in_sem.at[3]),
        pltpu.make_async_copy(tl_in, tl, in_sem.at[4]),
        pltpu.make_async_copy(ratio_in, ratio, in_sem.at[5]),
        pltpu.make_async_copy(weight_in, weight, in_sem.at[6]),
    ]
    for load in loads:
        load.start()

    peers = 1 + len(nearest)
    pl.semaphore_wait(barrier, jnp.where(has_cross, peers + 1, peers))

    def hail(i, chips):
        for other in chips:
            pl.semaphore_signal(
                round_sem.at[i], inc=1, device_id=(2 * other + core,), device_id_type=MESH
            )

    def halo_copies(side):
        for piece in range(2 + len(PIECES)):
            j = min(piece, 2)
            first, last = (0, SIZE) if piece < 2 else PIECES[piece - 2]
            rows = pl.ds(first, last - first)
            source, target = (3 - j, 2 - j) if side == 0 else (j, 7 + j)
            yield pltpu.make_async_remote_copy(
                src_ref=frac_in.at[source, rows], dst_ref=fx.at[target, rows],
                send_sem=fs_sem.at[side, piece], recv_sem=fr_sem.at[side, piece],
                device_id=(me + 1 - 2 * side,), device_id_type=MESH,
            )

    def send_halo(side):
        for copy in halo_copies(side):
            copy.start()

    @pl.when(jnp.logical_and(core == 0, has_below))
    def _():
        send_halo(1)

    @pl.when(core == 0)
    def _():
        send_halo(0)

    @pl.when(jnp.logical_and(core == 1, has_above))
    def _():
        send_halo(0)

    @pl.when(core == 1)
    def _():
        send_halo(1)

    hail(0, nearest)
    zero_plane = jnp.zeros((SIZE, SIZE), F32)

    @pl.when(jnp.logical_not(has_below))
    def _():
        for j in range(3):
            fx[j] = zero_plane

    @pl.when(jnp.logical_not(has_above))
    def _():
        for j in range(3):
            fx[7 + j] = zero_plane

    def flat_heights(t):
        f = fx[t + 3]
        cx = window7(f, 0)
        lift, drop = up(cx, 1), down(cx, 1)
        axc[t + 1] = cx
        axd[t + 1] = lift - drop
        axs[t + 1] = lift + drop - 2.0 * cx
        cy = window7(f, 1)
        lift, drop = up(cy, 0), down(cy, 0)
        ayc[t + 1] = cy
        ayd[t + 1] = lift - drop
        ays[t + 1] = lift + drop - 2.0 * cy

    def flat_bend(t):
        along_x = dirs[t] == 1

        def pick(a, b):
            return jnp.where(along_x, a, b)

        lo = pick(axc[t], ayc[t])
        at = pick(axc[t + 1], ayc[t + 1])
        hi = pick(axc[t + 2], ayc[t + 2])
        d_lo = pick(axd[t], ayd[t])
        d_at = pick(axd[t + 1], ayd[t + 1])
        d_hi = pick(axd[t + 2], ayd[t + 2])
        s_at = pick(axs[t + 1], ays[t + 1])
        kap[t] = bend(hi - lo, d_at, hi + lo - 2.0 * at, s_at, d_hi - d_lo)

    def upright(h):
        right, left = up(h, 1), down(h, 1)
        db = right - left
        sb = right + left
        plus, minus = up(h, 0), down(h, 0)
        dab = up(db, 0) - down(db, 0)
        return bend(plus - minus, db, plus + minus - 2.0 * h, sb - 2.0 * h, dab)

    def upright_bend(t):
        h = fx[t]
        for j in range(1, 7):
            h = h + fx[t + j]
        value = upright(h)
        where = dirs[t]
        kap[t] = jnp.where(where == 0, value, jnp.where(where == 3, 0.0, kap[t]))

    def store(t, value):
        shi[t + 1], slo[t + 1] = split(value)

    def source(t, hidden):
        f = fx[t + 3]
        k = kap[t]
        face = (k + up(k, 0)) * (up(f, 0) - f)
        total = face - down(face, 0)
        face = (k + up(k, 1)) * (up(f, 1) - f)
        total = total + face - down(face, 1)

        def beside(other):
            shown = jnp.logical_and(jnp.logical_and(other >= 0, other < SLAB), other != hidden)
            return jnp.where(shown, kap[jnp.clip(other, 0, SLAB - 1)], 0.0)

        total = total + (k + beside(t + 1)) * (fx[t + 4] - f) - (k + beside(t - 1)) * (f - fx[t + 2])
        return divs[t] + (0.5 * TENSION) * total

    def beyond(t, outer):
        store(outer, (0.5 * TENSION) * kap[t] * (fx[t + 3] - fx[outer + 3]))

    def ring(ref, t, first, last):
        if first < 0:
            return jnp.concatenate([ref[t, first + SIZE : SIZE], ref[t, 0:last]], axis=0)
        if last > SIZE:
            return jnp.concatenate([ref[t, first:SIZE], ref[t, 0 : last - SIZE]], axis=0)
        return ref[t, first:last]

    def put(ref, t, first, last, value):
        if last > SIZE:
            ref[t, first:SIZE] = value[: SIZE - first]
            ref[t, 0 : last - SIZE] = value[SIZE - first :]
        else:
            ref[t, first:last] = value

    def inner_rows(x):
        return x[8 : x.shape[0] - 8]

    def first_stage(planes):
        for t in planes:
            fhi[t + 1], flo[t + 1] = split(mm3(shi[t + 1], slo[t + 1], th[...], tl[...]))

    def second_stage(planes, rows):
        for t in planes:
            spec[t + 1, rows, :] = mm3(th[rows, :], tl[rows, :], fhi[t + 1], flo[t + 1])

    near = 3 - 3 * core
    step = 2 * core - 1

    def place(d):
        return near + step * d

    near_side = 1 - core
    near_halo = 4 - 5 * core
    far_halo = 5 * core - 1

    def wait_frac(side, piece):
        first, last = (0, SIZE) if piece < 2 else PIECES[piece - 2]
        rows = pl.ds(first, last - first)
        pltpu.make_async_copy(frac_in.at[0, rows], fx.at[0, rows], fr_sem.at[side, piece]).wait()

    def wait_far(piece):
        @pl.when(has_cross)
        def _():
            wait_frac(core, piece)

    loads[0].wait()
    lax.fori_loop(0, SLAB, lambda t, c: (flat_heights(t), c)[1], 0)
    pl.semaphore_wait(round_sem.at[0], len(nearest))
    hail(1, y_ring)
    loads[1].wait()
    lax.fori_loop(1, 3, lambda t, c: (flat_bend(t), c)[1], 0)
    for piece in range(2 + len(PIECES)):
        wait_frac(near_side, piece)
    flat_heights(near_halo)
    flat_bend(near)
    upright_bend(near)
    for load in loads[2:]:
        load.wait()
    beyond(near, near_halo)
    pl.semaphore_wait(round_sem.at[1], len(y_ring))
    hail(2, z_ring)
    wait_far(0)
    flat_heights(far_halo)
    flat_bend(place(3))
    upright_bend(place(1))
    store(near, source(near, -1))
    second = place(1)
    part[1] = source(second, place(2))
    first_stage((near_halo, near))
    second_stage((near_halo, near), slice(None))
    wait_far(1)
    upright_bend(place(2))
    store(second, part[1] + (0.5 * TENSION) * kap[place(2)] * (fx[place(2) + 3] - fx[second + 3]))
    outer, third = place(3), place(2)
    late = (third, outer, far_halo)

    def prepare():
        part[0] = source(third, outer)
        summed = fx[1 + 2 * core]
        for j in range(1, 6):
            summed = summed + fx[1 + 2 * core + j]
        heights[0] = summed

    def late_piece(c):
        scale = jnp.where(has_cross, 0.5 * TENSION, 0.0)
        a, b = BENT[c]
        h = ring(heights, 0, a - 8, b + 8) + ring(fx, 9 * core, a - 8, b + 8)
        value = inner_rows(upright(h))
        where = ring(dirs, outer, a, b)
        flat = ring(kap, outer, a, b)
        put(kap, outer, a, b, jnp.where(where == 0, value, jnp.where(where == 3, 0.0, flat)))
        a, b = FED[c]
        f, k = ring(fx, outer + 3, a - 8, b + 8), ring(kap, outer, a - 8, b + 8)
        face = (k + up(k, 0)) * (up(f, 0) - f)
        total = inner_rows(face - down(face, 0))
        f, k = inner_rows(f), inner_rows(k)
        face = (k + up(k, 1)) * (up(f, 1) - f)
        total = total + face - down(face, 1)
        f_third, f_halo = ring(fx, third + 3, a, b), ring(fx, far_halo + 3, a, b)
        total = total + (ring(kap, third, a, b) + k) * (f_third - f) + k * (f_halo - f)
        fed = (
            ring(part, 0, a, b) + (0.5 * TENSION) * k * (f - f_third),
            ring(divs, outer, a, b) + (0.5 * TENSION) * total,
            scale * k * (f - f_halo),
        )
        high, low = split(mm3(*split(jnp.concatenate(fed, axis=0)), th[...], tl[...]))
        for n, t in enumerate(late):
            rows = slice(n * (b - a), (n + 1) * (b - a))
            put(fhi, t + 1, a, b, high[rows])
            put(flo, t + 1, a, b, low[rows])

    prepare()
    for c in range(len(PIECES)):
        wait_far(2 + c)
        late_piece(c)
        if c == 0:
            first_stage((second,))
        if c == 1:
            second_stage((second,), slice(None))

    def half_rows(half):
        return pl.ds(pl.multiple_of(half * 128, 128), 128)

    def sums(half, i):
        rows = pl.ds(pl.multiple_of(half * 128 + i * ROWS, ROWS), ROWS)
        r = ratio[rows, :]
        f = [spec[t, rows, :] for t in range(SLAB + 2)]
        low, high = f[0], f[SLAB + 1]
        for t in range(1, SLAB + 1):
            low = r * low + f[t]
            high = r * high + f[SLAB + 1 - t]
        low = r * low + f[SLAB + 1]
        high = r * high + f[0]
        return low, high

    second_stage(late, half_rows(1 - core))

    def give(q):
        rows = pl.ds(64 * q, 64)
        return pltpu.make_async_remote_copy(
            src_ref=lus.at[:, rows], dst_ref=rc.at[core, :, rows], send_sem=c_sem.at[0, q], recv_sem=c_sem.at[1, q],
            device_id=(sibling,), device_id_type=MESH,
        )

    for q in range(2):
        for i in (2 * q, 2 * q + 1):
            rows = pl.ds(i * ROWS, ROWS)
            lus[0, rows, :], lus[1, rows, :] = sums(1 - core, i)
        give(q).start()

    second_stage(late, half_rows(core))
    for i in range(4):
        rows = pl.ds(i * ROWS, ROWS)
        rc[core, 0, rows, :], rc[core, 1, rows, :] = sums(core, i)

    def power4(x):
        x = x * x
        return x * x

    first_half = lax.broadcasted_iota(jnp.int32, (8, 128), 0) < 4

    def swap(x):
        return pltpu.roll(x, 4, 0)

    def cut(i, carry):
        rows = pl.ds(pl.multiple_of(i * 8, 8), 8)
        rho = power4(ratio[pl.ds(pl.multiple_of(core * 128 + i * 8, 8), 8), :])
        low = rho * rc[0, 0, rows, :] + rc[1, 0, rows, :]
        high = rc[0, 1, rows, :] + rho * rc[1, 1, rows, :]
        for lane in range(2):
            lt = low[:, 128 * lane : 128 * lane + 128]
            ut = high[:, 128 * lane : 128 * lane + 128]
            pu[i * 4 + lane * 2] = jnp.where(first_half, lt, swap(ut))
            pu[i * 4 + lane * 2 + 1] = jnp.where(first_half, swap(lt), ut)
        return carry

    for q in range(2):
        give(q).wait_recv()
        lax.fori_loop(8 * q, 8 * q + 8, cut, 0, unroll=True)

    def send_part(other, level, source_ref, target_ref):
        return pltpu.make_async_remote_copy(
            src_ref=source_ref.at[other], dst_ref=target_ref.at[chip], send_sem=u_sem.at[level, 0],
            recv_sem=u_sem.at[level, 1], device_id=(2 * other + core,), device_id_type=MESH,
        )

    def wait_parts(level, way):
        span = pl.ds(0, CHIPS - 1)
        pltpu.make_async_copy(pu.at[span], ru.at[span], u_sem.at[level, way]).wait()

    pl.semaphore_wait(round_sem.at[2], len(z_ring))
    for other in others:
        send_part(other, 0, pu, ru).start()
    ru[chip] = pu[chip]
    tile_row = lax.div(chip, 4)
    tile_lane = lax.rem(lax.div(chip, 2), 2)
    tile_half = lax.rem(chip, 2)
    rt = ratio[
        pl.ds(pl.multiple_of(core * 128 + tile_row * 8, 8), 8),
        pl.ds(pl.multiple_of(tile_lane * 128, 128), 128),
    ]
    keep = first_half == (tile_half == 0)
    rt = jnp.where(keep, rt, swap(rt))
    r8 = power4(rt * rt)
    r64 = power4(r8 * r8)
    r513 = power4(r64 * r64) * rt
    settle = 1.0 / (1.0 - r513 * r513)
    wait_parts(0, 1)

    merged = [jnp.where(first_half, ru[j], ru[CHIPS - 1 - j]) for j in range(CHIPS)]
    blocks = []
    for b in range(8):
        total = merged[8 * b]
        for j in range(1, 8):
            total = r8 * total + merged[8 * b + j]
        blocks.append(total)
    ends = blocks[0]
    for b in range(1, 8):
        ends = r64 * ends + blocks[b]
    walls = (swap(ends) - r513 * ends) * settle
    starts = [-(rt * walls)]
    for b in range(7):
        starts.append(r64 * starts[b] + blocks[b])
    sweep = []
    for b in range(8):
        sweep.append(starts[b])
        for j in range(7):
            sweep.append(r8 * sweep[-1] + merged[8 * b + j])
    for j in range(CHIPS):
        od[j] = jnp.where(first_half, sweep[j], sweep[CHIPS - 1 - j])

    for other in others:
        send_part(other, 1, od, rd).start()
    rd[chip] = od[chip]
    wait_parts(1, 1)

    def spread(i, carry):
        rows = pl.ds(pl.multiple_of(i * 8, 8), 8)
        rho = power4(ratio[pl.ds(pl.multiple_of(core * 128 + i * 8, 8), 8), :])
        tiles = [rd[i * 4 + k] for k in range(4)]
        a = jnp.concatenate([jnp.where(first_half, tiles[k], swap(tiles[k + 1])) for k in (0, 2)], axis=1)
        b = jnp.concatenate([jnp.where(first_half, swap(tiles[k]), tiles[k + 1]) for k in (0, 2)], axis=1)
        a_far = rho * a + rc[0, 0, rows, :]
        b_far = rho * b + rc[1, 1, rows, :]
        even = core == 0
        ab[core, 0, rows, :] = jnp.where(even, a, a_far)
        ab[core, 1, rows, :] = jnp.where(even, b_far, b)
        sd[0, rows, :] = jnp.where(even, a_far, a)
        sd[1, rows, :] = jnp.where(even, b, b_far)
        return carry

    def hand(q):
        rows = pl.ds(64 * q, 64)
        return pltpu.make_async_remote_copy(
            src_ref=sd.at[:, rows], dst_ref=ab.at[core, :, rows], send_sem=c_sem.at[2, q], recv_sem=c_sem.at[3, q],
            device_id=(sibling,), device_id_type=MESH,
        )

    for q in range(2):
        lax.fori_loop(8 * q, 8 * q + 8, spread, 0, unroll=True)
        hand(q).start()

    def modal(half, q):
        local = pl.ds(64 * q, 64)
        rows = pl.ds(pl.multiple_of(half * 128 + 64 * q, 64), 64)
        r = ratio[rows, :]
        w = weight[rows, :]
        f = [spec[t, rows, :] for t in range(SLAB + 2)]
        rising = [r * f[0] + ab[half, 0, local, :] + f[1]]
        for t in range(1, SLAB):
            rising.append(r * rising[t - 1] + f[t + 1])
        falling = ab[half, 1, local, :] + r * f[SLAB + 1]
        values = [None] * SLAB
        for t in range(SLAB - 1, -1, -1):
            values[t] = w * (rising[t] + falling)
            falling = r * (falling + f[t + 1])
        high, low = split(mm3(*split(jnp.concatenate(values, axis=0)), th[...], tl[...]))
        for t in range(SLAB):
            inner_high[t, rows, :] = high[64 * t : 64 * t + 64]
            inner_low[t, rows, :] = low[64 * t : 64 * t + 64]

    for q in range(2):
        modal(core, q)
    for q in range(2):
        hand(q).wait_recv()
        modal(1 - core, q)

    @pl.when(has_above)
    def _():
        for copy in halo_copies(0):
            copy.wait_send()

    @pl.when(has_below)
    def _():
        for copy in halo_copies(1):
            copy.wait_send()

    for q in range(2):
        give(q).wait_send()
        hand(q).wait_send()
    wait_parts(0, 0)
    wait_parts(1, 0)


def finish(kap, high, low, th, tl, kap_out, pre_out, pre, sem):
    passing = pltpu.make_async_copy(kap, kap_out, sem.at[SLAB])
    passing.start()
    stores = []
    for t in range(SLAB):
        pre[t] = mm3(th[...], tl[...], high[t], low[t])
        stores.append(pltpu.make_async_copy(pre.at[t], pre_out.at[t], sem.at[t]))
        stores[t].start()
    passing.wait()
    for copy in stores:
        copy.wait()


def shards(fraction, column_dir, divergence):
    shape = (SLAB, SIZE, SIZE)
    plane = (SIZE, SIZE)
    high, low, ratio, weight = tables()
    far = pl.BlockSpec(memory_space=pltpu.HBM)
    vm = pltpu.VMEM
    close = pl.BlockSpec(memory_space=vm)
    dma = pltpu.SemaphoreType.DMA
    whole = jax.ShapeDtypeStruct(shape, F32)
    half = jax.ShapeDtypeStruct(shape, BF16)
    table = jax.ShapeDtypeStruct(plane, BF16)
    params = dict(vmem_limit_bytes=40 * 1024 * 1024)
    six = vm((SLAB + 2,) + plane, F32)
    six_half = vm((SLAB + 2,) + plane, BF16)
    inputs = (
        fraction, column_dir, divergence, jnp.asarray(high), jnp.asarray(low), jnp.asarray(ratio), jnp.asarray(weight),
    )
    handed_on = pl.pallas_call(
        kernel,
        out_shape=(whole, half, half, table, table),
        in_specs=[far] * 7,
        out_specs=(close,) * 5,
        scratch_shapes=[
            vm((10,) + plane, F32), vm(shape, jnp.int32), vm(shape, F32),
            vm(plane, F32), vm(plane, F32),
            six, six, six, six, six, six,
            six_half, six_half, six_half, six_half, six,
            vm((2,) + plane, F32), vm((1,) + plane, F32),
            vm((2, 128, SIZE), F32), vm((2, 2, 128, SIZE), F32),
            vm((CHIPS, 8, 128), F32), vm((CHIPS, 8, 128), F32),
            vm((CHIPS, 8, 128), F32), vm((CHIPS, 8, 128), F32),
            vm((2, 128, SIZE), F32), vm((2, 2, 128, SIZE), F32),
            dma((7,)), dma((2, 5)), dma((2, 5)), dma((4, 2)), dma((2, 2)), pltpu.SemaphoreType.REGULAR((3,)),
        ],
        compiler_params=pltpu.CompilerParams(collective_id=0, has_side_effects=True, **params),
    )(*(pltpu.with_memory_space_constraint(value, pltpu.HBM) for value in inputs))
    return pl.pallas_call(
        finish,
        out_shape=(whole, whole),
        in_specs=[close] * 5,
        out_specs=(far,) * 2,
        scratch_shapes=[
            vm(shape, F32), dma((SLAB + 1,)),
        ],
        compiler_params=pltpu.CompilerParams(**params),
    )(*handed_on)


def solution(mesh):
    spec = P("gz", None, None)
    return jax.shard_map(
        shards, mesh=mesh, in_specs=(spec, spec, spec), out_specs=(spec, spec), check_vma=False
    )
```

```python
import jax
import jax.numpy as jnp
import numpy as np
from jax import lax
from jax.experimental import pallas as pl
from jax.experimental.pallas import tpu as pltpu
from jax.sharding import PartitionSpec as P

TENSION = 0.2
SHIFT_SCALE = 16.0
SIZE = 256
PLANES = 512
SLAB = 4
DEVICES = 128
CHIPS = 64
ROWS = 32
PIECES = ((0, 96), (96, 192), (192, 256))
BENT = ((8, 88), (88, 184), (184, 264))
FED = ((16, 80), (80, 176), (176, 272))
MESH = pl.DeviceIdType.MESH
F32 = jnp.float32
BF16 = jnp.bfloat16


def tables():
    count = np.arange(SIZE)
    angle = 2.0 * np.pi / SIZE * ((count[:, None] * count[None, :]) % SIZE)
    cas = np.cos(angle) + np.sin(angle)
    high = cas.astype(jnp.bfloat16)
    low = (cas - high.astype(np.float64)).astype(jnp.bfloat16)
    waves = (2.0 * np.sin(np.pi * count / SIZE)) ** 2
    excess = waves[:, None] + waves[None, :] + SHIFT_SCALE / float(PLANES * PLANES)
    root = np.sqrt(excess * (excess + 4.0))
    ratio = 2.0 / (2.0 + excess + root)
    weight = -1.0 / (root * SIZE * SIZE)
    return high, low, ratio.astype(np.float32), weight.astype(np.float32)


def split(x):
    high = x.astype(BF16)
    return high, (x - high.astype(F32)).astype(BF16)


def mm(a, b):
    return jnp.dot(a, b, preferred_element_type=F32)


def mm3(ah, al, bh, bl):
    return mm(ah, bh) + (mm(ah, bl) + mm(al, bh))


def up(x, axis):
    return pltpu.roll(x, x.shape[axis] - 1, axis)


def down(x, axis):
    return pltpu.roll(x, 1, axis)


def window7(x, axis):
    size = x.shape[axis]
    three = x + pltpu.roll(x, 1, axis) + pltpu.roll(x, size - 1, axis)
    return x + pltpu.roll(three, 2, axis) + pltpu.roll(three, size - 2, axis)


def bend(da, db, haa, hbb, dab):
    qa = 0.25 * da * da
    qb = 0.25 * db * db
    root = lax.rsqrt(1.0 + qa + qb)
    upper = haa * (1.0 + qb) + hbb * (1.0 + qa) - 0.125 * (da * db * dab)
    return upper * (root * root * root)


def kernel(
    frac_in, dir_in, div_in, th_in, tl_in, ratio_in, weight_in,
    kap, inner_high, inner_low, th, tl,
    fx, dirs, divs, ratio, weight,
    axc, axd, axs, ayc, ayd, ays, shi, slo, fhi, flo, spec, part, heights,
    lus, rc, rz, pu, ru, od, rd, sd, ab,
    in_sem, fs_sem, fr_sem, c_sem, z_sem, u_sem, h_sem, round_sem,
):
    me = lax.axis_index("gz")
    core = lax.rem(me, 2)
    chip = lax.div(me, 2)
    sibling = me + 1 - 2 * core
    has_below = me > 0
    has_above = me < DEVICES - 1
    cross = me - 1 + 2 * core
    has_cross = jnp.logical_and(cross >= 0, cross < DEVICES)

    digits = [lax.div(chip, 16), lax.rem(lax.div(chip, 4), 4), lax.rem(chip, 4)]
    parts = [[lax.rem(v + d, 4) * scale for d in range(4)] for v, scale in zip(digits, (16, 4, 1))]
    reach = (0, 1, 2, 1)
    offsets = [(a, b, c) for a in range(4) for b in range(4) for c in range(4) if a or b or c]
    offsets.sort(key=lambda o: -sum(reach[d] for d in o))

    def chips_at(places):
        return [parts[0][a] + parts[1][b] + parts[2][c] for a, b, c in places]

    others = chips_at(offsets)
    nearest = chips_at([(1, 0, 0), (3, 0, 0), (0, 1, 0), (0, 3, 0), (0, 0, 1), (0, 0, 3)])
    y_ring = chips_at([(0, 2, 0), (0, 1, 0), (0, 3, 0)])
    z_ring = chips_at([(2, 0, 0), (1, 0, 0), (3, 0, 0)])
    x_near = chips_at([(0, 0, 1), (0, 0, 3)])

    barrier = pltpu.get_barrier_semaphore()

    def greet(target):
        pl.semaphore_signal(barrier, inc=1, device_id=(target,), device_id_type=MESH)

    @pl.when(has_cross)
    def _():
        greet(cross)

    greet(sibling)
    for other in nearest:
        greet(2 * other + core)

    loads = [
        pltpu.make_async_copy(frac_in, fx.at[pl.ds(3, SLAB)], in_sem.at[0]),
        pltpu.make_async_copy(dir_in, dirs, in_sem.at[1]),
        pltpu.make_async_copy(div_in, divs, in_sem.at[2]),
        pltpu.make_async_copy(th_in, th, in_sem.at[3]),
        pltpu.make_async_copy(tl_in, tl, in_sem.at[4]),
        pltpu.make_async_copy(ratio_in, ratio, in_sem.at[5]),
        pltpu.make_async_copy(weight_in, weight, in_sem.at[6]),
    ]
    for load in loads:
        load.start()

    peers = 1 + len(nearest)
    pl.semaphore_wait(barrier, jnp.where(has_cross, peers + 1, peers))

    def hail(i, chips):
        for other in chips:
            pl.semaphore_signal(
                round_sem.at[i], inc=1, device_id=(2 * other + core,), device_id_type=MESH
            )

    def halo_copies(side):
        for piece in range(2 + len(PIECES)):
            j = min(piece, 2)
            first, last = (0, SIZE) if piece < 2 else PIECES[piece - 2]
            rows = pl.ds(first, last - first)
            source, target = (3 - j, 2 - j) if side == 0 else (j, 7 + j)
            yield pltpu.make_async_remote_copy(
                src_ref=frac_in.at[source, rows], dst_ref=fx.at[target, rows],
                send_sem=fs_sem.at[side, piece], recv_sem=fr_sem.at[side, piece],
                device_id=(me + 1 - 2 * side,), device_id_type=MESH,
            )

    def send_halo(side):
        for copy in halo_copies(side):
            copy.start()

    @pl.when(jnp.logical_and(core == 0, has_below))
    def _():
        send_halo(1)

    @pl.when(core == 0)
    def _():
        send_halo(0)

    @pl.when(jnp.logical_and(core == 1, has_above))
    def _():
        send_halo(0)

    @pl.when(core == 1)
    def _():
        send_halo(1)

    hail(0, nearest)
    zero_plane = jnp.zeros((SIZE, SIZE), F32)

    @pl.when(jnp.logical_not(has_below))
    def _():
        for j in range(3):
            fx[j] = zero_plane

    @pl.when(jnp.logical_not(has_above))
    def _():
        for j in range(3):
            fx[7 + j] = zero_plane

    def flat_heights(t):
        f = fx[t + 3]
        cx = window7(f, 0)
        lift, drop = up(cx, 1), down(cx, 1)
        axc[t + 1] = cx
        axd[t + 1] = lift - drop
        axs[t + 1] = lift + drop - 2.0 * cx
        cy = window7(f, 1)
        lift, drop = up(cy, 0), down(cy, 0)
        ayc[t + 1] = cy
        ayd[t + 1] = lift - drop
        ays[t + 1] = lift + drop - 2.0 * cy

    def flat_bend(t):
        along_x = dirs[t] == 1

        def pick(a, b):
            return jnp.where(along_x, a, b)

        lo = pick(axc[t], ayc[t])
        at = pick(axc[t + 1], ayc[t + 1])
        hi = pick(axc[t + 2], ayc[t + 2])
        d_lo = pick(axd[t], ayd[t])
        d_at = pick(axd[t + 1], ayd[t + 1])
        d_hi = pick(axd[t + 2], ayd[t + 2])
        s_at = pick(axs[t + 1], ays[t + 1])
        kap[t] = bend(hi - lo, d_at, hi + lo - 2.0 * at, s_at, d_hi - d_lo)

    def upright(h):
        right, left = up(h, 1), down(h, 1)
        db = right - left
        sb = right + left
        plus, minus = up(h, 0), down(h, 0)
        dab = up(db, 0) - down(db, 0)
        return bend(plus - minus, db, plus + minus - 2.0 * h, sb - 2.0 * h, dab)

    def upright_bend(t):
        h = fx[t]
        for j in range(1, 7):
            h = h + fx[t + j]
        value = upright(h)
        where = dirs[t]
        kap[t] = jnp.where(where == 0, value, jnp.where(where == 3, 0.0, kap[t]))

    def store(t, value):
        shi[t + 1], slo[t + 1] = split(value)

    def source(t, hidden):
        f = fx[t + 3]
        k = kap[t]
        face = (k + up(k, 0)) * (up(f, 0) - f)
        total = face - down(face, 0)
        face = (k + up(k, 1)) * (up(f, 1) - f)
        total = total + face - down(face, 1)

        def beside(other):
            shown = jnp.logical_and(jnp.logical_and(other >= 0, other < SLAB), other != hidden)
            return jnp.where(shown, kap[jnp.clip(other, 0, SLAB - 1)], 0.0)

        total = total + (k + beside(t + 1)) * (fx[t + 4] - f) - (k + beside(t - 1)) * (f - fx[t + 2])
        return divs[t] + (0.5 * TENSION) * total

    def beyond(t, outer):
        store(outer, (0.5 * TENSION) * kap[t] * (fx[t + 3] - fx[outer + 3]))

    def ring(ref, t, first, last):
        if first < 0:
            return jnp.concatenate([ref[t, first + SIZE : SIZE], ref[t, 0:last]], axis=0)
        if last > SIZE:
            return jnp.concatenate([ref[t, first:SIZE], ref[t, 0 : last - SIZE]], axis=0)
        return ref[t, first:last]

    def put(ref, t, first, last, value):
        if last > SIZE:
            ref[t, first:SIZE] = value[: SIZE - first]
            ref[t, 0 : last - SIZE] = value[SIZE - first :]
        else:
            ref[t, first:last] = value

    def inner_rows(x):
        return x[8 : x.shape[0] - 8]

    def first_stage(planes):
        for t in planes:
            fhi[t + 1], flo[t + 1] = split(mm3(shi[t + 1], slo[t + 1], th[...], tl[...]))

    def second_stage(planes, rows):
        for t in planes:
            spec[t + 1, rows, :] = mm3(th[rows, :], tl[rows, :], fhi[t + 1], flo[t + 1])

    near = 3 - 3 * core
    step = 2 * core - 1

    def place(d):
        return near + step * d

    near_side = 1 - core
    near_halo = 4 - 5 * core
    far_halo = 5 * core - 1

    def wait_frac(side, piece):
        first, last = (0, SIZE) if piece < 2 else PIECES[piece - 2]
        rows = pl.ds(first, last - first)
        pltpu.make_async_copy(frac_in.at[0, rows], fx.at[0, rows], fr_sem.at[side, piece]).wait()

    def wait_far(piece):
        @pl.when(has_cross)
        def _():
            wait_frac(core, piece)

    loads[0].wait()
    lax.fori_loop(0, SLAB, lambda t, c: (flat_heights(t), c)[1], 0)
    pl.semaphore_wait(round_sem.at[0], len(nearest))
    hail(1, y_ring)
    loads[1].wait()
    lax.fori_loop(1, 3, lambda t, c: (flat_bend(t), c)[1], 0)
    for piece in range(2 + len(PIECES)):
        wait_frac(near_side, piece)
    flat_heights(near_halo)
    flat_bend(near)
    upright_bend(near)
    for load in loads[2:]:
        load.wait()
    beyond(near, near_halo)
    pl.semaphore_wait(round_sem.at[1], len(y_ring))
    hail(2, z_ring)
    wait_far(0)
    flat_heights(far_halo)
    flat_bend(place(3))
    upright_bend(place(1))
    store(near, source(near, -1))
    second = place(1)
    part[1] = source(second, place(2))
    first_stage((near_halo, near))
    second_stage((near_halo, near), slice(None))
    wait_far(1)
    upright_bend(place(2))
    store(second, part[1] + (0.5 * TENSION) * kap[place(2)] * (fx[place(2) + 3] - fx[second + 3]))
    outer, third = place(3), place(2)
    late = (third, outer, far_halo)

    def prepare():
        part[0] = source(third, outer)
        summed = fx[1 + 2 * core]
        for j in range(1, 6):
            summed = summed + fx[1 + 2 * core + j]
        heights[0] = summed

    def late_piece(c):
        scale = jnp.where(has_cross, 0.5 * TENSION, 0.0)
        a, b = BENT[c]
        h = ring(heights, 0, a - 8, b + 8) + ring(fx, 9 * core, a - 8, b + 8)
        value = inner_rows(upright(h))
        where = ring(dirs, outer, a, b)
        flat = ring(kap, outer, a, b)
        put(kap, outer, a, b, jnp.where(where == 0, value, jnp.where(where == 3, 0.0, flat)))
        a, b = FED[c]
        f, k = ring(fx, outer + 3, a - 8, b + 8), ring(kap, outer, a - 8, b + 8)
        face = (k + up(k, 0)) * (up(f, 0) - f)
        total = inner_rows(face - down(face, 0))
        f, k = inner_rows(f), inner_rows(k)
        face = (k + up(k, 1)) * (up(f, 1) - f)
        total = total + face - down(face, 1)
        f_third, f_halo = ring(fx, third + 3, a, b), ring(fx, far_halo + 3, a, b)
        total = total + (ring(kap, third, a, b) + k) * (f_third - f) + k * (f_halo - f)
        fed = (
            ring(part, 0, a, b) + (0.5 * TENSION) * k * (f - f_third),
            ring(divs, outer, a, b) + (0.5 * TENSION) * total,
            scale * k * (f - f_halo),
        )
        high, low = split(mm3(*split(jnp.concatenate(fed, axis=0)), th[...], tl[...]))
        for n, t in enumerate(late):
            rows = slice(n * (b - a), (n + 1) * (b - a))
            put(fhi, t + 1, a, b, high[rows])
            put(flo, t + 1, a, b, low[rows])

    prepare()
    for c in range(len(PIECES)):
        wait_far(2 + c)
        late_piece(c)
        if c == 0:
            first_stage((second,))

    def half_rows(half):
        return pl.ds(pl.multiple_of(half * 128, 128), 128)

    def sums(half, i):
        rows = pl.ds(pl.multiple_of(half * 128 + i * ROWS, ROWS), ROWS)
        r = ratio[rows, :]
        f = [spec[t, rows, :] for t in range(SLAB + 2)]
        low, high = f[0], f[SLAB + 1]
        for t in range(1, SLAB + 1):
            low = r * low + f[t]
            high = r * high + f[SLAB + 1 - t]
        low = r * low + f[SLAB + 1]
        high = r * high + f[0]
        return low, high

    second_stage((second,) + late, half_rows(1 - core))

    def give(q):
        rows = pl.ds(64 * q, 64)
        return pltpu.make_async_remote_copy(
            src_ref=lus.at[:, rows], dst_ref=rc.at[core, :, rows], send_sem=c_sem.at[0, q], recv_sem=c_sem.at[1, q],
            device_id=(sibling,), device_id_type=MESH,
        )

    for q in range(2):
        for i in (2 * q, 2 * q + 1):
            rows = pl.ds(i * ROWS, ROWS)
            lus[0, rows, :], lus[1, rows, :] = sums(1 - core, i)
        give(q).start()

    second_stage((second,) + late, half_rows(core))
    for i in range(4):
        rows = pl.ds(i * ROWS, ROWS)
        rc[core, 0, rows, :], rc[core, 1, rows, :] = sums(core, i)

    share = pltpu.make_async_remote_copy(
        src_ref=rc.at[0], dst_ref=rz, send_sem=z_sem.at[0], recv_sem=z_sem.at[1],
        device_id=(sibling,), device_id_type=MESH,
    )

    @pl.when(core == 0)
    def _():
        share.start()

    def power4(x):
        x = x * x
        return x * x

    first_half = lax.broadcasted_iota(jnp.int32, (8, 128), 0) < 4

    def swap(x):
        return pltpu.roll(x, 4, 0)

    def cut(i, carry):
        rows = pl.ds(pl.multiple_of(i * 8, 8), 8)
        rho = power4(ratio[pl.ds(pl.multiple_of(core * 128 + i * 8, 8), 8), :])
        low = rho * rc[0, 0, rows, :] + rc[1, 0, rows, :]
        high = rc[0, 1, rows, :] + rho * rc[1, 1, rows, :]
        for lane in range(2):
            lt = low[:, 128 * lane : 128 * lane + 128]
            ut = high[:, 128 * lane : 128 * lane + 128]
            pu[i * 4 + lane * 2] = jnp.where(first_half, lt, swap(ut))
            pu[i * 4 + lane * 2 + 1] = jnp.where(first_half, swap(lt), ut)
        return carry

    for q in range(2):
        give(q).wait_recv()
        lax.fori_loop(8 * q, 8 * q + 8, cut, 0, unroll=True)

    def send_up(other):
        return pltpu.make_async_remote_copy(
            src_ref=pu.at[other], dst_ref=ru.at[chip], send_sem=u_sem.at[0], recv_sem=u_sem.at[1],
            device_id=(2 * other + core,), device_id_type=MESH,
        )

    def send_down(other):
        return pltpu.make_async_remote_copy(
            src_ref=od.at[other], dst_ref=rd.at[core, chip], send_sem=u_sem.at[2], recv_sem=u_sem.at[3 + core],
            device_id=(2 * other + 1,), device_id_type=MESH,
        )

    def wait_parts(sem, count=CHIPS - 1):
        span = pl.ds(0, count)
        pltpu.make_async_copy(pu.at[span], ru.at[span], u_sem.at[sem]).wait()

    pl.semaphore_wait(round_sem.at[2], len(z_ring))
    hail(3, x_near)
    for other in others:
        send_up(other).start()
    ru[chip] = pu[chip]
    wait_parts(1)

    tile_row = lax.div(chip, 4)
    tile_lane = lax.rem(lax.div(chip, 2), 2)
    tile_half = lax.rem(chip, 2)
    rt = ratio[
        pl.ds(pl.multiple_of(core * 128 + tile_row * 8, 8), 8),
        pl.ds(pl.multiple_of(tile_lane * 128, 128), 128),
    ]
    keep = first_half == (tile_half == 0)
    rt = jnp.where(keep, rt, swap(rt))
    r8 = power4(rt * rt)
    r64 = power4(r8 * r8)
    r513 = power4(r64 * r64) * rt
    merged = [jnp.where(first_half, ru[j], ru[CHIPS - 1 - j]) for j in range(CHIPS)]
    blocks = []
    for b in range(8):
        total = merged[8 * b]
        for j in range(1, 8):
            total = r8 * total + merged[8 * b + j]
        blocks.append(total)
    ends = blocks[0]
    for b in range(1, 8):
        ends = r64 * ends + blocks[b]
    walls = (swap(ends) - r513 * ends) / (1.0 - r513 * r513)
    starts = [-(rt * walls)]
    for b in range(7):
        starts.append(r64 * starts[b] + blocks[b])
    sweep = []
    for b in range(8):
        sweep.append(starts[b])
        for j in range(7):
            sweep.append(r8 * sweep[-1] + merged[8 * b + j])
    for j in range(CHIPS):
        od[j] = jnp.where(first_half, sweep[j], sweep[CHIPS - 1 - j])

    pl.semaphore_wait(round_sem.at[3], len(x_near))
    for other in others:
        send_down(other).start()

    @pl.when(core == 0)
    def _():
        send_down(chip).start()

    def spread(half):
        even_low, odd_high = (rz.at[0], lus.at[1]) if half == 0 else (rc.at[0, 0], rc.at[1, 1])

        def body(i, carry):
            rows = pl.ds(pl.multiple_of(i * 8, 8), 8)
            rho = power4(ratio[pl.ds(pl.multiple_of(half * 128 + i * 8, 8), 8), :])
            tiles = [rd[half, i * 4 + k] for k in range(4)]
            a = jnp.concatenate([jnp.where(first_half, tiles[k], swap(tiles[k + 1])) for k in (0, 2)], axis=1)
            b = jnp.concatenate([jnp.where(first_half, swap(tiles[k]), tiles[k + 1]) for k in (0, 2)], axis=1)
            sd[half, 0, rows, :] = a
            sd[half, 1, rows, :] = rho * b + odd_high[rows, :]
            ab[half, 0, rows, :] = rho * a + even_low[rows, :]
            ab[half, 1, rows, :] = b
            return carry

        lax.fori_loop(0, 16, body, 0, unroll=True)

    def hand(half):
        return pltpu.make_async_remote_copy(
            src_ref=sd.at[half], dst_ref=ab.at[half], send_sem=h_sem.at[0, half], recv_sem=h_sem.at[1, half],
            device_id=(sibling,), device_id_type=MESH,
        )

    def modal(half):
        rows = pl.ds(128 * half, 128)
        r = ratio[rows, :]
        w = weight[rows, :]
        f = [spec[t, rows, :] for t in range(SLAB + 2)]
        rising = [r * f[0] + ab[half, 0] + f[1]]
        for t in range(1, SLAB):
            rising.append(r * rising[t - 1] + f[t + 1])
        falling = ab[half, 1] + r * f[SLAB + 1]
        values = [None] * SLAB
        for t in range(SLAB - 1, -1, -1):
            values[t] = w * (rising[t] + falling)
            falling = r * (falling + f[t + 1])
        high, low = split(mm3(*split(jnp.concatenate(values, axis=0)), th[...], tl[...]))
        for t in range(SLAB):
            inner_high[t, rows, :] = high[128 * t : 128 * t + 128]
            inner_low[t, rows, :] = low[128 * t : 128 * t + 128]

    @pl.when(core == 1)
    def _():
        rd[1, chip] = od[chip]
        for half in (1, 0):
            wait_parts(3 + half, CHIPS - half)
            if half == 0:
                share.wait_recv()
            spread(half)
            hand(half).start()
            modal(half)
        for half in (1, 0):
            hand(half).wait_send()
        wait_parts(2, CHIPS - 1)

    @pl.when(core == 0)
    def _():
        for half in (1, 0):
            hand(half).wait_recv()
            modal(half)
        share.wait_send()
        wait_parts(2, CHIPS)

    @pl.when(has_above)
    def _():
        for copy in halo_copies(0):
            copy.wait_send()

    @pl.when(has_below)
    def _():
        for copy in halo_copies(1):
            copy.wait_send()

    for q in range(2):
        give(q).wait_send()
    wait_parts(0)


def finish(kap, high, low, th, tl, kap_out, pre_out, pre, sem):
    passing = pltpu.make_async_copy(kap, kap_out, sem.at[SLAB])
    passing.start()
    stores = []
    for t in range(SLAB):
        pre[t] = mm3(th[...], tl[...], high[t], low[t])
        stores.append(pltpu.make_async_copy(pre.at[t], pre_out.at[t], sem.at[t]))
        stores[t].start()
    passing.wait()
    for copy in stores:
        copy.wait()


def shards(fraction, column_dir, divergence):
    shape = (SLAB, SIZE, SIZE)
    plane = (SIZE, SIZE)
    high, low, ratio, weight = tables()
    far = pl.BlockSpec(memory_space=pltpu.HBM)
    vm = pltpu.VMEM
    close = pl.BlockSpec(memory_space=vm)
    dma = pltpu.SemaphoreType.DMA
    whole = jax.ShapeDtypeStruct(shape, F32)
    half = jax.ShapeDtypeStruct(shape, BF16)
    table = jax.ShapeDtypeStruct(plane, BF16)
    params = dict(vmem_limit_bytes=40 * 1024 * 1024)
    six = vm((SLAB + 2,) + plane, F32)
    six_half = vm((SLAB + 2,) + plane, BF16)
    inputs = (
        fraction, column_dir, divergence, jnp.asarray(high), jnp.asarray(low), jnp.asarray(ratio), jnp.asarray(weight),
    )
    handed_on = pl.pallas_call(
        kernel,
        out_shape=(whole, half, half, table, table),
        in_specs=[far] * 7,
        out_specs=(close,) * 5,
        scratch_shapes=[
            vm((10,) + plane, F32), vm(shape, jnp.int32), vm(shape, F32),
            vm(plane, F32), vm(plane, F32),
            six, six, six, six, six, six,
            six_half, six_half, six_half, six_half, six,
            vm((2,) + plane, F32), vm((1,) + plane, F32),
            vm((2, 128, SIZE), F32), vm((2, 2, 128, SIZE), F32), vm((2, 128, SIZE), F32),
            vm((CHIPS, 8, 128), F32), vm((CHIPS, 8, 128), F32),
            vm((CHIPS, 8, 128), F32), vm((2, CHIPS, 8, 128), F32),
            vm((2, 2, 128, SIZE), F32), vm((2, 2, 128, SIZE), F32),
            dma((7,)), dma((2, 5)), dma((2, 5)), dma((2, 2)), dma((2,)), dma((5,)), dma((2, 2)), pltpu.SemaphoreType.REGULAR((4,)),
        ],
        compiler_params=pltpu.CompilerParams(collective_id=0, has_side_effects=True, **params),
    )(*(pltpu.with_memory_space_constraint(value, pltpu.HBM) for value in inputs))
    return pl.pallas_call(
        finish,
        out_shape=(whole, whole),
        in_specs=[close] * 5,
        out_specs=(far,) * 2,
        scratch_shapes=[
            vm(shape, F32), dma((SLAB + 1,)),
        ],
        compiler_params=pltpu.CompilerParams(**params),
    )(*handed_on)


def solution(mesh):
    spec = P("gz", None, None)
    return jax.shard_map(
        shards, mesh=mesh, in_specs=(spec, spec, spec), out_specs=(spec, spec), check_vma=False
    )
```

```python
import jax
import jax.numpy as jnp
import numpy as np
from jax import lax
from jax.experimental import pallas as pl
from jax.experimental.pallas import tpu as pltpu
from jax.sharding import PartitionSpec as P

TENSION = 0.2
SHIFT_SCALE = 16.0
SIZE = 256
PLANES = 512
SLAB = 4
DEVICES = 128
CHIPS = 64
ROWS = 32
PIECES = ((0, 96), (96, 192), (192, 256))
BENT = ((8, 88), (88, 184), (184, 264))
FED = ((16, 80), (80, 176), (176, 272))
MESH = pl.DeviceIdType.MESH
F32 = jnp.float32
BF16 = jnp.bfloat16


def tables():
    count = np.arange(SIZE)
    angle = 2.0 * np.pi / SIZE * ((count[:, None] * count[None, :]) % SIZE)
    cas = np.cos(angle) + np.sin(angle)
    high = cas.astype(jnp.bfloat16)
    low = (cas - high.astype(np.float64)).astype(jnp.bfloat16)
    waves = (2.0 * np.sin(np.pi * count / SIZE)) ** 2
    excess = waves[:, None] + waves[None, :] + SHIFT_SCALE / float(PLANES * PLANES)
    root = np.sqrt(excess * (excess + 4.0))
    ratio = 2.0 / (2.0 + excess + root)
    weight = -1.0 / (root * SIZE * SIZE)
    return high, low, ratio.astype(np.float32), weight.astype(np.float32)


def split(x):
    high = x.astype(BF16)
    return high, (x - high.astype(F32)).astype(BF16)


def mm(a, b):
    return jnp.dot(a, b, preferred_element_type=F32)


def mm3(ah, al, bh, bl):
    return mm(ah, bh) + (mm(ah, bl) + mm(al, bh))


def up(x, axis):
    return pltpu.roll(x, x.shape[axis] - 1, axis)


def down(x, axis):
    return pltpu.roll(x, 1, axis)


def window7(x, axis):
    size = x.shape[axis]
    three = x + pltpu.roll(x, 1, axis) + pltpu.roll(x, size - 1, axis)
    return x + pltpu.roll(three, 2, axis) + pltpu.roll(three, size - 2, axis)


def bend(da, db, haa, hbb, dab):
    qa = 0.25 * da * da
    qb = 0.25 * db * db
    root = lax.rsqrt(1.0 + qa + qb)
    upper = haa * (1.0 + qb) + hbb * (1.0 + qa) - 0.125 * (da * db * dab)
    return upper * (root * root * root)


def kernel(
    frac_in, dir_in, div_in, th_in, tl_in, ratio_in, weight_in,
    kap, inner_high, inner_low, th, tl,
    fx, dirs, divs, ratio, weight,
    axc, axd, axs, ayc, ayd, ays, shi, slo, fhi, flo, spec, part, heights,
    lus, rc, rz, pu, ru, od, rd, sd, ab,
    in_sem, fs_sem, fr_sem, c_sem, z_sem, u_sem, h_sem, round_sem,
):
    me = lax.axis_index("gz")
    core = lax.rem(me, 2)
    chip = lax.div(me, 2)
    sibling = me + 1 - 2 * core
    has_below = me > 0
    has_above = me < DEVICES - 1
    cross = me - 1 + 2 * core
    has_cross = jnp.logical_and(cross >= 0, cross < DEVICES)

    digits = [lax.div(chip, 16), lax.rem(lax.div(chip, 4), 4), lax.rem(chip, 4)]
    parts = [[lax.rem(v + d, 4) * scale for d in range(4)] for v, scale in zip(digits, (16, 4, 1))]
    reach = (0, 1, 2, 1)
    offsets = [(a, b, c) for a in range(4) for b in range(4) for c in range(4) if a or b or c]
    offsets.sort(key=lambda o: -sum(reach[d] for d in o))

    def chips_at(places):
        return [parts[0][a] + parts[1][b] + parts[2][c] for a, b, c in places]

    others = chips_at(offsets)
    nearest = chips_at([(1, 0, 0), (3, 0, 0), (0, 1, 0), (0, 3, 0), (0, 0, 1), (0, 0, 3)])
    y_ring = chips_at([(0, 2, 0), (0, 1, 0), (0, 3, 0)])
    z_ring = chips_at([(2, 0, 0), (1, 0, 0), (3, 0, 0)])
    x_near = chips_at([(0, 0, 1), (0, 0, 3)])

    barrier = pltpu.get_barrier_semaphore()

    def greet(target):
        pl.semaphore_signal(barrier, inc=1, device_id=(target,), device_id_type=MESH)

    @pl.when(has_cross)
    def _():
        greet(cross)

    greet(sibling)
    for other in nearest:
        greet(2 * other + core)

    loads = [
        pltpu.make_async_copy(frac_in, fx.at[pl.ds(3, SLAB)], in_sem.at[0]),
        pltpu.make_async_copy(dir_in, dirs, in_sem.at[1]),
        pltpu.make_async_copy(div_in, divs, in_sem.at[2]),
        pltpu.make_async_copy(th_in, th, in_sem.at[3]),
        pltpu.make_async_copy(tl_in, tl, in_sem.at[4]),
        pltpu.make_async_copy(ratio_in, ratio, in_sem.at[5]),
        pltpu.make_async_copy(weight_in, weight, in_sem.at[6]),
    ]
    for load in loads:
        load.start()

    peers = 1 + len(nearest)
    pl.semaphore_wait(barrier, jnp.where(has_cross, peers + 1, peers))

    def hail(i, chips):
        for other in chips:
            pl.semaphore_signal(
                round_sem.at[i], inc=1, device_id=(2 * other + core,), device_id_type=MESH
            )

    def halo_copies(side):
        for piece in range(2 + len(PIECES)):
            j = min(piece, 2)
            first, last = (0, SIZE) if piece < 2 else PIECES[piece - 2]
            rows = pl.ds(first, last - first)
            source, target = (3 - j, 2 - j) if side == 0 else (j, 7 + j)
            yield pltpu.make_async_remote_copy(
                src_ref=frac_in.at[source, rows], dst_ref=fx.at[target, rows],
                send_sem=fs_sem.at[side, piece], recv_sem=fr_sem.at[side, piece],
                device_id=(me + 1 - 2 * side,), device_id_type=MESH,
            )

    def send_halo(side):
        for copy in halo_copies(side):
            copy.start()

    @pl.when(jnp.logical_and(core == 0, has_below))
    def _():
        send_halo(1)

    @pl.when(core == 0)
    def _():
        send_halo(0)

    @pl.when(jnp.logical_and(core == 1, has_above))
    def _():
        send_halo(0)

    @pl.when(core == 1)
    def _():
        send_halo(1)

    hail(0, nearest)
    zero_plane = jnp.zeros((SIZE, SIZE), F32)

    @pl.when(jnp.logical_not(has_below))
    def _():
        for j in range(3):
            fx[j] = zero_plane

    @pl.when(jnp.logical_not(has_above))
    def _():
        for j in range(3):
            fx[7 + j] = zero_plane

    def flat_heights(t):
        f = fx[t + 3]
        cx = window7(f, 0)
        lift, drop = up(cx, 1), down(cx, 1)
        axc[t + 1] = cx
        axd[t + 1] = lift - drop
        axs[t + 1] = lift + drop - 2.0 * cx
        cy = window7(f, 1)
        lift, drop = up(cy, 0), down(cy, 0)
        ayc[t + 1] = cy
        ayd[t + 1] = lift - drop
        ays[t + 1] = lift + drop - 2.0 * cy

    def flat_bend(t):
        along_x = dirs[t] == 1

        def pick(a, b):
            return jnp.where(along_x, a, b)

        lo = pick(axc[t], ayc[t])
        at = pick(axc[t + 1], ayc[t + 1])
        hi = pick(axc[t + 2], ayc[t + 2])
        d_lo = pick(axd[t], ayd[t])
        d_at = pick(axd[t + 1], ayd[t + 1])
        d_hi = pick(axd[t + 2], ayd[t + 2])
        s_at = pick(axs[t + 1], ays[t + 1])
        kap[t] = bend(hi - lo, d_at, hi + lo - 2.0 * at, s_at, d_hi - d_lo)

    def upright(h):
        right, left = up(h, 1), down(h, 1)
        db = right - left
        sb = right + left
        plus, minus = up(h, 0), down(h, 0)
        dab = up(db, 0) - down(db, 0)
        return bend(plus - minus, db, plus + minus - 2.0 * h, sb - 2.0 * h, dab)

    def upright_bend(t):
        h = fx[t]
        for j in range(1, 7):
            h = h + fx[t + j]
        value = upright(h)
        where = dirs[t]
        kap[t] = jnp.where(where == 0, value, jnp.where(where == 3, 0.0, kap[t]))

    def store(t, value):
        shi[t + 1], slo[t + 1] = split(value)

    def source(t, hidden):
        f = fx[t + 3]
        k = kap[t]
        face = (k + up(k, 0)) * (up(f, 0) - f)
        total = face - down(face, 0)
        face = (k + up(k, 1)) * (up(f, 1) - f)
        total = total + face - down(face, 1)

        def beside(other):
            shown = jnp.logical_and(jnp.logical_and(other >= 0, other < SLAB), other != hidden)
            return jnp.where(shown, kap[jnp.clip(other, 0, SLAB - 1)], 0.0)

        total = total + (k + beside(t + 1)) * (fx[t + 4] - f) - (k + beside(t - 1)) * (f - fx[t + 2])
        return divs[t] + (0.5 * TENSION) * total

    def beyond(t, outer):
        store(outer, (0.5 * TENSION) * kap[t] * (fx[t + 3] - fx[outer + 3]))

    def ring(ref, t, first, last):
        if first < 0:
            return jnp.concatenate([ref[t, first + SIZE : SIZE], ref[t, 0:last]], axis=0)
        if last > SIZE:
            return jnp.concatenate([ref[t, first:SIZE], ref[t, 0 : last - SIZE]], axis=0)
        return ref[t, first:last]

    def put(ref, t, first, last, value):
        if last > SIZE:
            ref[t, first:SIZE] = value[: SIZE - first]
            ref[t, 0 : last - SIZE] = value[SIZE - first :]
        else:
            ref[t, first:last] = value

    def inner_rows(x):
        return x[8 : x.shape[0] - 8]

    def first_stage(planes):
        for t in planes:
            fhi[t + 1], flo[t + 1] = split(mm3(shi[t + 1], slo[t + 1], th[...], tl[...]))

    def second_stage(planes, rows):
        for t in planes:
            spec[t + 1, rows, :] = mm3(th[rows, :], tl[rows, :], fhi[t + 1], flo[t + 1])

    near = 3 - 3 * core
    step = 2 * core - 1

    def place(d):
        return near + step * d

    near_side = 1 - core
    near_halo = 4 - 5 * core
    far_halo = 5 * core - 1

    def wait_frac(side, piece):
        first, last = (0, SIZE) if piece < 2 else PIECES[piece - 2]
        rows = pl.ds(first, last - first)
        pltpu.make_async_copy(frac_in.at[0, rows], fx.at[0, rows], fr_sem.at[side, piece]).wait()

    def wait_far(piece):
        @pl.when(has_cross)
        def _():
            wait_frac(core, piece)

    loads[0].wait()
    lax.fori_loop(0, SLAB, lambda t, c: (flat_heights(t), c)[1], 0)
    pl.semaphore_wait(round_sem.at[0], len(nearest))
    hail(1, y_ring)
    loads[1].wait()
    lax.fori_loop(1, 3, lambda t, c: (flat_bend(t), c)[1], 0)
    for piece in range(2 + len(PIECES)):
        wait_frac(near_side, piece)
    flat_heights(near_halo)
    flat_bend(near)
    upright_bend(near)
    for load in loads[2:]:
        load.wait()
    beyond(near, near_halo)
    pl.semaphore_wait(round_sem.at[1], len(y_ring))
    hail(2, z_ring)
    wait_far(0)
    flat_heights(far_halo)
    flat_bend(place(3))
    upright_bend(place(1))
    store(near, source(near, -1))
    second = place(1)
    part[1] = source(second, place(2))
    first_stage((near_halo, near))
    second_stage((near_halo, near), slice(None))
    wait_far(1)
    upright_bend(place(2))
    store(second, part[1] + (0.5 * TENSION) * kap[place(2)] * (fx[place(2) + 3] - fx[second + 3]))
    outer, third = place(3), place(2)
    late = (third, outer, far_halo)

    def prepare():
        part[0] = source(third, outer)
        summed = fx[1 + 2 * core]
        for j in range(1, 6):
            summed = summed + fx[1 + 2 * core + j]
        heights[0] = summed

    def late_piece(c):
        scale = jnp.where(has_cross, 0.5 * TENSION, 0.0)
        a, b = BENT[c]
        h = ring(heights, 0, a - 8, b + 8) + ring(fx, 9 * core, a - 8, b + 8)
        value = inner_rows(upright(h))
        where = ring(dirs, outer, a, b)
        flat = ring(kap, outer, a, b)
        put(kap, outer, a, b, jnp.where(where == 0, value, jnp.where(where == 3, 0.0, flat)))
        a, b = FED[c]
        f, k = ring(fx, outer + 3, a - 8, b + 8), ring(kap, outer, a - 8, b + 8)
        face = (k + up(k, 0)) * (up(f, 0) - f)
        total = inner_rows(face - down(face, 0))
        f, k = inner_rows(f), inner_rows(k)
        face = (k + up(k, 1)) * (up(f, 1) - f)
        total = total + face - down(face, 1)
        f_third, f_halo = ring(fx, third + 3, a, b), ring(fx, far_halo + 3, a, b)
        total = total + (ring(kap, third, a, b) + k) * (f_third - f) + k * (f_halo - f)
        fed = (
            ring(part, 0, a, b) + (0.5 * TENSION) * k * (f - f_third),
            ring(divs, outer, a, b) + (0.5 * TENSION) * total,
            scale * k * (f - f_halo),
        )
        high, low = split(mm3(*split(jnp.concatenate(fed, axis=0)), th[...], tl[...]))
        for n, t in enumerate(late):
            rows = slice(n * (b - a), (n + 1) * (b - a))
            put(fhi, t + 1, a, b, high[rows])
            put(flo, t + 1, a, b, low[rows])

    prepare()
    for c in range(len(PIECES)):
        wait_far(2 + c)
        late_piece(c)
        if c == 0:
            first_stage((second,))

    def half_rows(half):
        return pl.ds(pl.multiple_of(half * 128, 128), 128)

    def sums(half, i):
        rows = pl.ds(pl.multiple_of(half * 128 + i * ROWS, ROWS), ROWS)
        r = ratio[rows, :]
        f = [spec[t, rows, :] for t in range(SLAB + 2)]
        low, high = f[0], f[SLAB + 1]
        for t in range(1, SLAB + 1):
            low = r * low + f[t]
            high = r * high + f[SLAB + 1 - t]
        low = r * low + f[SLAB + 1]
        high = r * high + f[0]
        return low, high

    second_stage((second,) + late, half_rows(1 - core))

    def give(q):
        rows = pl.ds(64 * q, 64)
        return pltpu.make_async_remote_copy(
            src_ref=lus.at[:, rows], dst_ref=rc.at[core, :, rows], send_sem=c_sem.at[0, q], recv_sem=c_sem.at[1, q],
            device_id=(sibling,), device_id_type=MESH,
        )

    for q in range(2):
        for i in (2 * q, 2 * q + 1):
            rows = pl.ds(i * ROWS, ROWS)
            lus[0, rows, :], lus[1, rows, :] = sums(1 - core, i)
        give(q).start()

    second_stage((second,) + late, half_rows(core))
    for i in range(4):
        rows = pl.ds(i * ROWS, ROWS)
        rc[core, 0, rows, :], rc[core, 1, rows, :] = sums(core, i)

    share = pltpu.make_async_remote_copy(
        src_ref=rc.at[0], dst_ref=rz, send_sem=z_sem.at[0], recv_sem=z_sem.at[1],
        device_id=(sibling,), device_id_type=MESH,
    )

    @pl.when(core == 0)
    def _():
        share.start()

    def power4(x):
        x = x * x
        return x * x

    first_half = lax.broadcasted_iota(jnp.int32, (8, 128), 0) < 4

    def swap(x):
        return pltpu.roll(x, 4, 0)

    def cut(i, carry):
        rows = pl.ds(pl.multiple_of(i * 8, 8), 8)
        rho = power4(ratio[pl.ds(pl.multiple_of(core * 128 + i * 8, 8), 8), :])
        low = rho * rc[0, 0, rows, :] + rc[1, 0, rows, :]
        high = rc[0, 1, rows, :] + rho * rc[1, 1, rows, :]
        for lane in range(2):
            lt = low[:, 128 * lane : 128 * lane + 128]
            ut = high[:, 128 * lane : 128 * lane + 128]
            pu[i * 4 + lane * 2] = jnp.where(first_half, lt, swap(ut))
            pu[i * 4 + lane * 2 + 1] = jnp.where(first_half, swap(lt), ut)
        return carry

    for q in range(2):
        give(q).wait_recv()
        lax.fori_loop(8 * q, 8 * q + 8, cut, 0, unroll=True)

    def send_up(other):
        return pltpu.make_async_remote_copy(
            src_ref=pu.at[other], dst_ref=ru.at[chip], send_sem=u_sem.at[0], recv_sem=u_sem.at[1],
            device_id=(2 * other + core,), device_id_type=MESH,
        )

    def send_down(other):
        return pltpu.make_async_remote_copy(
            src_ref=od.at[other], dst_ref=rd.at[core, chip], send_sem=u_sem.at[2], recv_sem=u_sem.at[3 + core],
            device_id=(2 * other + 1,), device_id_type=MESH,
        )

    def send_across(other):
        return pltpu.make_async_remote_copy(
            src_ref=od.at[other], dst_ref=rd.at[0, chip], send_sem=u_sem.at[5], recv_sem=u_sem.at[3],
            device_id=(2 * other,), device_id_type=MESH,
        )

    def wait_parts(sem, count=CHIPS - 1):
        span = pl.ds(0, count)
        pltpu.make_async_copy(pu.at[span], ru.at[span], u_sem.at[sem]).wait()

    pl.semaphore_wait(round_sem.at[2], len(z_ring))
    hail(3, x_near)
    for other in others:
        send_up(other).start()
    ru[chip] = pu[chip]
    wait_parts(1)

    tile_row = lax.div(chip, 4)
    tile_lane = lax.rem(lax.div(chip, 2), 2)
    tile_half = lax.rem(chip, 2)
    rt = ratio[
        pl.ds(pl.multiple_of(core * 128 + tile_row * 8, 8), 8),
        pl.ds(pl.multiple_of(tile_lane * 128, 128), 128),
    ]
    keep = first_half == (tile_half == 0)
    rt = jnp.where(keep, rt, swap(rt))
    r8 = power4(rt * rt)
    r64 = power4(r8 * r8)
    r513 = power4(r64 * r64) * rt
    merged = [jnp.where(first_half, ru[j], ru[CHIPS - 1 - j]) for j in range(CHIPS)]
    blocks = []
    for b in range(8):
        total = merged[8 * b]
        for j in range(1, 8):
            total = r8 * total + merged[8 * b + j]
        blocks.append(total)
    ends = blocks[0]
    for b in range(1, 8):
        ends = r64 * ends + blocks[b]
    walls = (swap(ends) - r513 * ends) / (1.0 - r513 * r513)
    starts = [-(rt * walls)]
    for b in range(7):
        starts.append(r64 * starts[b] + blocks[b])
    sweep = []
    for b in range(8):
        sweep.append(starts[b])
        for j in range(7):
            sweep.append(r8 * sweep[-1] + merged[8 * b + j])
    for j in range(CHIPS):
        od[j] = jnp.where(first_half, sweep[j], sweep[CHIPS - 1 - j])

    pl.semaphore_wait(round_sem.at[3], len(x_near))

    @pl.when(core == 0)
    def _():
        for other in others:
            send_down(other).start()
            send_across(other).start()
        send_down(chip).start()

    @pl.when(core == 1)
    def _():
        for other in others:
            send_down(other).start()

    def spread(half, even=False):
        even_low, odd_high = (rz.at[0], lus.at[1]) if half == 0 else (rc.at[0, 0], rc.at[1, 1])

        def body(i, carry):
            rows = pl.ds(pl.multiple_of(i * 8, 8), 8)
            rho = power4(ratio[pl.ds(pl.multiple_of(half * 128 + i * 8, 8), 8), :])
            tiles = [rd[half, i * 4 + k] for k in range(4)]
            a = jnp.concatenate([jnp.where(first_half, tiles[k], swap(tiles[k + 1])) for k in (0, 2)], axis=1)
            b = jnp.concatenate([jnp.where(first_half, swap(tiles[k]), tiles[k + 1]) for k in (0, 2)], axis=1)
            if even:
                ab[half, 0, rows, :] = a
                ab[half, 1, rows, :] = rho * b + rc[1, 1, rows, :]
                return carry
            if half == 1:
                sd[half, 0, rows, :] = a
                sd[half, 1, rows, :] = rho * b + odd_high[rows, :]
            ab[half, 0, rows, :] = rho * a + even_low[rows, :]
            ab[half, 1, rows, :] = b
            return carry

        lax.fori_loop(0, 16, body, 0, unroll=True)

    def hand(half):
        return pltpu.make_async_remote_copy(
            src_ref=sd.at[half], dst_ref=ab.at[half], send_sem=h_sem.at[0, half], recv_sem=h_sem.at[1, half],
            device_id=(sibling,), device_id_type=MESH,
        )

    def modal(half):
        rows = pl.ds(128 * half, 128)
        r = ratio[rows, :]
        w = weight[rows, :]
        f = [spec[t, rows, :] for t in range(SLAB + 2)]
        rising = [r * f[0] + ab[half, 0] + f[1]]
        for t in range(1, SLAB):
            rising.append(r * rising[t - 1] + f[t + 1])
        falling = ab[half, 1] + r * f[SLAB + 1]
        values = [None] * SLAB
        for t in range(SLAB - 1, -1, -1):
            values[t] = w * (rising[t] + falling)
            falling = r * (falling + f[t + 1])
        high, low = split(mm3(*split(jnp.concatenate(values, axis=0)), th[...], tl[...]))
        for t in range(SLAB):
            inner_high[t, rows, :] = high[128 * t : 128 * t + 128]
            inner_low[t, rows, :] = low[128 * t : 128 * t + 128]

    @pl.when(core == 1)
    def _():
        rd[1, chip] = od[chip]
        for half in (1, 0):
            wait_parts(3 + half, CHIPS - half)
            if half == 0:
                share.wait_recv()
            spread(half)
            if half == 1:
                hand(half).start()
            modal(half)
        hand(1).wait_send()
        wait_parts(2, CHIPS - 1)

    @pl.when(core == 0)
    def _():
        rd[0, chip] = od[chip]
        hand(1).wait_recv()
        modal(1)
        wait_parts(3)
        spread(0, True)
        modal(0)
        share.wait_send()
        wait_parts(2, CHIPS)
        wait_parts(5)

    @pl.when(has_above)
    def _():
        for copy in halo_copies(0):
            copy.wait_send()

    @pl.when(has_below)
    def _():
        for copy in halo_copies(1):
            copy.wait_send()

    for q in range(2):
        give(q).wait_send()
    wait_parts(0)


def finish(kap, high, low, th, tl, kap_out, pre_out, pre, sem):
    passing = pltpu.make_async_copy(kap, kap_out, sem.at[SLAB])
    passing.start()
    stores = []
    for t in range(SLAB):
        pre[t] = mm3(th[...], tl[...], high[t], low[t])
        stores.append(pltpu.make_async_copy(pre.at[t], pre_out.at[t], sem.at[t]))
        stores[t].start()
    passing.wait()
    for copy in stores:
        copy.wait()


def shards(fraction, column_dir, divergence):
    shape = (SLAB, SIZE, SIZE)
    plane = (SIZE, SIZE)
    high, low, ratio, weight = tables()
    far = pl.BlockSpec(memory_space=pltpu.HBM)
    vm = pltpu.VMEM
    close = pl.BlockSpec(memory_space=vm)
    dma = pltpu.SemaphoreType.DMA
    whole = jax.ShapeDtypeStruct(shape, F32)
    half = jax.ShapeDtypeStruct(shape, BF16)
    table = jax.ShapeDtypeStruct(plane, BF16)
    params = dict(vmem_limit_bytes=40 * 1024 * 1024)
    six = vm((SLAB + 2,) + plane, F32)
    six_half = vm((SLAB + 2,) + plane, BF16)
    inputs = (
        fraction, column_dir, divergence, jnp.asarray(high), jnp.asarray(low), jnp.asarray(ratio), jnp.asarray(weight),
    )
    handed_on = pl.pallas_call(
        kernel,
        out_shape=(whole, half, half, table, table),
        in_specs=[far] * 7,
        out_specs=(close,) * 5,
        scratch_shapes=[
            vm((10,) + plane, F32), vm(shape, jnp.int32), vm(shape, F32),
            vm(plane, F32), vm(plane, F32),
            six, six, six, six, six, six,
            six_half, six_half, six_half, six_half, six,
            vm((2,) + plane, F32), vm((1,) + plane, F32),
            vm((2, 128, SIZE), F32), vm((2, 2, 128, SIZE), F32), vm((2, 128, SIZE), F32),
            vm((CHIPS, 8, 128), F32), vm((CHIPS, 8, 128), F32),
            vm((CHIPS, 8, 128), F32), vm((2, CHIPS, 8, 128), F32),
            vm((2, 2, 128, SIZE), F32), vm((2, 2, 128, SIZE), F32),
            dma((7,)), dma((2, 5)), dma((2, 5)), dma((2, 2)), dma((2,)), dma((6,)), dma((2, 2)), pltpu.SemaphoreType.REGULAR((4,)),
        ],
        compiler_params=pltpu.CompilerParams(collective_id=0, has_side_effects=True, **params),
    )(*(pltpu.with_memory_space_constraint(value, pltpu.HBM) for value in inputs))
    return pl.pallas_call(
        finish,
        out_shape=(whole, whole),
        in_specs=[close] * 5,
        out_specs=(far,) * 2,
        scratch_shapes=[
            vm(shape, F32), dma((SLAB + 1,)),
        ],
        compiler_params=pltpu.CompilerParams(**params),
    )(*handed_on)


def solution(mesh):
    spec = P("gz", None, None)
    return jax.shard_map(
        shards, mesh=mesh, in_specs=(spec, spec, spec), out_specs=(spec, spec), check_vma=False
    )
```
